32 devices in a mesh: dp: 16 (over z, y, x), tensor: 2 (over core).
Axes of the slice: x: 2, y: 2, z: 4, core: 2. Of those that a mesh axis runs over, the one named last changes fastest.
Arguments:
- tokens: bfloat16 [16384, 1536], P(('dp', 'tensor')), may hold values from -6 to 6
- w_query: float32 [1536, 1536], P('dp', 'tensor'), may hold values from -0.15625 to 0.15625
- w_key: float32 [1536, 1536], P('dp', 'tensor'), may hold values from -0.15625 to 0.15625
- w_value: float32 [1536, 1536], P('dp', 'tensor'), may hold values from -0.15625 to 0.15625
- w_gate_attn: float32 [1536, 1536], P('dp', 'tensor'), may hold values from -0.15625 to 0.15625
- w_forget: float32 [1536, 24], P('dp', 'tensor'), may hold values from -0.15625 to 0.15625
- forget_bias: float32 [24], P('tensor'), may hold values from 1 to 7
- w_out: float32 [1536, 1536], P('tensor', 'dp'), may hold values from -2.5 to 2.5
- norm_attn: float32 [1536], P(('dp', 'tensor')), may hold values from 0.25 to 1.75
- norm_mlp: float32 [1536], P(('dp', 'tensor')), may hold values from 0.25 to 1.75
- w_gate: float32 [1536, 4096], P('dp', 'tensor'), may hold values from -0.15625 to 0.15625
- w_up: float32 [1536, 4096], P('dp', 'tensor'), may hold values from -0.15625 to 0.15625
- w_down: float32 [4096, 1536], P('tensor', 'dp'), may hold values from -0.09375 to 0.09375
- cotangent: bfloat16 [16384, 1536], P(('dp', 'tensor')), may hold values from -6 to 6
Outputs:
- mixed: bfloat16 [16384, 1536], P(('dp', 'tensor'))
- tokens_grad: bfloat16 [16384, 1536], P(('dp', 'tensor'))
- query_grad: float32 [1536, 1536], P('dp', 'tensor')
- key_grad: float32 [1536, 1536], P('dp', 'tensor')
- value_grad: float32 [1536, 1536], P('dp', 'tensor')
- gate_attn_grad: float32 [1536, 1536], P('dp', 'tensor')
- forget_grad: float32 [1536, 24], P('dp', 'tensor')
- forget_bias_grad: float32 [24], P('tensor')
- out_grad: float32 [1536, 1536], P('tensor', 'dp')
- norm_attn_grad: float32 [1536], P(('dp', 'tensor'))
- norm_mlp_grad: float32 [1536], P(('dp', 'tensor'))
- gate_grad: float32 [1536, 4096], P('dp', 'tensor')
- up_grad: float32 [1536, 4096], P('dp', 'tensor')
- down_grad: float32 [4096, 1536], P('tensor', 'dp')
The draws below stay inside these ranges and needn't reach their ends.
All inputs are finite; a program needn't handle non-finite values.
Results may differ from the reference program's by a relative error of at most 0.014.
The reference program's roundings to bfloat16 on the way count: a program that leaves them out, or rounds other values in their place, can miss the bound.
Values may be sent and summed in bfloat16 or wider, within the bound.
No kernel may reach another device: no remote copies, remote signals or barrier semaphores. Data moves between devices by JAX's collectives and lax.ppermute only.
A program may use at most 256 MiB of HBM per device.

```python
import jax
import jax.numpy as jnp
from jax import lax

D = 1536
H = 24
HD = 64
FF = 4096
SEQ = 1024
HH = 1536
TOKENS = 16384
N_DP = 16


def raised(drawn, key, source, target, parts, factor):
    def block_of(axis_at):
        return (jnp.arange(drawn.shape[axis_at]) // (drawn.shape[axis_at] // parts)).reshape((-1,) + (1,) * (drawn.ndim - 1 - axis_at))

    first = jax.random.permutation(key, parts)[block_of(target)]
    second = (block_of(target) + parts // 2) % parts
    return jnp.where((block_of(source) == first) | (block_of(source) == second), factor * drawn, drawn)


def block_levels(rng, dims, cuts, smallest, top_value):
    factor_of, own = 1.0, jax.random.fold_in(rng, 6)
    for dim, parts in cuts:
        heights = jnp.exp(jax.random.uniform(jax.random.fold_in(own, dim), (parts,), jnp.float32, smallest / len(cuts), top_value / len(cuts)))
        factor_of = factor_of * jnp.repeat(heights, dims[dim] // parts).reshape([-1 if axis == dim else 1 for axis in range(len(dims))])
    return factor_of


def scatter_about(rng, shape, deviation, reach, cuts=(), kind=jnp.bfloat16):
    result = deviation * jax.random.normal(rng, shape, jnp.float32)
    if cuts:
        result = result * block_levels(rng, shape, cuts, -0.22, 0.18)
    return jnp.clip(result, -reach, reach).astype(kind)


def heavy_noise(rng, dims, spread, bound, pieces, heavy, dtype=jnp.bfloat16):
    array = spread * jax.random.normal(rng, dims, jnp.float32)
    if pieces:
        array = array * block_levels(rng, dims, pieces, -0.22, 0.18)
    return jnp.clip(raised(array, jax.random.fold_in(rng, 3), *heavy), -bound, bound).astype(dtype)


def setup_inputs(seed: int = 0) -> dict:
    key_of = jax.random.split(jax.random.key(seed), 15)
    tokens = scatter_about(key_of[0], (TOKENS, D), 1.0, 6.0, ((0, 32),))
    w_query = scatter_about(key_of[1], (D, HH), D ** -0.5, 0.15625, ((0, 16), (1, 2)), jnp.float32)
    w_key = scatter_about(key_of[2], (D, HH), D ** -0.5, 0.15625, ((0, 16), (1, 2)), jnp.float32)
    w_value = scatter_about(key_of[3], (D, HH), D ** -0.5, 0.15625, ((0, 16), (1, 2)), jnp.float32)
    w_gate_attn = scatter_about(key_of[4], (D, HH), D ** -0.5, 0.15625, ((0, 16), (1, 2)), jnp.float32)
    w_forget = scatter_about(key_of[5], (D, H), D ** -0.5, 0.15625, ((0, 16), (1, 2)), jnp.float32)
    forget_bias = jnp.clip(1.0 + 6.0 * jax.random.uniform(key_of[6], (H,), jnp.float32) ** block_levels(key_of[6], (H,), ((0, 2),), -0.2, 0.2), 1.0, 7.0)
    w_out = scatter_about(key_of[7], (HH, D), (max(HH // 256, 1)) ** -0.5, 2.5, ((0, 2), (1, 16)), jnp.float32)
    norm_attn = jnp.clip(1.0 + 0.15 * jax.random.normal(key_of[8], (D,), jnp.float32), 0.25, 1.75)
    norm_mlp = jnp.clip(1.0 + 0.15 * jax.random.normal(key_of[9], (D,), jnp.float32), 0.25, 1.75)
    w_gate = scatter_about(key_of[10], (D, FF), D ** -0.5, 0.15625, ((0, 16), (1, 2)), jnp.float32)
    w_up = scatter_about(key_of[11], (D, FF), D ** -0.5, 0.15625, ((0, 16), (1, 2)), jnp.float32)
    w_down = scatter_about(key_of[12], (FF, D), FF ** -0.5, 0.09375, ((0, 2), (1, 16)), jnp.float32)
    cotangent = heavy_noise(key_of[13], (TOKENS, D), 1.0, 6.0, ((0, 32),), (0, 1, 32, 2.75))
    return dict(tokens=tokens, w_query=w_query, w_key=w_key, w_value=w_value, w_gate_attn=w_gate_attn, w_forget=w_forget, forget_bias=forget_bias, w_out=w_out, norm_attn=norm_attn, norm_mlp=norm_mlp, w_gate=w_gate, w_up=w_up, w_down=w_down, cotangent=cotangent)


@jax.custom_vjp
def low(v):
    return lax.optimization_barrier(v.astype(jnp.bfloat16)).astype(jnp.float32)

@jax.custom_vjp
def low_back(v):
    return v

def low_keep(v):
    return (low(v), None)

def low_pass(kept, grad):
    return (grad,)

def back_keep(v):
    return (v, None)

def back_low(kept, grad):
    return (low(grad),)
low.defvjp(low_keep, low_pass)
low_back.defvjp(back_keep, back_low)
EPSILON = 1e-06

def product(left, right):
    return jnp.dot(left, right, precision=lax.Precision.HIGHEST, preferred_element_type=jnp.float32)

def normalize(values, gain):
    return values * lax.rsqrt(lax.optimization_barrier(jnp.mean(values * values, axis=-1, keepdims=True)) + EPSILON) * gain

def head_attention(operands):
    query_rows, key_rows, value_rows, decay = operands
    length = query_rows.shape[0]
    row_place = lax.broadcasted_iota(jnp.int32, (length, length), 0)
    col_place = lax.broadcasted_iota(jnp.int32, (length, length), 1)
    scores = product(query_rows, key_rows.T) * HD ** (-0.5) + decay[:, None] - decay[None, :]
    scores = low_back(scores)
    scores = jnp.where(col_place <= row_place, scores, -1e+30)
    highest = lax.optimization_barrier(jnp.max(scores, axis=-1, keepdims=True))
    exp_scores = jnp.exp(scores - highest)
    probs = exp_scores / lax.optimization_barrier(jnp.sum(exp_scores, axis=-1, keepdims=True))
    return product(low(probs), value_rows)

def layer(resid, w_query, w_key, w_value, w_gate_attn, w_forget, forget_bias, w_out, norm_attn, norm_mlp, w_gate, w_up, w_down):
    length = resid.shape[0]
    normed_attn = low(normalize(resid, norm_attn))
    queries = low(low_back(product(normed_attn, low(w_query))))
    keys = low(low_back(product(normed_attn, low(w_key))))
    values = low(low_back(product(normed_attn, low(w_value))))
    forget_logit = low_back(product(normed_attn, low(w_forget)) + forget_bias)
    decay = jnp.cumsum(-jnp.log1p(jnp.exp(-forget_logit)), axis=0)
    gate_logit = low_back(product(normed_attn, low(w_gate_attn)))

    def by_head(table):
        return table.reshape(length, H, HD).transpose(1, 0, 2)
    head_outputs = lax.map(jax.checkpoint(head_attention), (by_head(queries), by_head(keys), by_head(values), decay.T))
    attended = low_back(head_outputs.transpose(1, 0, 2).reshape(length, HH))
    gated = low(attended * jax.nn.sigmoid(gate_logit))
    mid = resid + low_back(product(gated, low(w_out)))
    normed_mlp = low(normalize(mid, norm_mlp))
    gate_act = low_back(product(normed_mlp, low(w_gate)))
    up_act = low_back(product(normed_mlp, low(w_up)))
    hidden = low(gate_act * jax.nn.sigmoid(gate_act) * up_act)
    return mid + product(hidden, low(w_down))

def reference(tokens, w_query, w_key, w_value, w_gate_attn, w_forget, forget_bias, w_out, norm_attn, norm_mlp, w_gate, w_up, w_down, cotangent):
    weights = (w_query, w_key, w_value, w_gate_attn, w_forget, forget_bias, w_out, norm_attn, norm_mlp, w_gate, w_up, w_down)
    weights = tuple((item.astype(jnp.float32) for item in weights))
    inputs = tokens.astype(jnp.float32).reshape(N_DP, SEQ, D)
    grads_in = cotangent.astype(jnp.float32).reshape(N_DP, SEQ, D)

    def one_sequence(totals, pair):
        sequence, seq_grad = pair
        output, pull = jax.vjp(layer, sequence, *weights)
        grads = pull(seq_grad)
        totals = tuple((total + grad for total, grad in zip(totals, grads[1:])))
        return (totals, (output, grads[0]))
    zeros = tuple((jnp.zeros_like(item) for item in weights))
    totals, (outputs, input_grads) = lax.scan(one_sequence, zeros, (inputs, grads_in))
    return (outputs.reshape(TOKENS, D).astype(jnp.bfloat16), input_grads.reshape(TOKENS, D).astype(jnp.bfloat16), totals[0], totals[1], totals[2], totals[3], totals[4], totals[5], totals[6], totals[7], totals[8], totals[9], totals[10], totals[11])
```

```python
import functools

import jax
import jax.numpy as jnp
from jax import lax
from jax.experimental import pallas as pl
from jax.experimental.pallas import tpu as pltpu
from jax.sharding import PartitionSpec as P

EPSILON = 1e-06
LANES = 128
VMEM_LIMIT = 48 * 2**20


def lower(values):
    return values.astype(jnp.bfloat16)


def wide(values):
    return values.astype(jnp.float32)


def matmul(left, right):
    return jnp.dot(left, right, preferred_element_type=jnp.float32)


def first_contract(left, right):
    return lax.dot_general(
        left, right, (((0,), (0,)), ((), ())), preferred_element_type=jnp.float32
    )


def second_contract(left, right):
    return lax.dot_general(
        left, right, (((1,), (1,)), ((), ())), preferred_element_type=jnp.float32
    )


def statistics(values):
    inverse = lax.rsqrt(jnp.mean(values * values, axis=-1, keepdims=True) + EPSILON)
    return (values * inverse, inverse)


def norm_backward(unit, inverse, gain, grad):
    scaled = gain * grad
    return inverse * (scaled - unit * jnp.mean(scaled * unit, axis=-1, keepdims=True))


def partner(values):
    return lax.ppermute(values, "tensor", [(0, 1), (1, 0)])


class Grid:
    def __init__(self):
        self.count = lax.axis_size("dp")
        self.index = lax.axis_index("dp")
        bits = self.count.bit_length() - 1
        self.line_bits = list(range(2, bits))

    def bit(self, number):
        return (self.index >> number) & 1

    def swap(self, values, number):
        pairs = [(i, i ^ (1 << number)) for i in range(self.count)]
        return lax.ppermute(values, "dp", pairs)

    def place(self, pieces):
        rows, columns = pieces[0][1].shape[1:]
        arrays = [piece for _, piece in pieces]
        codes = [code for found, _ in pieces for code in found]
        kind = arrays[0].dtype

        def body(*refs):
            inputs, (result, sem) = refs[: len(arrays)], refs[len(arrays) :]
            here = lax.axis_index("dp")
            copies = []
            for (found, _), ref in zip(pieces, inputs):
                for number, code in enumerate(found):
                    copies.append(
                        pltpu.make_async_copy(
                            ref.at[number], result.at[here ^ code], sem.at[len(copies)]
                        )
                    )
            for copy in copies:
                copy.start()
            for copy in copies:
                copy.wait()

        size = self.count * rows * columns * kind.itemsize
        return pl.pallas_call(
            body,
            out_shape=jax.ShapeDtypeStruct((self.count, rows, columns), kind),
            in_specs=[pl.BlockSpec(memory_space=pl.ANY)] * len(arrays),
            out_specs=pl.BlockSpec(memory_space=pltpu.VMEM),
            scratch_shapes=[pltpu.SemaphoreType.DMA((len(codes),))],
            compiler_params=pltpu.CompilerParams(vmem_limit_bytes=VMEM_LIMIT),
            cost_estimate=pl.CostEstimate(flops=0, bytes_accessed=2 * size, transcendentals=0),
        )(*arrays).reshape(self.count * rows, columns)

    def spread(self, block, codes, number):
        found = self.swap(block, number)
        return found, [code ^ (1 << number) for code in codes]

    def plane_pieces(self, block, codes):
        half = block.shape[0] // 2
        side_x, codes_x = self.spread(block, codes, 0)
        side_y, codes_y = self.spread(block, codes, 1)
        corner_a, codes_a = self.spread(side_x[:half], codes_x[:half], 1)
        corner_b, codes_b = self.spread(side_y[half:], codes_y[half:], 0)
        return [
            (codes, block),
            (codes_x, side_x),
            (codes_y, side_y),
            (codes_a, corner_a),
            (codes_b, corner_b),
        ]

    def gather_line_first(self, shard):
        block, codes = shard[None], [0]
        for number in reversed(self.line_bits):
            found, found_codes = self.spread(block, codes, number)
            block = jnp.concatenate([block, found], axis=0)
            codes = codes + found_codes
        return self.place(self.plane_pieces(block, codes))

    def gather_plane_first(self, shard):
        rows, columns = shard.shape
        halves = shard.reshape(2, rows // 2, columns)
        pieces = self.plane_pieces(halves, [0, 0])
        (_, mine), (_, side_x), (_, side_y), (_, corner_a), (_, corner_b) = pieces
        block = jnp.concatenate([mine, side_x, side_y, corner_a, corner_b], axis=0)
        block = block.reshape(4, rows, columns)
        codes = [0, 1, 2, 3]
        last = self.line_bits[0]
        for number in reversed(self.line_bits[1:]):
            found, found_codes = self.spread(block, codes, number)
            block = jnp.concatenate([block, found], axis=0)
            codes = codes + found_codes
        found, found_codes = self.spread(block, codes, last)
        return self.place([(codes, block), (found_codes, found)])

    def reduce_rows(self, parts, kind=jnp.bfloat16):
        rows = parts.shape[0] // self.count
        line = self.count // 4
        blocks = parts.astype(kind).reshape(line, 2, 2, rows, parts.shape[1])

        def take(terms, axis, place):
            return [lax.dynamic_index_in_dim(t, place, axis, keepdims=False) for t in terms]

        def total(terms):
            return sum(wide(term) for term in terms)

        def step(terms, axis, number):
            side = self.bit(number)
            sent = self.swap(total(take(terms, axis, 1 - side)).astype(kind), number)
            return take(terms, axis, side) + [sent]

        half = line // 2
        first = step(step([blocks[:half]], 1, 1), 1, 0)
        second = step(step([blocks[half:]], 2, 0), 1, 1)
        terms = [jnp.concatenate([total(first), total(second)], axis=0).astype(kind)]
        for number in self.line_bits:
            terms = [t.reshape((t.shape[0] // 2, 2) + t.shape[1:]) for t in terms]
            terms = step(terms, 1, number)
        return total(terms)[0]


def fwd_kernel(scale, head, q_ref, k_ref, v_ref, col_ref, row_ref, o_ref, lse_ref, out_t):
    length, lanes = q_ref.shape
    span = min(256, length)
    lane = lax.broadcasted_iota(jnp.int32, (span, lanes), 1) // head
    below = lax.broadcasted_iota(jnp.int32, (span, span), 0) <= lax.broadcasted_iota(jnp.int32, (span, span), 1)
    v_t = v_ref[...].T
    for h in range(lanes // head):
        for b in range(length // span):
            lo, hi = b * span, (b + 1) * span
            q = jnp.where(lane == h, q_ref[lo:hi, :] * scale, 0).astype(jnp.bfloat16)
            row = row_ref[0, h:h+1, lo:hi]
            diag = second_contract(k_ref[lo:hi, :], q) + row - col_ref[0, lo:hi, h:h+1]
            diag = jnp.where(below, diag, -1e30)
            top = jnp.max(diag, axis=0, keepdims=True)
            if lo:
                off = second_contract(k_ref[:lo, :], q) + row - col_ref[0, :lo, h:h+1]
                top = jnp.maximum(top, jnp.max(off, axis=0, keepdims=True))
            e = jnp.exp(diag - top)
            total = jnp.sum(e, axis=0, keepdims=True)
            v_h = v_t[h*head:(h+1)*head]
            acc = matmul(v_h[:, lo:hi], lower(e))
            if lo:
                e = jnp.exp(off - top)
                total = total + jnp.sum(e, axis=0, keepdims=True)
                acc = acc + matmul(v_h[:, :lo], lower(e))
            out_t[h*head:(h+1)*head, lo:hi] = acc / total
            lse_ref[0, h:h+1, lo:hi] = top + jnp.log(total)
    o_ref[...] = out_t[...].T

def bwd_kernel(scale, head, q_ref, k_ref, v_ref, do_ref, col_ref, row_ref, lse_ref, dq_ref, dk_ref, dv_ref, drow_ref, dcol_ref, dq_t, dk_acc, dv_acc):
    length, lanes = q_ref.shape
    span = min(256, length)
    heads = lanes // head
    lane = lax.broadcasted_iota(jnp.int32, (span, lanes), 1) // head
    sub = lax.broadcasted_iota(jnp.int32, (lanes, length), 0) // head
    below = lax.broadcasted_iota(jnp.int32, (span, span), 0) <= lax.broadcasted_iota(jnp.int32, (span, span), 1)
    k_t = k_ref[...].T
    one = jnp.bfloat16(1)
    for h in range(heads):
        kt_h = jnp.where(sub == h, k_t, one)
        mine = lane == h
        for b in range(length // span):
            lo, hi = b * span, (b + 1) * span
            q = q_ref[lo:hi, :] * jnp.bfloat16(scale)
            qz = jnp.where(mine, q, jnp.bfloat16(0))
            q1 = jnp.where(mine, q, one)
            do = do_ref[lo:hi, :]
            doz = jnp.where(mine, do, jnp.bfloat16(0))
            row = row_ref[0, h:h+1, lo:hi] - lse_ref[0, h:h+1, lo:hi]
            s = second_contract(k_ref[lo:hi, :], qz) + row - col_ref[0, lo:hi, h:h+1]
            p = jnp.exp(jnp.where(below, s, -1e30))
            dp = second_contract(v_ref[lo:hi, :], doz)
            centre = jnp.sum(p * dp, axis=0, keepdims=True)
            if lo:
                s0 = second_contract(k_ref[:lo, :], qz) + row - col_ref[0, :lo, h:h+1]
                p0 = jnp.exp(s0)
                dp0 = second_contract(v_ref[:lo, :], doz)
                centre = centre + jnp.sum(p0 * dp0, axis=0, keepdims=True)
            ds = lower(p * (dp - centre))
            dqt = matmul(kt_h[:, lo:hi], ds)
            dv_acc[h, lo:hi, :] = matmul(lower(p), do)
            dk_acc[h, lo:hi, :] = matmul(ds, q1)
            if lo:
                ds0 = lower(p0 * (dp0 - centre))
                dqt = dqt + matmul(kt_h[:, :lo], ds0)
                dv_acc[h, :lo, :] = dv_acc[h, :lo, :] + matmul(lower(p0), do)
                dk_acc[h, :lo, :] = dk_acc[h, :lo, :] + matmul(ds0, q1)
            dq_t[h*head:(h+1)*head, lo:hi] = dqt[h*head:(h+1)*head] * scale
            other = ((h + 1) % heads) * head
            drow_ref[0, h:h+1, lo:hi] = dqt[other:other+1]
    lane_all = lax.broadcasted_iota(jnp.int32, (length, lanes), 1) // head
    dk, dv = dk_acc[0], dv_acc[0]
    for h in range(1, heads):
        dk = jnp.where(lane_all == h, dk_acc[h], dk)
        dv = jnp.where(lane_all == h, dv_acc[h], dv)
    for h in range(heads):
        other = ((h + 1) % heads) * head
        dcol_ref[0, :, h:h+1] = dk_acc[h][:, other:other+1]
    dq_ref[...] = lower(dq_t[...].T)
    dk_ref[...] = lower(dk)
    dv_ref[...] = lower(dv)


def pair_specs(length, groups, per):
    def block(offset):
        return pl.BlockSpec((length, LANES), lambda group: (0, group + offset))

    column = pl.BlockSpec((1, length, per), lambda group: (group, 0, 0))
    row = pl.BlockSpec((1, per, length), lambda group: (group, 0, 0))
    return block, column, row


def attention_cost(length, width, head, products):
    return pl.CostEstimate(
        flops=products * length * length * width,
        bytes_accessed=8 * length * width * 2,
        transcendentals=length * length * width // head // 2,
    )


def attend(qk, values, column, row, head):
    length, width = values.shape[0], qk.shape[1] // 2
    groups, per, _ = row.shape
    block, column_spec, row_spec = pair_specs(length, groups, per)
    return pl.pallas_call(
        functools.partial(fwd_kernel, head**-0.5, head),
        grid=(groups,),
        in_specs=[block(0), block(groups), block(0), column_spec, row_spec],
        out_specs=[block(0), row_spec],
        out_shape=[
            jax.ShapeDtypeStruct((length, width), jnp.float32),
            jax.ShapeDtypeStruct(row.shape, jnp.float32),
        ],
        scratch_shapes=[pltpu.VMEM((LANES, length), jnp.float32)],
        cost_estimate=attention_cost(length, width, head, 2),
        compiler_params=pltpu.CompilerParams(vmem_limit_bytes=VMEM_LIMIT),
    )(qk, qk, values, column, row)


def attend_backward(qk, values, grad, column, row, logsum, head):
    length, width = values.shape[0], qk.shape[1] // 2
    groups, per, _ = row.shape
    block, column_spec, row_spec = pair_specs(length, groups, per)
    wide_out = jax.ShapeDtypeStruct((length, width), jnp.bfloat16)
    return pl.pallas_call(
        functools.partial(bwd_kernel, head**-0.5, head),
        grid=(groups,),
        in_specs=[block(0), block(groups), block(0), block(0), column_spec, row_spec, row_spec],
        out_specs=[block(0), block(0), block(0), row_spec, column_spec],
        out_shape=[
            wide_out,
            wide_out,
            wide_out,
            jax.ShapeDtypeStruct(row.shape, jnp.float32),
            jax.ShapeDtypeStruct(column.shape, jnp.float32),
        ],
        scratch_shapes=[
            pltpu.VMEM((LANES, length), jnp.float32),
            pltpu.VMEM((per, length, LANES), jnp.float32),
            pltpu.VMEM((per, length, LANES), jnp.float32),
        ],
        cost_estimate=attention_cost(length, width, head, 5),
        compiler_params=pltpu.CompilerParams(vmem_limit_bytes=VMEM_LIMIT),
    )(qk, qk, values, grad, column, row, logsum)


def per_device(
    tokens,
    w_query,
    w_key,
    w_value,
    w_gate_attn,
    w_forget,
    forget_bias,
    w_out,
    norm_attn,
    norm_mlp,
    w_gate,
    w_up,
    w_down,
    cotangent,
):
    grid = Grid()
    side = lax.axis_index("tensor")
    heads_here = forget_bias.shape[0]
    width = w_query.shape[1]
    head_size = width // heads_here
    hidden_here = w_gate.shape[1]
    scale = head_size ** (-0.5)
    rows_here = tokens.shape[0]
    length = 2 * rows_here

    def in_order(own, other):
        result = jnp.zeros((length,) + own.shape[1:], own.dtype)
        result = lax.dynamic_update_slice_in_dim(result, own, side * rows_here, 0)
        return lax.dynamic_update_slice_in_dim(result, other, (1 - side) * rows_here, 0)

    def gather_rows(values):
        return in_order(values, partner(values))

    def reduce_pair(values):
        own = lax.dynamic_slice_in_dim(values, side * rows_here, rows_here, 0)
        other = lax.dynamic_slice_in_dim(values, (1 - side) * rows_here, rows_here, 0)
        return own + partner(other)

    own_gains = jnp.stack([norm_attn, norm_mlp])
    other_gains = partner(own_gains)
    pair_gains = jnp.where(
        side == 0,
        jnp.concatenate([own_gains, other_gains], axis=1),
        jnp.concatenate([other_gains, own_gains], axis=1),
    )
    gains = grid.gather_line_first(pair_gains)
    gains = gains.reshape(grid.count, 2, pair_gains.shape[1])
    gain_attn = gains[:, 0].reshape(-1)
    gain_mlp = gains[:, 1].reshape(-1)

    padding = jnp.zeros((w_forget.shape[0], LANES - heads_here), jnp.bfloat16)
    pack_qk = grid.gather_line_first(
        jnp.concatenate([lower(w_query), lower(w_key)], axis=1)
    )
    pack_vf = grid.gather_plane_first(
        jnp.concatenate([lower(w_value), lower(w_forget), padding], axis=1)
    )
    pack_go = grid.gather_line_first(
        jnp.concatenate([lower(w_gate_attn), lower(w_out).T], axis=1)
    )
    pack_gu = grid.gather_line_first(jnp.concatenate([lower(w_gate), lower(w_up)], axis=1))
    pack_d = grid.gather_plane_first(lower(w_down).T)

    residual = wide(tokens)
    unit_attn, inverse_attn = statistics(residual)
    normed_attn = gather_rows(lower(unit_attn * gain_attn))
    qk = lower(matmul(normed_attn, pack_qk))
    vf = matmul(normed_attn, pack_vf)
    values_all = lower(vf[:, :width])
    forget_logit = vf[:, width : width + heads_here] + forget_bias
    decay = jnp.cumsum(-jnp.log1p(jnp.exp(-forget_logit)), axis=0)
    per = LANES // head_size
    groups = heads_here // per
    decay_column = decay.reshape(length, groups, per).transpose(1, 0, 2)
    decay_row = decay.T.reshape(groups, per, length)
    gate_w = pack_go[:, :width]
    out_w = pack_go[:, width:]
    gate_logit = matmul(normed_attn, gate_w)
    attended, logsum = attend(qk, values_all, decay_column, decay_row, head_size)
    gate_sig = jax.nn.sigmoid(gate_logit)
    gated = lower(attended * gate_sig)
    middle = residual + reduce_pair(second_contract(gated, out_w))
    unit_mlp, inverse_mlp = statistics(middle)
    own_normed = lower(unit_mlp * gain_mlp)
    normed_mlp = jnp.concatenate([own_normed, partner(own_normed)], axis=0)
    act = matmul(normed_mlp, pack_gu)
    gate_act = act[:, :hidden_here]
    up_act = act[:, hidden_here:]
    gate_sigmoid = jax.nn.sigmoid(gate_act)
    hidden = lower(gate_act * gate_sigmoid * up_act)
    down_rows = second_contract(hidden, pack_d)
    mixed = (middle + (down_rows[:rows_here] + partner(down_rows[rows_here:]))).astype(
        jnp.bfloat16
    )
    grad_output = jnp.concatenate([cotangent, partner(cotangent)], axis=0)
    down_part = lower(first_contract(grad_output, hidden))
    grad_hidden = matmul(grad_output, pack_d)
    grad_up = lower(grad_hidden * (gate_act * gate_sigmoid))
    grad_gate = lower(grad_hidden * up_act * gate_sigmoid * (1.0 + gate_act * (1.0 - gate_sigmoid)))
    grad_gu = jnp.concatenate([grad_gate, grad_up], axis=1)
    down_grad = grid.reduce_rows(down_part).T
    gu_grad = grid.reduce_rows(lower(first_contract(normed_mlp, grad_gu)))
    normed_rows = second_contract(grad_gu, pack_gu)
    grad_normed_mlp = normed_rows[:rows_here] + partner(normed_rows[rows_here:])
    gain_mlp_part = jnp.sum(grad_normed_mlp * unit_mlp, axis=0)
    grad_middle = wide(cotangent) + norm_backward(
        unit_mlp, inverse_mlp, gain_mlp, grad_normed_mlp
    )
    grad_branch = gather_rows(lower(grad_middle))
    out_part = lower(first_contract(grad_branch, gated))
    grad_gated = matmul(grad_branch, out_w)
    grad_attended = lower(grad_gated * gate_sig)
    grad_gate_logit = lower(grad_gated * attended * gate_sig * (1.0 - gate_sig))
    out_grad = grid.reduce_rows(out_part).T
    gate_attn_grad = grid.reduce_rows(lower(first_contract(normed_attn, grad_gate_logit)))

    grad_queries, grad_keys, grad_values, row_total, column_total = attend_backward(
        qk, values_all, grad_attended, decay_column, decay_row, logsum, head_size
    )
    grad_decay = row_total.reshape(heads_here, length).T - column_total.transpose(
        1, 0, 2
    ).reshape(length, heads_here)
    grad_log = lax.cumsum(grad_decay, axis=0, reverse=True)
    grad_forget = lower(grad_log * jax.nn.sigmoid(-forget_logit))
    bias_part = jnp.sum(grad_forget.astype(jnp.float32), axis=0)
    grad_qk = jnp.concatenate([grad_queries, grad_keys], axis=1)
    grad_vf = jnp.concatenate(
        [grad_values, grad_forget, jnp.zeros((length, LANES - heads_here), jnp.bfloat16)], axis=1
    )
    qk_grad = grid.reduce_rows(lower(first_contract(normed_attn, grad_qk)))
    vf_grad = grid.reduce_rows(lower(first_contract(normed_attn, grad_vf)))
    grad_normed_attn = reduce_pair(
        second_contract(grad_qk, pack_qk)
        + second_contract(grad_vf, pack_vf)
        + second_contract(grad_gate_logit, gate_w)
    )
    gain_attn_part = jnp.sum(grad_normed_attn * unit_attn, axis=0)
    tokens_grad = (
        grad_middle + norm_backward(unit_attn, inverse_attn, gain_attn, grad_normed_attn)
    ).astype(jnp.bfloat16)
    small = jnp.concatenate(
        [
            gain_attn_part.reshape(grid.count, -1),
            gain_mlp_part.reshape(grid.count, -1),
            jnp.broadcast_to(bias_part[None, :], (grid.count, heads_here)),
        ],
        axis=1,
    )
    small_sum = grid.reduce_rows(small, jnp.float32).reshape(-1)
    share = norm_attn.shape[0]
    gain_sums = small_sum[: 4 * share].reshape(2, 2, share)
    other_sums = lax.dynamic_index_in_dim(gain_sums, 1 - side, 1, keepdims=False)
    own_sums = lax.dynamic_index_in_dim(gain_sums, side, 1, keepdims=False)
    gain_grads = own_sums + partner(other_sums)
    return (
        mixed,
        tokens_grad,
        qk_grad[:, :width],
        qk_grad[:, width:],
        vf_grad[:, :width],
        gate_attn_grad,
        vf_grad[:, width : width + heads_here],
        small_sum[4 * share :],
        out_grad,
        gain_grads[0],
        gain_grads[1],
        gu_grad[:, :hidden_here],
        gu_grad[:, hidden_here:],
        down_grad,
    )


def solution(mesh):
    return jax.shard_map(
        per_device,
        mesh=mesh,
        in_specs=(
            P(("dp", "tensor"), None),
            P("dp", "tensor"),
            P("dp", "tensor"),
            P("dp", "tensor"),
            P("dp", "tensor"),
            P("dp", "tensor"),
            P("tensor"),
            P("tensor", "dp"),
            P(("dp", "tensor")),
            P(("dp", "tensor")),
            P("dp", "tensor"),
            P("dp", "tensor"),
            P("tensor", "dp"),
            P(("dp", "tensor"), None),
        ),
        out_specs=(
            P(("dp", "tensor"), None),
            P(("dp", "tensor"), None),
            P("dp", "tensor"),
            P("dp", "tensor"),
            P("dp", "tensor"),
            P("dp", "tensor"),
            P("dp", "tensor"),
            P("tensor"),
            P("tensor", "dp"),
            P(("dp", "tensor")),
            P(("dp", "tensor")),
            P("dp", "tensor"),
            P("dp", "tensor"),
            P("tensor", "dp"),
        ),
        check_vma=False,
    )
```

```python
import functools

import jax
import jax.numpy as jnp
from jax import lax
from jax.experimental import pallas as pl
from jax.experimental.pallas import tpu as pltpu
from jax.sharding import PartitionSpec as P

EPSILON = 1e-06
LANES = 128
VMEM_LIMIT = 50 * 2**20
COST_SCALE = 0.02


def lower(values):
    return values.astype(jnp.bfloat16)


def wide(values):
    return values.astype(jnp.float32)


def matmul(left, right):
    return jnp.dot(left, right, preferred_element_type=jnp.float32)


def first_contract(left, right):
    return lax.dot_general(
        left, right, (((0,), (0,)), ((), ())), preferred_element_type=jnp.float32
    )


def second_contract(left, right):
    return lax.dot_general(
        left, right, (((1,), (1,)), ((), ())), preferred_element_type=jnp.float32
    )


def statistics(values):
    inverse = lax.rsqrt(jnp.mean(values * values, axis=-1, keepdims=True) + EPSILON)
    return (values * inverse, inverse)


def norm_backward(unit, inverse, gain, grad):
    scaled = gain * grad
    return inverse * (scaled - unit * jnp.mean(scaled * unit, axis=-1, keepdims=True))


def partner(values):
    return lax.ppermute(values, "tensor", [(0, 1), (1, 0)])


def tie(value, *others):
    if not others:
        return value
    return lax.optimization_barrier((value, *others))[0]


def small_cost(flops, size):
    return pl.CostEstimate(
        flops=int(COST_SCALE * flops), bytes_accessed=int(COST_SCALE * size), transcendentals=0
    )


class Grid:
    def __init__(self):
        self.count = lax.axis_size("dp")
        self.index = lax.axis_index("dp")
        bits = self.count.bit_length() - 1
        self.line_bits = list(range(2, bits))

    def bit(self, number):
        return (self.index >> number) & 1

    def swap(self, values, number):
        pairs = [(i, i ^ (1 << number)) for i in range(self.count)]
        return lax.ppermute(values, "dp", pairs)

    def place(self, pieces, splits):
        rows = pieces[0][1].shape[1]
        arrays = [piece for _, piece in pieces]
        codes = [code for found, _ in pieces for code in found]
        kind = arrays[0].dtype

        def body(*refs):
            inputs, results, sem = refs[: len(arrays)], refs[len(arrays) : -1], refs[-1]
            here = lax.axis_index("dp")
            copies = []
            for (found, _), ref in zip(pieces, inputs):
                for number, code in enumerate(found):
                    start = 0
                    for width, result in zip(splits, results):
                        copies.append(
                            pltpu.make_async_copy(
                                ref.at[number, :, pl.ds(start, width)],
                                result.at[here ^ code],
                                sem.at[len(copies)],
                            )
                        )
                        start += width
            for copy in copies:
                copy.start()
            for copy in copies:
                copy.wait()

        size = self.count * rows * sum(splits) * kind.itemsize
        results = pl.pallas_call(
            body,
            out_shape=[jax.ShapeDtypeStruct((self.count, rows, w), kind) for w in splits],
            in_specs=[pl.BlockSpec(memory_space=pl.ANY)] * len(arrays),
            out_specs=[pl.BlockSpec(memory_space=pltpu.VMEM)] * len(splits),
            scratch_shapes=[pltpu.SemaphoreType.DMA((len(codes) * len(splits),))],
            compiler_params=pltpu.CompilerParams(vmem_limit_bytes=VMEM_LIMIT),
            cost_estimate=small_cost(0, 2 * size),
        )(*arrays)
        return [r.reshape(self.count * rows, w) for r, w in zip(results, splits)]


class Weight:
    def __init__(self, grid, pieces, first=0, width=None):
        self.grid, self.pieces, self.first = grid, pieces, first
        self.rows = pieces[0][1].shape[1]
        self.width = width or pieces[0][1].shape[2]
        self.in_kernel = self.rows % 16 == 0

    def part(self, first, width):
        return Weight(self.grid, self.pieces, self.first + first, width)

    def arrays(self):
        return [piece for _, piece in self.pieces]

    def assembled(self):
        pieces = [
            (codes, piece[:, :, self.first : self.first + self.width])
            for codes, piece in self.pieces
        ]
        return self.grid.place(pieces, [self.width])[0]

    def copies(self, refs, target, sem, tiles):
        here = lax.axis_index("dp")
        tile = self.width // tiles
        found = []
        for step in range(tiles):
            for (codes, _), ref in zip(self.pieces, refs):
                for number, code in enumerate(codes):
                    block = here ^ code
                    source = ref.at[number, :, pl.ds(self.first + step * tile, tile)]
                    found.append(
                        pltpu.make_async_copy(source, target(step, block), sem.at[step, block])
                    )
        return found


def multiply(left, weight, tiles, epilogue, extras, outs):
    if not weight.in_kernel:
        return epilogue(matmul(left, weight.assembled()), *extras)
    grid, rows = weight.grid, weight.rows
    length, depth = left.shape
    tile = weight.width // tiles
    arrays = weight.arrays()

    def body(*refs):
        left_ref, refs = refs[0], refs[1:]
        piece_refs, refs = refs[: len(arrays)], refs[len(arrays) :]
        extra_refs, refs = refs[: len(extras)], refs[len(extras) :]
        out_refs, (held, sem) = refs[: len(outs)], refs[len(outs) :]
        step = pl.program_id(0)

        def target(place, block):
            return held.at[place, pl.ds(pl.multiple_of(block * rows, 16), rows)]

        @pl.when(step == 0)
        def _():
            for copy in weight.copies(piece_refs, target, sem, tiles):
                copy.start()

        for block in range(grid.count):
            there = target(step, block)
            pltpu.make_async_copy(there, there, sem.at[step, block]).wait()
        results = epilogue(matmul(left_ref[...], held[step]), *[ref[...] for ref in extra_refs])
        for ref, result in zip(out_refs, results):
            ref[...] = result

    def column_block(width):
        return pl.BlockSpec((length, width // tiles), lambda step: (0, step))

    size = (
        left.size * 2
        + depth * weight.width * 2
        + sum(e.size * e.dtype.itemsize for e in extras)
        + sum(length * w * jnp.dtype(kind).itemsize for w, kind in outs)
    )
    return pl.pallas_call(
        body,
        grid=(tiles,),
        in_specs=[pl.BlockSpec((length, depth), lambda step: (0, 0))]
        + [pl.BlockSpec(memory_space=pl.ANY)] * len(arrays)
        + [column_block(extra.shape[1]) for extra in extras],
        out_specs=[column_block(width) for width, _ in outs],
        out_shape=[jax.ShapeDtypeStruct((length, width), kind) for width, kind in outs],
        scratch_shapes=[
            pltpu.VMEM((tiles, depth, tile), jnp.bfloat16),
            pltpu.SemaphoreType.DMA((tiles, grid.count)),
        ],
        cost_estimate=small_cost(2 * length * depth * weight.width, size),
        compiler_params=pltpu.CompilerParams(vmem_limit_bytes=VMEM_LIMIT),
    )(left, *arrays, *extras)


def multiply_back(terms, half, tiles=4):
    grid, rows = terms[0][1].grid, terms[0][1].rows
    length = terms[0][0].shape[0] // 2
    if not terms[0][1].in_kernel:
        return sum(
            second_contract(
                lax.dynamic_slice_in_dim(left, half * length, length, 0), weight.assembled()
            )
            for left, weight in terms
        )
    depth = grid.count * rows
    tile, share = depth // tiles, grid.count // tiles
    sources, counts = [], []
    for _, weight in terms:
        sources = sources + weight.arrays()
        counts.append(len(weight.pieces))

    def body(half_ref, *refs):
        left_refs, refs = refs[: len(terms)], refs[len(terms) :]
        piece_refs, refs = refs[: len(sources)], refs[len(sources) :]
        out_ref, held, sems = refs[0], refs[1 : 1 + len(terms)], refs[1 + len(terms) :]
        step = pl.program_id(0)

        def target(number):
            def found(_, block):
                return held[number].at[pl.ds(pl.multiple_of(block * rows, 16), rows)]

            return found

        @pl.when(step == 0)
        def _():
            first = 0
            for number, (_, weight) in enumerate(terms):
                mine = piece_refs[first : first + counts[number]]
                first += counts[number]
                for copy in weight.copies(mine, target(number), sems[number], 1):
                    copy.start()

        total = None
        for number in range(len(terms)):
            for part in range(share):
                block = step * share + part
                there = target(number)(0, block)
                pltpu.make_async_copy(there, there, sems[number].at[0, block]).wait()
            found = held[number][pl.ds(pl.multiple_of(step * tile, 16), tile), :]
            product = second_contract(left_refs[number][...], found)
            total = product if total is None else total + product
        out_ref[...] = total

    size = length * depth * 4 + sum(l.size + depth * w.width * 2 for l, w in terms)
    flops = sum(2 * length * depth * w.width for _, w in terms)
    return pl.pallas_call(
        body,
        grid_spec=pltpu.PrefetchScalarGridSpec(
            num_scalar_prefetch=1,
            grid=(tiles,),
            in_specs=[
                pl.BlockSpec((length, left.shape[1]), lambda step, which: (which[0], 0))
                for left, _ in terms
            ]
            + [pl.BlockSpec(memory_space=pl.ANY)] * len(sources),
            out_specs=pl.BlockSpec((length, tile), lambda step, which: (0, step)),
            scratch_shapes=[pltpu.VMEM((depth, w.width), jnp.bfloat16) for _, w in terms]
            + [pltpu.SemaphoreType.DMA((1, grid.count)) for _ in terms],
        ),
        out_shape=jax.ShapeDtypeStruct((length, depth), jnp.float32),
        cost_estimate=small_cost(flops, size),
        compiler_params=pltpu.CompilerParams(vmem_limit_bytes=VMEM_LIMIT),
    )(jnp.reshape(half, (1,)).astype(jnp.int32), *[left for left, _ in terms], *sources)


class Gather:
    def __init__(self, grid, shard, fine=False, after_line=(), after_plane=()):
        near, codes = tie(shard[None], *after_line), [0]
        for number in reversed(grid.line_bits[1:]):
            found = grid.swap(near, number)
            near = jnp.concatenate([near, found], axis=0)
            codes = codes + [code ^ (1 << number) for code in codes]
        last = grid.line_bits[0]
        far = grid.swap(near, last)
        far_codes = [code ^ (1 << last) for code in codes]

        def moved(found, plane):
            return [code ^ plane for code in found]

        half = len(codes)
        if fine:
            near_x, near_y = grid.swap(near, 0), grid.swap(near, 1)
            far_x, far_y = grid.swap(far, 0), grid.swap(far, 1)
            sides = [
                (codes, near),
                (far_codes, far),
                (moved(codes, 1), near_x),
                (moved(codes, 2), near_y),
                (moved(far_codes, 1), far_x),
                (moved(far_codes, 2), far_y),
            ]
            self.sides_done = (near_x, near_y, far_x, far_y)
        else:
            block = tie(jnp.concatenate([near, far], axis=0), *after_plane)
            side_x, side_y = grid.swap(block, 0), grid.swap(block, 1)
            near_x, far_y = side_x[:half], side_y[half:]
            both = codes + far_codes
            sides = [(both, block), (moved(both, 1), side_x), (moved(both, 2), side_y)]
            self.sides_done = (side_x, side_y)
        near_corner, far_corner = grid.swap(near_x, 1), grid.swap(far_y, 0)
        self.line_done, self.plane_done = (far,), (near_corner, far_corner, *self.sides_done)
        self.ready = far if fine else block
        corners = [(moved(codes, 3), near_corner), (moved(far_codes, 3), far_corner)]
        self.weight = Weight(grid, sides + corners)


def gradient_parts(grid, pairs, tiles, number):
    depth, length = pairs[0][0].shape
    rows, line = depth // grid.count, grid.count // 4
    width = sum(right.shape[1] for _, right in pairs)
    lefts = []
    for left, _ in pairs:
        if not any(left is other for other in lefts):
            lefts.append(left)
    which = [[left is other for other in lefts].index(True) for left, _ in pairs]
    tile = width // tiles
    starts, first = [], 0
    for _, right in pairs:
        starts.append(first)
        first += right.shape[1]

    def body(*refs):
        left_refs, refs = refs[: len(lefts)], refs[len(lefts) :]
        right_refs, refs = refs[: len(pairs)], refs[len(pairs) :]
        away, own, total = refs
        step = pl.program_id(0)
        if tiles == 1:
            for place in range(len(pairs)):
                ahead = starts[place]
                total[:, ahead : ahead + pairs[place][1].shape[1]] = matmul(
                    left_refs[which[place]][...], right_refs[place][...]
                )
        elif len(pairs) == 1:
            total[...] = matmul(left_refs[0][...], right_refs[0][...])
        else:
            for place in range(len(pairs)):
                low = starts[place] // tile
                high = low + pairs[place][1].shape[1] // tile

                @pl.when((step >= low) & (step < high))
                def _():
                    total[...] = matmul(left_refs[which[place]][...], right_refs[place][...])

        here = (lax.axis_index("dp") >> number) & 1

        def block(place):
            return lower(total[pl.ds(pl.multiple_of(place * rows, 8), rows), :])

        other = 3 - (1 << number)
        for place in range(line):
            for side in range(2):
                base = place * 4 + side * other
                away[place, side] = block(base + ((1 - here) << number))
                own[place, side] = block(base + (here << number))

    def right_spec(place):
        columns = pairs[place][1].shape[1]
        if tiles == 1:
            return pl.BlockSpec((length, columns), lambda step: (0, 0))
        low, count = starts[place] // tile, columns // tile
        return pl.BlockSpec((length, tile), lambda step: (0, jnp.clip(step - low, 0, count - 1)))

    out = jax.ShapeDtypeStruct((line, 2, rows, width), jnp.bfloat16)
    out_spec = pl.BlockSpec((line, 2, rows, tile), lambda step: (0, 0, 0, step))
    size = depth * width * 2 + sum(l.size * 2 for l in lefts) + sum(r.size * 2 for _, r in pairs)
    return pl.pallas_call(
        body,
        grid=(tiles,),
        in_specs=[pl.BlockSpec((depth, length), lambda step: (0, 0))] * len(lefts)
        + [right_spec(place) for place in range(len(pairs))],
        out_specs=[out_spec] * 2,
        out_shape=[out] * 2,
        scratch_shapes=[pltpu.VMEM((depth, tile), jnp.float32)],
        cost_estimate=small_cost(2 * depth * length * width, size),
        compiler_params=pltpu.CompilerParams(vmem_limit_bytes=VMEM_LIMIT),
    )(*lefts, *[right for _, right in pairs])


def pick(array, axis, place):
    return lax.dynamic_index_in_dim(array, place, axis, keepdims=False)


def cut_parts(grid, array, number):
    line, rows = grid.count // 4, array.shape[0] // grid.count
    blocks = array.reshape(line, 2, 2, rows, array.shape[1])
    here, axis = grid.bit(number), 2 - number
    return pick(blocks, axis, 1 - here), pick(blocks, axis, here)


def weight_gradient(grid, pairs, tiles, number):
    rows = pairs[0][0].shape[0] // grid.count
    if rows % 16 == 0:
        return Reduce(grid, gradient_parts(grid, pairs, tiles, number), number)
    found = [lower(matmul(left, right)) for left, right in pairs]
    return Reduce(grid, cut_parts(grid, jnp.concatenate(found, axis=1), number), number)


def add_halves(terms, number):
    count, _, rows, columns = terms[0].shape
    tile = next(t for t in (512, 384, 256, 128, columns) if columns % t == 0)

    def body(*refs):
        inputs, (away, kept) = refs[: len(terms)], refs[len(terms) :]
        side = (lax.axis_index("dp") >> number) & 1
        for place in range(count):
            away[place] = lower(sum(wide(ref[place, 1 - side]) for ref in inputs))
            kept[place] = lower(sum(wide(ref[place, side]) for ref in inputs))

    block = pl.BlockSpec((count, 2, rows, tile), lambda step: (0, 0, 0, step))
    half = pl.BlockSpec((count, rows, tile), lambda step: (0, 0, step))
    size = terms[0].size * (2 * len(terms) + 2)
    return pl.pallas_call(
        body,
        grid=(columns // tile,),
        in_specs=[block] * len(terms),
        out_specs=[half] * 2,
        out_shape=[jax.ShapeDtypeStruct((count, rows, columns), jnp.bfloat16)] * 2,
        cost_estimate=small_cost(0, size),
        compiler_params=pltpu.CompilerParams(vmem_limit_bytes=VMEM_LIMIT),
    )(*terms)


def joined_rows(own, other, in_sequence):
    rows, columns = own.shape
    tile = columns // 4

    def body(own_ref, other_ref, rows_ref, turned_ref):
        first, second = own_ref[...], other_ref[...]
        if in_sequence:
            ahead = lax.axis_index("tensor") == 0
            first, second = jnp.where(ahead, first, second), jnp.where(ahead, second, first)
        rows_ref[:rows] = first
        rows_ref[rows:] = second
        turned_ref[:, :rows] = first.T
        turned_ref[:, rows:] = second.T

    block = pl.BlockSpec((rows, tile), lambda step: (0, step))
    return pl.pallas_call(
        body,
        grid=(4,),
        in_specs=[block] * 2,
        out_specs=[
            pl.BlockSpec((2 * rows, tile), lambda step: (0, step)),
            pl.BlockSpec((tile, 2 * rows), lambda step: (step, 0)),
        ],
        out_shape=[
            jax.ShapeDtypeStruct((2 * rows, columns), own.dtype),
            jax.ShapeDtypeStruct((columns, 2 * rows), own.dtype),
        ],
        cost_estimate=small_cost(0, 12 * rows * columns),
        compiler_params=pltpu.CompilerParams(vmem_limit_bytes=VMEM_LIMIT),
    )(own, other)


def row_kernel(body, inputs, outs, sums=0):
    length, columns = inputs[0].shape
    tile = length // 4

    def spec(rows):
        if rows == 1:
            return pl.BlockSpec((1, columns), lambda step: (0, 0))
        return pl.BlockSpec((tile, columns), lambda step: (step, 0))

    def kernel(*refs):
        found = body(*[ref[...] for ref in refs[: len(inputs)]])
        out_refs = refs[len(inputs) :]
        for ref, value in zip(out_refs[: len(outs)], found):
            ref[...] = value
        for ref, value in zip(out_refs[len(outs) :], found[len(outs) :]):

            @pl.when(pl.program_id(0) == 0)
            def _():
                ref[...] = jnp.zeros_like(ref)

            ref[...] += value

    size = length * columns * (sum(i.dtype.itemsize for i in inputs) + 4 * len(outs))
    return pl.pallas_call(
        kernel,
        grid=(4,),
        in_specs=[spec(i.shape[0]) for i in inputs],
        out_specs=[spec(length)] * len(outs) + [spec(1)] * sums,
        out_shape=[jax.ShapeDtypeStruct((length, columns), kind) for kind in outs]
        + [jax.ShapeDtypeStruct((1, columns), jnp.float32)] * sums,
        cost_estimate=small_cost(0, size),
        compiler_params=pltpu.CompilerParams(vmem_limit_bytes=VMEM_LIMIT),
    )(*inputs)


def norm_forward(residual, own, arrived, gain):
    middle = wide(residual) + (own + arrived)
    unit, _ = statistics(middle)
    return middle, lower(unit * gain)


def norm_gradient(source, own, arrived, base, gain):
    unit, inverse = statistics(wide(source))
    grad = own + arrived
    total = wide(base) + norm_backward(unit, inverse, gain, grad)
    return total, lower(total), jnp.sum(grad * unit, axis=0, keepdims=True)


class Reduce:
    def __init__(self, grid, parts, number):
        self.grid, self.number = grid, number
        self.sent, own = parts
        self.kind = own.dtype
        self.terms = [own]

    def start(self, *after):
        self.got = self.grid.swap(tie(self.sent, *after), self.number)
        return self

    def step(self, number, after):
        terms = self.terms + [tie(self.got, *after)]
        if number >= 2:
            terms = [t.reshape((t.shape[0] // 2, 2) + t.shape[1:]) for t in terms]
        if self.kind == jnp.bfloat16:
            self.sent, kept = add_halves(terms, number)
            self.terms = [kept]
        else:
            side = self.grid.bit(number)
            self.sent = sum(pick(t, 1, 1 - side) for t in terms)
            self.terms = [pick(t, 1, side) for t in terms]
        self.got = self.grid.swap(self.sent, number)
        return self

    def second(self, *after):
        return self.step(1 - self.number, after)

    def third(self, *after):
        return self.step(self.grid.line_bits[0], after)

    def fourth(self, *after):
        for number in self.grid.line_bits[1:]:
            self.step(number, after)
        return self

    def result(self):
        return sum(wide(term[0]) for term in self.terms + [self.got])


def running_sum(values, reverse):
    length = values.shape[1]
    place = lax.broadcasted_iota(jnp.int32, values.shape, 1)
    shift = 1
    while shift < length:
        if reverse:
            moved = jnp.where(place < length - shift, pltpu.roll(values, length - shift, 1), 0.0)
        else:
            moved = jnp.where(place >= shift, pltpu.roll(values, shift, 1), 0.0)
        values = values + moved
        shift *= 2
    return values


def decay_kernel(heads, logit_ref, bias_ref, row_ref, column_ref):
    length, lanes = logit_ref.shape
    groups, per, _ = row_ref.shape
    padded = -(-heads // 8) * 8
    logit = (logit_ref[...] + bias_ref[...]).T[:padded]
    decay = running_sum(-jnp.log1p(jnp.exp(-logit)), False)
    columns = jnp.concatenate([decay, jnp.zeros((lanes - padded, length), jnp.float32)], axis=0).T
    for group in range(groups):
        row_ref[group] = decay[group * per : (group + 1) * per]
        column_ref[group] = columns[:, group * per : (group + 1) * per]


def decays(logit, bias, heads, per):
    length = logit.shape[0]
    groups = heads // per
    return pl.pallas_call(
        functools.partial(decay_kernel, heads),
        out_shape=[
            jax.ShapeDtypeStruct((groups, per, length), jnp.float32),
            jax.ShapeDtypeStruct((groups, length, per), jnp.float32),
        ],
        compiler_params=pltpu.CompilerParams(vmem_limit_bytes=VMEM_LIMIT),
    )(logit, bias)


def forget_kernel(heads, row_ref, column_ref, logit_ref, bias_ref, grad_ref, sum_ref):
    length, lanes = logit_ref.shape
    groups, per, _ = row_ref.shape
    padded = -(-heads // 8) * 8
    rows = [row_ref[group] for group in range(groups)]
    columns = [column_ref[group] for group in range(groups)]
    columns = jnp.concatenate(
        columns + [jnp.zeros((length, lanes - heads), jnp.float32)], axis=1
    ).T[:padded]
    if padded > heads:
        rows = rows + [jnp.zeros((padded - heads, length), jnp.float32)]
    grad_log = running_sum(jnp.concatenate(rows, axis=0) - columns, True)
    grad_log = jnp.concatenate([grad_log, jnp.zeros((lanes - padded, length), jnp.float32)], axis=0).T
    grad = lower(grad_log * jax.nn.sigmoid(-(logit_ref[...] + bias_ref[...])))
    lane = lax.broadcasted_iota(jnp.int32, grad.shape, 1)
    grad = jnp.where(lane < heads, grad, jnp.bfloat16(0))
    grad_ref[...] = grad
    sum_ref[...] = jnp.sum(wide(grad), axis=0, keepdims=True)


def forget_backward(row, column, logit, bias, heads):
    return pl.pallas_call(
        functools.partial(forget_kernel, heads),
        out_shape=[
            jax.ShapeDtypeStruct(logit.shape, jnp.bfloat16),
            jax.ShapeDtypeStruct(bias.shape, jnp.float32),
        ],
        compiler_params=pltpu.CompilerParams(vmem_limit_bytes=VMEM_LIMIT),
    )(row, column, logit, bias)


def fwd_kernel(scale, head, q_ref, k_ref, v_ref, col_ref, row_ref, o_ref, lse_ref, out_t):
    length, lanes = q_ref.shape
    span = min(256, length)
    lane = lax.broadcasted_iota(jnp.int32, (span, lanes), 1) // head
    below = lax.broadcasted_iota(jnp.int32, (span, span), 0) <= lax.broadcasted_iota(jnp.int32, (span, span), 1)
    v_t = v_ref[...].T
    for h in range(lanes // head):
        for b in range(length // span):
            lo, hi = b * span, (b + 1) * span
            q = jnp.where(lane == h, q_ref[lo:hi, :] * scale, 0).astype(jnp.bfloat16)
            row = row_ref[0, h:h+1, lo:hi]
            diag = second_contract(k_ref[lo:hi, :], q) + row - col_ref[0, lo:hi, h:h+1]
            diag = jnp.where(below, diag, -1e30)
            top = jnp.max(diag, axis=0, keepdims=True)
            if lo:
                off = second_contract(k_ref[:lo, :], q) + row - col_ref[0, :lo, h:h+1]
                top = jnp.maximum(top, jnp.max(off, axis=0, keepdims=True))
            e = jnp.exp(diag - top)
            total = jnp.sum(e, axis=0, keepdims=True)
            v_h = v_t[h*head:(h+1)*head]
            acc = matmul(v_h[:, lo:hi], lower(e))
            if lo:
                e = jnp.exp(off - top)
                total = total + jnp.sum(e, axis=0, keepdims=True)
                acc = acc + matmul(v_h[:, :lo], lower(e))
            out_t[h*head:(h+1)*head, lo:hi] = acc / total
            lse_ref[0, h:h+1, lo:hi] = top + jnp.log(total)
    o_ref[...] = out_t[...].T

def bwd_kernel(scale, head, q_ref, k_ref, v_ref, do_ref, col_ref, row_ref, lse_ref, dq_ref, dk_ref, dv_ref, drow_ref, dcol_ref, dq_t, dk_acc, dv_acc):
    length, lanes = q_ref.shape
    span = min(256, length)
    heads = lanes // head
    lane = lax.broadcasted_iota(jnp.int32, (span, lanes), 1) // head
    sub = lax.broadcasted_iota(jnp.int32, (lanes, length), 0) // head
    below = lax.broadcasted_iota(jnp.int32, (span, span), 0) <= lax.broadcasted_iota(jnp.int32, (span, span), 1)
    k_t = k_ref[...].T
    one = jnp.bfloat16(1)
    for h in range(heads):
        kt_h = jnp.where(sub == h, k_t, one)
        mine = lane == h
        for b in range(length // span):
            lo, hi = b * span, (b + 1) * span
            q = q_ref[lo:hi, :] * jnp.bfloat16(scale)
            qz = jnp.where(mine, q, jnp.bfloat16(0))
            q1 = jnp.where(mine, q, one)
            do = do_ref[lo:hi, :]
            doz = jnp.where(mine, do, jnp.bfloat16(0))
            row = row_ref[0, h:h+1, lo:hi] - lse_ref[0, h:h+1, lo:hi]
            s = second_contract(k_ref[lo:hi, :], qz) + row - col_ref[0, lo:hi, h:h+1]
            p = jnp.exp(jnp.where(below, s, -1e30))
            dp = second_contract(v_ref[lo:hi, :], doz)
            centre = jnp.sum(p * dp, axis=0, keepdims=True)
            if lo:
                s0 = second_contract(k_ref[:lo, :], qz) + row - col_ref[0, :lo, h:h+1]
                p0 = jnp.exp(s0)
                dp0 = second_contract(v_ref[:lo, :], doz)
                centre = centre + jnp.sum(p0 * dp0, axis=0, keepdims=True)
            ds = lower(p * (dp - centre))
            dqt = matmul(kt_h[:, lo:hi], ds)
            dv_acc[h, lo:hi, :] = matmul(lower(p), do)
            dk_acc[h, lo:hi, :] = matmul(ds, q1)
            if lo:
                ds0 = lower(p0 * (dp0 - centre))
                dqt = dqt + matmul(kt_h[:, :lo], ds0)
                dv_acc[h, :lo, :] = dv_acc[h, :lo, :] + matmul(lower(p0), do)
                dk_acc[h, :lo, :] = dk_acc[h, :lo, :] + matmul(ds0, q1)
            dq_t[h*head:(h+1)*head, lo:hi] = dqt[h*head:(h+1)*head] * scale
            other = ((h + 1) % heads) * head
            drow_ref[0, h:h+1, lo:hi] = dqt[other:other+1]
    lane_all = lax.broadcasted_iota(jnp.int32, (length, lanes), 1) // head
    dk, dv = dk_acc[0], dv_acc[0]
    for h in range(1, heads):
        dk = jnp.where(lane_all == h, dk_acc[h], dk)
        dv = jnp.where(lane_all == h, dv_acc[h], dv)
    for h in range(heads):
        other = ((h + 1) % heads) * head
        dcol_ref[0, :, h:h+1] = dk_acc[h][:, other:other+1]
    dq_ref[...] = lower(dq_t[...].T)
    dk_ref[...] = lower(dk)
    dv_ref[...] = lower(dv)


def pair_specs(length, groups, per):
    def block(offset):
        return pl.BlockSpec((length, LANES), lambda group: (0, group + offset))

    column = pl.BlockSpec((1, length, per), lambda group: (group, 0, 0))
    row = pl.BlockSpec((1, per, length), lambda group: (group, 0, 0))
    return block, column, row


def attention_cost(length, width, head, products):
    return small_cost(products * 6 * length * length * width, 16 * length * width)


def attend(qk, values, column, row, head):
    length, width = values.shape[0], qk.shape[1] // 2
    groups, per, _ = row.shape
    block, column_spec, row_spec = pair_specs(length, groups, per)
    return pl.pallas_call(
        functools.partial(fwd_kernel, head**-0.5, head),
        grid=(groups,),
        in_specs=[block(0), block(groups), block(0), column_spec, row_spec],
        out_specs=[block(0), row_spec],
        out_shape=[
            jax.ShapeDtypeStruct((length, width), jnp.float32),
            jax.ShapeDtypeStruct(row.shape, jnp.float32),
        ],
        scratch_shapes=[pltpu.VMEM((LANES, length), jnp.float32)],
        cost_estimate=attention_cost(length, width, head, 2),
        compiler_params=pltpu.CompilerParams(vmem_limit_bytes=VMEM_LIMIT),
    )(qk, qk, values, column, row)


def attend_backward(qk, values, grad, column, row, logsum, head):
    length, width = values.shape[0], qk.shape[1] // 2
    groups, per, _ = row.shape
    block, column_spec, row_spec = pair_specs(length, groups, per)
    wide_out = jax.ShapeDtypeStruct((length, width), jnp.bfloat16)
    return pl.pallas_call(
        functools.partial(bwd_kernel, head**-0.5, head),
        grid=(groups,),
        in_specs=[block(0), block(groups), block(0), block(0), column_spec, row_spec, row_spec],
        out_specs=[block(0), block(0), block(0), row_spec, column_spec],
        out_shape=[
            wide_out,
            wide_out,
            wide_out,
            jax.ShapeDtypeStruct(row.shape, jnp.float32),
            jax.ShapeDtypeStruct(column.shape, jnp.float32),
        ],
        scratch_shapes=[
            pltpu.VMEM((LANES, length), jnp.float32),
            pltpu.VMEM((per, length, LANES), jnp.float32),
            pltpu.VMEM((per, length, LANES), jnp.float32),
        ],
        cost_estimate=attention_cost(length, width, head, 5),
        compiler_params=pltpu.CompilerParams(vmem_limit_bytes=VMEM_LIMIT),
    )(qk, qk, values, grad, column, row, logsum)


def per_device(
    tokens,
    w_query,
    w_key,
    w_value,
    w_gate_attn,
    w_forget,
    forget_bias,
    w_out,
    norm_attn,
    norm_mlp,
    w_gate,
    w_up,
    w_down,
    cotangent,
):
    grid = Grid()
    side = lax.axis_index("tensor")
    heads_here = forget_bias.shape[0]
    width = w_query.shape[1]
    head_size = width // heads_here
    hidden_here = w_gate.shape[1]
    scale = head_size ** (-0.5)
    rows_here = tokens.shape[0]

    other_cotangent = partner(cotangent)
    own_gains = jnp.stack([norm_attn, norm_mlp])
    other_gains = partner(own_gains)
    gains = jnp.where(
        side == 0,
        jnp.concatenate([own_gains, other_gains], axis=1),
        jnp.concatenate([other_gains, own_gains], axis=1),
    )[None]
    gain_codes = [0]
    for number in range(len(grid.line_bits) + 2):
        gains = jnp.concatenate([gains, grid.swap(gains, number)], axis=0)
        gain_codes = gain_codes + [code ^ (1 << number) for code in gain_codes]
    (gains,) = grid.place([(gain_codes, gains)], [gains.shape[2]])
    gains = gains.reshape(grid.count, 2, gains.shape[1])
    gain_attn = gains[:, 0].reshape(-1)
    gain_mlp = gains[:, 1].reshape(-1)

    padding = jnp.zeros((w_forget.shape[0], LANES - heads_here), jnp.bfloat16)
    forget_lanes = jnp.concatenate([lower(w_forget), padding], axis=1)
    load_qk = Gather(grid, jnp.concatenate([lower(w_query), lower(w_key)], axis=1), fine=True)
    load_vf = Gather(
        grid,
        jnp.concatenate([lower(w_value), forget_lanes], axis=1),
        after_line=load_qk.line_done,
        after_plane=load_qk.plane_done,
    )
    load_go = Gather(
        grid,
        jnp.concatenate([lower(w_gate_attn), lower(w_out).T], axis=1),
        after_line=load_vf.line_done,
        after_plane=load_vf.sides_done,
    )
    load_gate = Gather(
        grid, lower(w_gate), after_line=load_go.line_done, after_plane=load_go.sides_done
    )
    load_up = Gather(
        grid, lower(w_up), after_line=load_gate.line_done, after_plane=load_gate.sides_done
    )
    load_down = Gather(
        grid, lower(w_down).T, after_line=load_up.line_done, after_plane=load_up.sides_done
    )
    query_w, key_w = load_qk.weight.part(0, width), load_qk.weight.part(width, width)
    value_w, forget_w = load_vf.weight.part(0, width), load_vf.weight.part(width, LANES)
    gate_w, out_w = load_go.weight.part(0, width), load_go.weight.part(width, width)
    mlp_gate, mlp_up, mlp_down = load_gate.weight, load_up.weight, load_down.weight

    gain_attn, gain_mlp = gain_attn[None], gain_mlp[None]
    (own_attn,) = row_kernel(
        lambda rows, gain: (lower(statistics(wide(rows))[0] * gain),),
        [tokens, gain_attn],
        [jnp.bfloat16],
    )
    normed_attn, normed_attn_t = joined_rows(own_attn, partner(own_attn), True)
    grad_output, grad_output_t = joined_rows(cotangent, other_cotangent, False)

    low = jnp.bfloat16
    (qk,) = multiply(
        normed_attn, load_qk.weight, 3, lambda p: (lower(p),), [], [(2 * width, low)]
    )
    values_all, forget_logit = multiply(
        normed_attn,
        load_vf.weight,
        1,
        lambda p: (lower(p[:, :width]), p[:, width:]),
        [],
        [(width, low), (LANES, jnp.float32)],
    )
    bias_lanes = jnp.pad(forget_bias, (0, LANES - heads_here))[None]
    decay_row, decay_column = decays(forget_logit, bias_lanes, heads_here, LANES // head_size)
    qk = tie(qk, load_gate.ready)
    attended, logsum = attend(qk, values_all, decay_column, decay_row, head_size)

    def gate_output(product, attended):
        sigmoid = jax.nn.sigmoid(product)
        return sigmoid, lower(attended * sigmoid)

    gate_sig, gated = multiply(
        normed_attn, gate_w, 2, gate_output, [attended], [(width, jnp.float32), (width, low)]
    )
    arrived = partner(multiply_back([(gated, out_w)], 1 - side))
    middle, own_normed = row_kernel(
        norm_forward,
        [tokens, multiply_back([(gated, out_w)], side), arrived, gain_mlp],
        [jnp.float32, low],
    )
    normed_mlp, normed_mlp_t = joined_rows(own_normed, partner(own_normed), False)
    (gate_act,) = multiply(
        normed_mlp, mlp_gate, 4, lambda p: (lower(p),), [], [(hidden_here, low)]
    )

    def hidden_units(up, gate):
        gate = wide(gate)
        return lower(up), lower(gate * jax.nn.sigmoid(gate) * up)

    up_act, hidden = multiply(
        normed_mlp, mlp_up, 4, hidden_units, [gate_act], [(hidden_here, low)] * 2
    )
    sum_down = weight_gradient(grid, [(grad_output_t, hidden)], 4, 1).start()
    hidden = tie(hidden, sum_down.sent)
    other_down = multiply_back([(hidden, mlp_down)], jnp.int32(1))
    arrived_down = partner(other_down)

    def hidden_backward(grad, gate, up):
        gate, up = wide(gate), wide(up)
        sigmoid = jax.nn.sigmoid(gate)
        return (
            lower(grad * (gate * sigmoid)),
            lower(grad * up * sigmoid * (1.0 + gate * (1.0 - sigmoid))),
        )

    grad_up, grad_gate = multiply(
        tie(grad_output, other_down),
        mlp_down,
        4,
        hidden_backward,
        [gate_act, up_act],
        [(hidden_here, low)] * 2,
    )
    sum_up = weight_gradient(grid, [(normed_mlp_t, grad_up)], 4, 0).start()
    grad_gate = tie(grad_gate, sum_up.sent)
    sum_gate = weight_gradient(grid, [(normed_mlp_t, grad_gate)], 4, 1)
    grad_gate = tie(grad_gate, sum_gate.sent)
    back = [(grad_gate, mlp_gate), (grad_up, mlp_up)]
    other_part = multiply_back(back, jnp.int32(1))
    arrived = partner(other_part)
    sum_down.second(other_part)
    sum_gate.start(sum_down.sent)
    back = [(tie(grad_gate, sum_down.sent), mlp_gate), (grad_up, mlp_up)]
    grad_middle, own_branch, gain_mlp_part = row_kernel(
        norm_gradient,
        [middle, multiply_back(back, jnp.int32(0)), arrived, cotangent, gain_mlp],
        [jnp.float32, low],
        sums=1,
    )
    other_branch = partner(own_branch)
    own_down = multiply_back([(tie(hidden, own_branch), mlp_down)], jnp.int32(0))
    (mixed,) = row_kernel(
        lambda middle, own, arrived: (lower(middle + (own + arrived)),),
        [middle, own_down, arrived_down],
        [low],
    )
    grad_branch, grad_branch_t = joined_rows(own_branch, tie(other_branch, own_down), True)

    def gate_backward(grad, sigmoid, attended):
        return lower(grad * sigmoid), lower(grad * attended * sigmoid * (1.0 - sigmoid))

    grad_attended, grad_gate_logit = multiply(
        grad_branch,
        out_w,
        2,
        gate_backward,
        [gate_sig, attended],
        [(width, low)] * 2,
    )
    sum_go = weight_gradient(
        grid, [(normed_attn_t, grad_gate_logit), (grad_branch_t, gated)], 4, 0
    ).start()
    sum_up.second(sum_go.sent)
    sum_gate.second(sum_go.sent)
    sum_down.third(sum_go.sent)
    grad_attended = tie(grad_attended, sum_go.sent, sum_up.sent, sum_gate.sent, sum_down.sent)
    grad_queries, grad_keys, grad_values, row_total, column_total = attend_backward(
        qk, values_all, grad_attended, decay_column, decay_row, logsum, head_size
    )
    sum_up.third(grad_queries)
    sum_down.fourth(grad_queries)
    grad_queries = tie(grad_queries, sum_up.sent, sum_down.sent)
    sum_qk = weight_gradient(
        grid, [(normed_attn_t, grad_queries), (normed_attn_t, grad_keys)], 4, 1
    ).start()
    grad_forget, bias_part = forget_backward(
        row_total, column_total, forget_logit, bias_lanes, heads_here
    )
    sum_vf = weight_gradient(
        grid, [(normed_attn_t, tie(grad_values, sum_qk.sent)), (normed_attn_t, grad_forget)], 1, 0
    ).start()
    back = [
        (tie(grad_gate_logit, sum_qk.sent, sum_vf.sent), gate_w),
        (grad_queries, query_w),
        (grad_keys, key_w),
        (grad_values, value_w),
        (grad_forget, forget_w),
    ]
    other_part = multiply_back(back, 1 - side)
    arrived = partner(other_part)
    sum_up.fourth(other_part)
    sum_gate.third(other_part)
    back[1] = (tie(grad_queries, sum_up.sent, sum_gate.sent), query_w)
    own_part = multiply_back(back, side)
    sum_go.second(own_part)
    _, tokens_grad, gain_attn_part = row_kernel(
        norm_gradient,
        [tokens, own_part, arrived, grad_middle, gain_attn],
        [jnp.float32, low],
        sums=1,
    )
    small = jnp.concatenate(
        [
            gain_attn_part.reshape(grid.count, -1),
            gain_mlp_part.reshape(grid.count, -1),
            jnp.broadcast_to(bias_part[:, :heads_here], (grid.count, heads_here)),
        ],
        axis=1,
    )
    sum_gate.fourth(gain_attn_part)
    sum_qk.second(sum_go.sent)
    sum_vf.second(sum_go.sent)
    sum_go.third(sum_qk.sent)
    sum_qk.third(sum_go.sent, sum_vf.sent)
    sum_small = Reduce(grid, cut_parts(grid, small, 1), 1).start(sum_qk.sent)
    sum_vf.third(sum_qk.sent)
    sum_go.fourth(sum_qk.sent)
    sum_small.second(sum_vf.sent)
    sum_qk.fourth(sum_small.sent)
    sum_small.third(sum_qk.sent)
    sum_vf.fourth(sum_qk.sent)
    sum_small.fourth(sum_vf.sent)
    down_grad, up_grad, gate_grad = sum_down.result().T, sum_up.result(), sum_gate.result()
    go_grad, qk_grad, vf_grad = sum_go.result(), sum_qk.result(), sum_vf.result()
    small_sum = sum_small.result().reshape(-1)
    share = norm_attn.shape[0]
    gain_sums = small_sum[: 4 * share].reshape(2, 2, share)
    other_sums = lax.dynamic_index_in_dim(gain_sums, 1 - side, 1, keepdims=False)
    own_sums = lax.dynamic_index_in_dim(gain_sums, side, 1, keepdims=False)
    gain_grads = own_sums + partner(other_sums)
    return (
        mixed,
        tokens_grad,
        qk_grad[:, :width],
        qk_grad[:, width:],
        vf_grad[:, :width],
        go_grad[:, :width],
        vf_grad[:, width : width + heads_here],
        small_sum[4 * share :],
        go_grad[:, width:].T,
        gain_grads[0],
        gain_grads[1],
        gate_grad,
        up_grad,
        down_grad,
    )


def solution(mesh):
    return jax.shard_map(
        per_device,
        mesh=mesh,
        in_specs=(
            P(("dp", "tensor"), None),
            P("dp", "tensor"),
            P("dp", "tensor"),
            P("dp", "tensor"),
            P("dp", "tensor"),
            P("dp", "tensor"),
            P("tensor"),
            P("tensor", "dp"),
            P(("dp", "tensor")),
            P(("dp", "tensor")),
            P("dp", "tensor"),
            P("dp", "tensor"),
            P("tensor", "dp"),
            P(("dp", "tensor"), None),
        ),
        out_specs=(
            P(("dp", "tensor"), None),
            P(("dp", "tensor"), None),
            P("dp", "tensor"),
            P("dp", "tensor"),
            P("dp", "tensor"),
            P("dp", "tensor"),
            P("dp", "tensor"),
            P("tensor"),
            P("tensor", "dp"),
            P(("dp", "tensor")),
            P(("dp", "tensor")),
            P("dp", "tensor"),
            P("dp", "tensor"),
            P("tensor", "dp"),
        ),
        check_vma=False,
    )
```

```python
import functools

import jax
import jax.numpy as jnp
from jax import lax
from jax.experimental import pallas as pl
from jax.experimental.pallas import tpu as pltpu
from jax.sharding import PartitionSpec as P

EPSILON = 1e-06
LANES = 128
VMEM_LIMIT = 50 * 2**20
COST_SCALE = 0.02


def lower(values):
    return values.astype(jnp.bfloat16)


def wide(values):
    return values.astype(jnp.float32)


def matmul(left, right):
    return jnp.dot(left, right, preferred_element_type=jnp.float32)


def first_contract(left, right):
    return lax.dot_general(
        left, right, (((0,), (0,)), ((), ())), preferred_element_type=jnp.float32
    )


def second_contract(left, right):
    return lax.dot_general(
        left, right, (((1,), (1,)), ((), ())), preferred_element_type=jnp.float32
    )


def statistics(values):
    inverse = lax.rsqrt(jnp.mean(values * values, axis=-1, keepdims=True) + EPSILON)
    return (values * inverse, inverse)


def norm_backward(unit, inverse, gain, grad):
    scaled = gain * grad
    return inverse * (scaled - unit * jnp.mean(scaled * unit, axis=-1, keepdims=True))


def partner(values):
    return lax.ppermute(values, "tensor", [(0, 1), (1, 0)])


def tie(value, *others):
    if not others:
        return value
    return lax.optimization_barrier((value, *others))[0]


def small_cost(flops, size):
    return pl.CostEstimate(
        flops=int(COST_SCALE * flops), bytes_accessed=int(COST_SCALE * size), transcendentals=0
    )


class Grid:
    def __init__(self):
        self.count = lax.axis_size("dp")
        self.index = lax.axis_index("dp")
        bits = self.count.bit_length() - 1
        self.line_bits = list(range(2, bits))

    def bit(self, number):
        return (self.index >> number) & 1

    def swap(self, values, number):
        pairs = [(i, i ^ (1 << number)) for i in range(self.count)]
        return lax.ppermute(values, "dp", pairs)

    def place(self, pieces, splits):
        rows = pieces[0][1].shape[1]
        arrays = [piece for _, piece in pieces]
        codes = [code for found, _ in pieces for code in found]
        kind = arrays[0].dtype

        def body(*refs):
            inputs, results, sem = refs[: len(arrays)], refs[len(arrays) : -1], refs[-1]
            here = lax.axis_index("dp")
            copies = []
            for (found, _), ref in zip(pieces, inputs):
                for number, code in enumerate(found):
                    start = 0
                    for width, result in zip(splits, results):
                        copies.append(
                            pltpu.make_async_copy(
                                ref.at[number, :, pl.ds(start, width)],
                                result.at[here ^ code],
                                sem.at[len(copies)],
                            )
                        )
                        start += width
            for copy in copies:
                copy.start()
            for copy in copies:
                copy.wait()

        size = self.count * rows * sum(splits) * kind.itemsize
        results = pl.pallas_call(
            body,
            out_shape=[jax.ShapeDtypeStruct((self.count, rows, w), kind) for w in splits],
            in_specs=[pl.BlockSpec(memory_space=pl.ANY)] * len(arrays),
            out_specs=[pl.BlockSpec(memory_space=pltpu.VMEM)] * len(splits),
            scratch_shapes=[pltpu.SemaphoreType.DMA((len(codes) * len(splits),))],
            compiler_params=pltpu.CompilerParams(vmem_limit_bytes=VMEM_LIMIT),
            cost_estimate=small_cost(0, 2 * size),
        )(*arrays)
        return [r.reshape(self.count * rows, w) for r, w in zip(results, splits)]


class Weight:
    def __init__(self, grid, pieces, first=0, width=None):
        self.grid, self.pieces, self.first = grid, pieces, first
        self.rows = pieces[0][1].shape[1]
        self.width = width or pieces[0][1].shape[2]
        self.in_kernel = self.rows % 16 == 0

    def part(self, first, width):
        return Weight(self.grid, self.pieces, self.first + first, width)

    def arrays(self):
        return [piece for _, piece in self.pieces]

    def assembled(self):
        pieces = [
            (codes, piece[:, :, self.first : self.first + self.width])
            for codes, piece in self.pieces
        ]
        return self.grid.place(pieces, [self.width])[0]

    def copies(self, refs, target, sem, tiles):
        here = lax.axis_index("dp")
        tile = self.width // tiles
        found = []
        for step in range(tiles):
            for (codes, _), ref in zip(self.pieces, refs):
                for number, code in enumerate(codes):
                    block = here ^ code
                    source = ref.at[number, :, pl.ds(self.first + step * tile, tile)]
                    found.append(
                        pltpu.make_async_copy(source, target(step, block), sem.at[step, block])
                    )
        return found


def multiply(left, weight, tiles, epilogue, extras, outs):
    if not weight.in_kernel:
        return epilogue(matmul(left, weight.assembled()), *extras)
    grid, rows = weight.grid, weight.rows
    length, depth = left.shape
    tile = weight.width // tiles
    arrays = weight.arrays()

    def body(*refs):
        left_ref, refs = refs[0], refs[1:]
        piece_refs, refs = refs[: len(arrays)], refs[len(arrays) :]
        extra_refs, refs = refs[: len(extras)], refs[len(extras) :]
        out_refs, (held, sem) = refs[: len(outs)], refs[len(outs) :]
        step = pl.program_id(0)

        def target(place, block):
            return held.at[place, pl.ds(pl.multiple_of(block * rows, 16), rows)]

        @pl.when(step == 0)
        def _():
            for copy in weight.copies(piece_refs, target, sem, tiles):
                copy.start()

        for block in range(grid.count):
            there = target(step, block)
            pltpu.make_async_copy(there, there, sem.at[step, block]).wait()
        results = epilogue(matmul(left_ref[...], held[step]), *[ref[...] for ref in extra_refs])
        for ref, result in zip(out_refs, results):
            ref[...] = result

    def column_block(width):
        return pl.BlockSpec((length, width // tiles), lambda step: (0, step))

    size = (
        left.size * 2
        + depth * weight.width * 2
        + sum(e.size * e.dtype.itemsize for e in extras)
        + sum(length * w * jnp.dtype(kind).itemsize for w, kind in outs)
    )
    return pl.pallas_call(
        body,
        grid=(tiles,),
        in_specs=[pl.BlockSpec((length, depth), lambda step: (0, 0))]
        + [pl.BlockSpec(memory_space=pl.ANY)] * len(arrays)
        + [column_block(extra.shape[1]) for extra in extras],
        out_specs=[column_block(width) for width, _ in outs],
        out_shape=[jax.ShapeDtypeStruct((length, width), kind) for width, kind in outs],
        scratch_shapes=[
            pltpu.VMEM((tiles, depth, tile), jnp.bfloat16),
            pltpu.SemaphoreType.DMA((tiles, grid.count)),
        ],
        cost_estimate=small_cost(2 * length * depth * weight.width, size),
        compiler_params=pltpu.CompilerParams(vmem_limit_bytes=VMEM_LIMIT),
    )(left, *arrays, *extras)


def multiply_back(terms, half, kind=jnp.float32, parts=1, tiles=4):
    grid, rows = terms[0][1].grid, terms[0][1].rows
    length = terms[0][0].shape[0] // 2
    if not terms[0][1].in_kernel:
        total = sum(
            second_contract(
                lax.dynamic_slice_in_dim(left, half * length, length, 0), weight.assembled()
            )
            for left, weight in terms
        )
        return jnp.split(total.astype(kind), parts, axis=1)
    depth = grid.count * rows
    tile, share = depth // tiles, grid.count // tiles
    run = tiles // parts

    def part_spec(number):
        return pl.BlockSpec(
            (length, tile), lambda step, which: (0, jnp.clip(step - number * run, 0, run - 1))
        )

    sources, counts = [], []
    for _, weight in terms:
        sources = sources + weight.arrays()
        counts.append(len(weight.pieces))

    def body(half_ref, *refs):
        left_refs, refs = refs[: len(terms)], refs[len(terms) :]
        piece_refs, refs = refs[: len(sources)], refs[len(sources) :]
        out_refs, refs = refs[:parts], refs[parts:]
        held, sems = refs[: len(terms)], refs[len(terms) :]
        step = pl.program_id(0)

        def target(number):
            def found(_, block):
                return held[number].at[pl.ds(pl.multiple_of(block * rows, 16), rows)]

            return found

        @pl.when(step == 0)
        def _():
            first = 0
            for number, (_, weight) in enumerate(terms):
                mine = piece_refs[first : first + counts[number]]
                first += counts[number]
                for copy in weight.copies(mine, target(number), sems[number], 1):
                    copy.start()

        total = None
        for number in range(len(terms)):
            for part in range(share):
                block = step * share + part
                there = target(number)(0, block)
                pltpu.make_async_copy(there, there, sems[number].at[0, block]).wait()
            found = held[number][pl.ds(pl.multiple_of(step * tile, 16), tile), :]
            product = second_contract(left_refs[number][...], found)
            total = product if total is None else total + product
        for number, out_ref in enumerate(out_refs):

            @pl.when(step // run == number)
            def _():
                out_ref[...] = total.astype(kind)

    size = length * depth * 4 + sum(l.size + depth * w.width * 2 for l, w in terms)
    flops = sum(2 * length * depth * w.width for _, w in terms)
    return pl.pallas_call(
        body,
        grid_spec=pltpu.PrefetchScalarGridSpec(
            num_scalar_prefetch=1,
            grid=(tiles,),
            in_specs=[
                pl.BlockSpec((length, left.shape[1]), lambda step, which: (which[0], 0))
                for left, _ in terms
            ]
            + [pl.BlockSpec(memory_space=pl.ANY)] * len(sources),
            out_specs=[part_spec(number) for number in range(parts)],
            scratch_shapes=[pltpu.VMEM((depth, w.width), jnp.bfloat16) for _, w in terms]
            + [pltpu.SemaphoreType.DMA((1, grid.count)) for _ in terms],
        ),
        out_shape=[jax.ShapeDtypeStruct((length, depth // parts), kind)] * parts,
        cost_estimate=small_cost(flops, size),
        compiler_params=pltpu.CompilerParams(vmem_limit_bytes=VMEM_LIMIT),
    )(jnp.reshape(half, (1,)).astype(jnp.int32), *[left for left, _ in terms], *sources)


class Gather:
    def __init__(self, grid, shard, *after):
        near, codes = tie(shard[None], *after), [0]
        for number in reversed(grid.line_bits[1:]):
            found = grid.swap(near, number)
            near = jnp.concatenate([near, found], axis=0)
            codes = codes + self.moved(codes, 1 << number)
        self.grid, self.near, self.codes = grid, near, codes

    def moved(self, found, plane):
        return [code ^ plane for code in found]

    def line_end(self, *after):
        last = self.grid.line_bits[0]
        self.near = tie(self.near, *after)
        self.far = self.grid.swap(self.near, last)
        self.far_codes = self.moved(self.codes, 1 << last)
        return self

    def plane(self, *after, fine=False):
        grid, near, far, codes, far_codes = (
            self.grid,
            self.near,
            self.far,
            self.codes,
            self.far_codes,
        )
        moved, both, half = self.moved, self.codes + self.far_codes, len(self.codes)
        if fine:
            near_x, near_y = grid.swap(near, 0), grid.swap(near, 1)
            far_x, far_y = grid.swap(far, 0), grid.swap(far, 1)
            sides = [
                (codes, near),
                (far_codes, far),
                (moved(codes, 1), near_x),
                (moved(codes, 2), near_y),
                (moved(far_codes, 1), far_x),
                (moved(far_codes, 2), far_y),
            ]
            received = (near_y, far_x)
        else:
            block = tie(jnp.concatenate([near, far], axis=0), *after)
            side_x, side_y = grid.swap(block, 0), grid.swap(block, 1)
            near_x, far_y = side_x[:half], side_y[half:]
            sides = [(both, block), (moved(both, 1), side_x), (moved(both, 2), side_y)]
            received = ()
            self.block = block
        near_corner, far_corner = grid.swap(near_x, 1), grid.swap(far_y, 0)
        self.corners = (near_corner, far_corner, *received)
        self.corner_parts = (near_x, far_y)
        corners = [(moved(codes, 3), near_corner), (moved(far_codes, 3), far_corner)]
        self.weight = Weight(grid, sides + corners)
        return self


def gradient_parts(grid, pairs, tiles, form):
    depth, length = pairs[0][0].shape
    rows, line = depth // grid.count, grid.count // 4
    width = sum(right.shape[1] for _, right in pairs)
    lefts = []
    for left, _ in pairs:
        if not any(left is other for other in lefts):
            lefts.append(left)
    which = [[left is other for other in lefts].index(True) for left, _ in pairs]
    tile = width // tiles
    starts, first = [], 0
    for _, right in pairs:
        starts.append(first)
        first += right.shape[1]

    def body(*refs):
        left_refs, refs = refs[: len(lefts)], refs[len(lefts) :]
        right_refs, refs = refs[: len(pairs)], refs[len(pairs) :]
        outs, total = refs[:-1], refs[-1]
        step = pl.program_id(0)
        if tiles == 1:
            for place in range(len(pairs)):
                ahead = starts[place]
                total[:, ahead : ahead + pairs[place][1].shape[1]] = matmul(
                    left_refs[which[place]][...], right_refs[place][...]
                )
        elif len(pairs) == 1:
            total[...] = matmul(left_refs[0][...], right_refs[0][...])
        else:
            for place in range(len(pairs)):
                low = starts[place] // tile
                high = low + pairs[place][1].shape[1] // tile

                @pl.when((step >= low) & (step < high))
                def _():
                    total[...] = matmul(left_refs[which[place]][...], right_refs[place][...])

        index = lax.axis_index("dp")

        def block(place):
            return lower(total[pl.ds(pl.multiple_of(place * rows, 8), rows), :])

        if form == "line":
            here = (index >> 2) & 1
            for place in range(half):
                for plane in range(4):
                    outs[0][place, plane] = block((2 * place + 1 - here) * 4 + plane)
                    outs[1][place, plane] = block((2 * place + here) * 4 + plane)
            return

        for number, first, count, away, own in (
            [(form, 0, line, *outs)]
            if form in (0, 1)
            else [(1, 0, half, outs[0], outs[2]), (0, half, half, outs[1], outs[3])]
        ):
            here = (index >> number) & 1
            for place in range(count):
                for side in range(2):
                    base = (first + place) * 4 + side * (3 - (1 << number))
                    away[place, side] = block(base + ((1 - here) << number))
                    own[place, side] = block(base + (here << number))

    def right_spec(place):
        columns = pairs[place][1].shape[1]
        if tiles == 1:
            return pl.BlockSpec((length, columns), lambda step: (0, 0))
        low, count = starts[place] // tile, columns // tile
        return pl.BlockSpec((length, tile), lambda step: (0, jnp.clip(step - low, 0, count - 1)))

    half = line // 2
    cut, parts = {"line": ((half, 4), 2), "halves": ((half, 2), 4)}.get(form, ((line, 2), 2))
    out = jax.ShapeDtypeStruct((*cut, rows, width), jnp.bfloat16)
    out_spec = pl.BlockSpec((*cut, rows, tile), lambda step: (0, 0, 0, step))
    size = depth * width * 2 + sum(l.size * 2 for l in lefts) + sum(r.size * 2 for _, r in pairs)
    return pl.pallas_call(
        body,
        grid=(tiles,),
        in_specs=[pl.BlockSpec((depth, length), lambda step: (0, 0))] * len(lefts)
        + [right_spec(place) for place in range(len(pairs))],
        out_specs=[out_spec] * parts,
        out_shape=[out] * parts,
        scratch_shapes=[pltpu.VMEM((depth, tile), jnp.float32)],
        cost_estimate=small_cost(2 * depth * length * width, size),
        compiler_params=pltpu.CompilerParams(vmem_limit_bytes=VMEM_LIMIT),
    )(*lefts, *[right for _, right in pairs])


def pick(array, axis, place):
    return lax.dynamic_index_in_dim(array, place, axis, keepdims=False)


def cut_parts(grid, array, form):
    line, rows = grid.count // 4, array.shape[0] // grid.count
    blocks = array.reshape(line, 2, 2, rows, array.shape[1])

    def cut(blocks, number):
        here, axis = grid.bit(number), 2 - number
        return pick(blocks, axis, 1 - here), pick(blocks, axis, here)

    if form in (0, 1):
        return cut(blocks, form)
    if form == "line":
        here, whole = grid.bit(2), array.reshape(line // 2, 2, 4, rows, array.shape[1])
        return pick(whole, 1, 1 - here), pick(whole, 1, here)
    low, high = cut(blocks[: line // 2], 1), cut(blocks[line // 2 :], 0)
    return low[0], high[0], low[1], high[1]


def weight_gradient(grid, pairs, tiles, form):
    rows = pairs[0][0].shape[0] // grid.count
    if rows % 16 == 0:
        parts = gradient_parts(grid, pairs, tiles, form)
    else:
        found = [lower(matmul(left, right)) for left, right in pairs]
        parts = cut_parts(grid, jnp.concatenate(found, axis=1), form)
    return BitSum(grid, parts) if form == "line" else PlaneSum(grid, parts, form)


def add_halves(terms, number):
    count, _, rows, columns = terms[0].shape
    tile = next(t for t in (512, 384, 256, 128, columns) if columns % t == 0)

    def body(*refs):
        inputs, (away, kept) = refs[: len(terms)], refs[len(terms) :]
        side = (lax.axis_index("dp") >> number) & 1
        for place in range(count):
            away[place] = lower(sum(wide(ref[place, 1 - side]) for ref in inputs))
            kept[place] = lower(sum(wide(ref[place, side]) for ref in inputs))

    block = pl.BlockSpec((count, 2, rows, tile), lambda step: (0, 0, 0, step))
    half = pl.BlockSpec((count, rows, tile), lambda step: (0, 0, step))
    size = terms[0].size * (2 * len(terms) + 2)
    return pl.pallas_call(
        body,
        grid=(columns // tile,),
        in_specs=[block] * len(terms),
        out_specs=[half] * 2,
        out_shape=[jax.ShapeDtypeStruct((count, rows, columns), jnp.bfloat16)] * 2,
        cost_estimate=small_cost(0, size),
        compiler_params=pltpu.CompilerParams(vmem_limit_bytes=VMEM_LIMIT),
    )(*terms)


def add_joined(packs, number):
    rows = packs[0][0][0].shape[2]
    widths = [pack[0][0].shape[3] for pack in packs]
    count = sum(group[0].shape[0] for group in packs[0])
    flat = [term for pack in packs for group in pack for term in group]

    def body(*refs):
        inputs, (away, kept) = list(refs[: len(flat)]), refs[len(flat) :]
        side = (lax.axis_index("dp") >> number) & 1
        start = 0
        for pack, width in zip(packs, widths):
            place = 0
            for group in pack:
                terms = [inputs.pop(0) for _ in group]
                for row in range(group[0].shape[0]):
                    other = sum(wide(term[row, 1 - side]) for term in terms)
                    own = sum(wide(term[row, side]) for term in terms)
                    away[place, :, start : start + width] = lower(other)
                    kept[place, :, start : start + width] = lower(own)
                    place += 1
            start += width

    out = jax.ShapeDtypeStruct((count, rows, sum(widths)), jnp.bfloat16)
    return pl.pallas_call(
        body,
        out_shape=[out] * 2,
        cost_estimate=small_cost(0, 2 * sum(term.size for term in flat)),
        compiler_params=pltpu.CompilerParams(vmem_limit_bytes=VMEM_LIMIT),
    )(*flat)


def joined_rows(own, others, in_sequence):
    rows, columns = own.shape
    tile, run = columns // 4, 4 // len(others)

    def body(own_ref, *refs):
        other_refs, (rows_ref, turned_ref) = refs[: len(others)], refs[len(others) :]
        first, second = own_ref[...], other_refs[0][...]
        for number in range(1, len(others)):
            later = pl.program_id(0) >= number * run
            second = jnp.where(later, other_refs[number][...], second)
        if in_sequence:
            ahead = lax.axis_index("tensor") == 0
            first, second = jnp.where(ahead, first, second), jnp.where(ahead, second, first)
        rows_ref[:rows] = first
        rows_ref[rows:] = second
        turned_ref[:, :rows] = first.T
        turned_ref[:, rows:] = second.T

    def part_spec(number):
        return pl.BlockSpec(
            (rows, tile), lambda step: (0, jnp.clip(step - number * run, 0, run - 1))
        )

    return pl.pallas_call(
        body,
        grid=(4,),
        in_specs=[pl.BlockSpec((rows, tile), lambda step: (0, step))]
        + [part_spec(number) for number in range(len(others))],
        out_specs=[
            pl.BlockSpec((2 * rows, tile), lambda step: (0, step)),
            pl.BlockSpec((tile, 2 * rows), lambda step: (step, 0)),
        ],
        out_shape=[
            jax.ShapeDtypeStruct((2 * rows, columns), own.dtype),
            jax.ShapeDtypeStruct((columns, 2 * rows), own.dtype),
        ],
        cost_estimate=small_cost(0, 12 * rows * columns),
        compiler_params=pltpu.CompilerParams(vmem_limit_bytes=VMEM_LIMIT),
    )(own, *others)


def row_kernel(body, inputs, outs, sums=0):
    length, columns = inputs[0].shape
    tile = length // 4

    def spec(rows, width):
        if rows == 1:
            return pl.BlockSpec((1, width), lambda step: (0, 0))
        return pl.BlockSpec((tile, width), lambda step: (step, 0))

    def kernel(*refs):
        found = body(*[ref[...] for ref in refs[: len(inputs)]])
        out_refs = refs[len(inputs) :]
        for ref, value in zip(out_refs[: len(outs)], found):
            ref[...] = value
        for ref, value in zip(out_refs[len(outs) :], found[len(outs) :]):

            @pl.when(pl.program_id(0) == 0)
            def _():
                ref[...] = jnp.zeros_like(ref)

            ref[...] += value

    size = length * columns * (sum(i.dtype.itemsize for i in inputs) + 4 * len(outs))
    return pl.pallas_call(
        kernel,
        grid=(4,),
        in_specs=[spec(*i.shape) for i in inputs],
        out_specs=[spec(length, width) for width, _ in outs] + [spec(1, columns)] * sums,
        out_shape=[jax.ShapeDtypeStruct((length, width), kind) for width, kind in outs]
        + [jax.ShapeDtypeStruct((1, columns), jnp.float32)] * sums,
        cost_estimate=small_cost(0, size),
        compiler_params=pltpu.CompilerParams(vmem_limit_bytes=VMEM_LIMIT),
    )(*inputs)


def halves(values):
    half = values.shape[1] // 2
    return values, values[:, :half], values[:, half:]


def both_parts(first, second):
    return wide(jnp.concatenate([first, second], axis=1))


def norm_forward(residual, own, first, second, gain):
    middle = wide(residual) + (own + both_parts(first, second))
    unit, _ = statistics(middle)
    return middle, *halves(lower(unit * gain))


def norm_gradient(source, own, first, second, base, gain):
    unit, inverse = statistics(wide(source))
    grad = own + both_parts(first, second)
    total = wide(base) + norm_backward(unit, inverse, gain, grad)
    return total, lower(total), jnp.sum(grad * unit, axis=0, keepdims=True)


def norm_gradient_halves(*values):
    total, rounded, summed = norm_gradient(*values)
    return total, *halves(rounded), summed


class PlaneSum:
    def __init__(self, grid, parts, form):
        half = len(parts) // 2
        self.grid, self.sent, self.own = grid, tuple(parts[:half]), tuple(parts[half:])
        self.numbers = (form,) if form in (0, 1) else (1, 0)

    def start(self, *after):
        swaps = zip(self.sent, self.numbers)
        self.got = [self.grid.swap(tie(sent, *after), number) for sent, number in swaps]
        return self

    def second(self, *after):
        sent, self.groups = [], []
        for own, got, number in zip(self.own, self.got, self.numbers):
            away, kept = add_halves([own, tie(got, *after)], 1 - number)
            sent.append(away)
            self.groups.append([kept, self.grid.swap(away, 1 - number)])
        self.sent = tuple(sent)
        return self


class BitSum:
    def __init__(self, grid, parts):
        self.grid, self.sent, self.kept = grid, *parts

    def start(self, *after):
        self.got = self.grid.swap(tie(self.sent, *after), 2)
        return self

    def step(self, number, *after):
        def cut(array):
            rows, columns = array.shape[-2:]
            count = array.size // (rows * columns)
            if number >= 2:
                count, rows = count // 4, rows * 4
            else:
                count = 1
                rows = array.size // (2 * columns)
            return array.reshape(count if number < 2 else count // 2, 2, rows, columns)

        self.sent, self.kept = add_halves([cut(self.kept), cut(tie(self.got, *after))], number)
        self.got = self.grid.swap(self.sent, number)
        if number >= 2:
            shape = (self.sent.shape[0], 4, self.sent.shape[1] // 4, self.sent.shape[2])
            self.kept, self.got = self.kept.reshape(shape), self.got.reshape(shape)
        return self

    def line(self, *after):
        for number in self.grid.line_bits[1:]:
            self.step(number, *after)
        return self

    def result(self):
        return wide(self.kept[0]) + wide(self.got[0])


class LineSum:
    def __init__(self, grid, sums):
        self.grid, self.packs = grid, [found.groups for found in sums]

    def step(self, number, after):
        packs = [
            [
                [t.reshape((t.shape[0] // 2, 2) + t.shape[1:]) for t in (*kept, tie(got, *after))]
                for *kept, got in groups
            ]
            for groups in self.packs
        ]
        self.sent, kept = add_joined(packs, number)
        self.packs = [[[kept, self.grid.swap(self.sent, number)]]]
        return self

    def third(self, *after):
        return self.step(self.grid.line_bits[0], after)

    def fourth(self, *after):
        for number in self.grid.line_bits[1:]:
            self.step(number, after)
        return self

    def result(self):
        return sum(wide(term[0]) for term in self.packs[0][0])


class SmallSum:
    def __init__(self, grid, array):
        rows = array.shape[0] // grid.count
        self.grid, self.terms = grid, [array.reshape(grid.count, rows, array.shape[1])]

    def step(self, number, *after):
        terms = [tie(t, *after).reshape((t.shape[0] // 2, 2) + t.shape[1:]) for t in self.terms]
        side = self.grid.bit(number)
        self.sent = sum(pick(t, 1, 1 - side) for t in terms)
        kept = sum(pick(t, 1, side) for t in terms)
        self.terms = [kept, self.grid.swap(self.sent, number)]
        return self

    def result(self):
        return sum(term[0] for term in self.terms)


def running_sum(values, reverse):
    length = values.shape[1]
    place = lax.broadcasted_iota(jnp.int32, values.shape, 1)
    shift = 1
    while shift < length:
        if reverse:
            moved = jnp.where(place < length - shift, pltpu.roll(values, length - shift, 1), 0.0)
        else:
            moved = jnp.where(place >= shift, pltpu.roll(values, shift, 1), 0.0)
        values = values + moved
        shift *= 2
    return values


def decay_kernel(heads, logit_ref, bias_ref, row_ref, column_ref):
    length, lanes = logit_ref.shape
    groups, per, _ = row_ref.shape
    padded = -(-heads // 8) * 8
    logit = (logit_ref[...] + bias_ref[...]).T[:padded]
    decay = running_sum(-jnp.log1p(jnp.exp(-logit)), False)
    columns = jnp.concatenate([decay, jnp.zeros((lanes - padded, length), jnp.float32)], axis=0).T
    for group in range(groups):
        row_ref[group] = decay[group * per : (group + 1) * per]
        column_ref[group] = columns[:, group * per : (group + 1) * per]


def decays(logit, bias, heads, per):
    length = logit.shape[0]
    groups = heads // per
    return pl.pallas_call(
        functools.partial(decay_kernel, heads),
        out_shape=[
            jax.ShapeDtypeStruct((groups, per, length), jnp.float32),
            jax.ShapeDtypeStruct((groups, length, per), jnp.float32),
        ],
        compiler_params=pltpu.CompilerParams(vmem_limit_bytes=VMEM_LIMIT),
    )(logit, bias)


def forget_kernel(heads, row_ref, column_ref, logit_ref, bias_ref, grad_ref, sum_ref):
    length, lanes = logit_ref.shape
    groups, per, _ = row_ref.shape
    padded = -(-heads // 8) * 8
    rows = [row_ref[group] for group in range(groups)]
    columns = [column_ref[group] for group in range(groups)]
    columns = jnp.concatenate(
        columns + [jnp.zeros((length, lanes - heads), jnp.float32)], axis=1
    ).T[:padded]
    if padded > heads:
        rows = rows + [jnp.zeros((padded - heads, length), jnp.float32)]
    grad_log = running_sum(jnp.concatenate(rows, axis=0) - columns, True)
    grad_log = jnp.concatenate([grad_log, jnp.zeros((lanes - padded, length), jnp.float32)], axis=0).T
    grad = lower(grad_log * jax.nn.sigmoid(-(logit_ref[...] + bias_ref[...])))
    lane = lax.broadcasted_iota(jnp.int32, grad.shape, 1)
    grad = jnp.where(lane < heads, grad, jnp.bfloat16(0))
    grad_ref[...] = grad
    sum_ref[...] = jnp.sum(wide(grad), axis=0, keepdims=True)


def forget_backward(row, column, logit, bias, heads):
    return pl.pallas_call(
        functools.partial(forget_kernel, heads),
        out_shape=[
            jax.ShapeDtypeStruct(logit.shape, jnp.bfloat16),
            jax.ShapeDtypeStruct(bias.shape, jnp.float32),
        ],
        compiler_params=pltpu.CompilerParams(vmem_limit_bytes=VMEM_LIMIT),
    )(row, column, logit, bias)


def fwd_kernel(scale, head, q_ref, k_ref, v_ref, col_ref, row_ref, o_ref, lse_ref, out_t):
    length, lanes = q_ref.shape
    span = min(256, length)
    lane = lax.broadcasted_iota(jnp.int32, (span, lanes), 1) // head
    below = lax.broadcasted_iota(jnp.int32, (span, span), 0) <= lax.broadcasted_iota(jnp.int32, (span, span), 1)
    v_t = v_ref[...].T
    for h in range(lanes // head):
        for b in range(length // span):
            lo, hi = b * span, (b + 1) * span
            q = jnp.where(lane == h, q_ref[lo:hi, :] * scale, 0).astype(jnp.bfloat16)
            row = row_ref[0, h:h+1, lo:hi]
            diag = second_contract(k_ref[lo:hi, :], q) + row - col_ref[0, lo:hi, h:h+1]
            diag = jnp.where(below, diag, -1e30)
            top = jnp.max(diag, axis=0, keepdims=True)
            if lo:
                off = second_contract(k_ref[:lo, :], q) + row - col_ref[0, :lo, h:h+1]
                top = jnp.maximum(top, jnp.max(off, axis=0, keepdims=True))
            e = jnp.exp(diag - top)
            total = jnp.sum(e, axis=0, keepdims=True)
            v_h = v_t[h*head:(h+1)*head]
            acc = matmul(v_h[:, lo:hi], lower(e))
            if lo:
                e = jnp.exp(off - top)
                total = total + jnp.sum(e, axis=0, keepdims=True)
                acc = acc + matmul(v_h[:, :lo], lower(e))
            out_t[h*head:(h+1)*head, lo:hi] = acc / total
            lse_ref[0, h:h+1, lo:hi] = top + jnp.log(total)
    o_ref[...] = out_t[...].T

def bwd_kernel(scale, head, q_ref, k_ref, v_ref, do_ref, col_ref, row_ref, lse_ref, dq_ref, dk_ref, dv_ref, drow_ref, dcol_ref, dq_t, dk_acc, dv_acc):
    length, lanes = q_ref.shape
    span = min(256, length)
    heads = lanes // head
    lane = lax.broadcasted_iota(jnp.int32, (span, lanes), 1) // head
    sub = lax.broadcasted_iota(jnp.int32, (lanes, length), 0) // head
    below = lax.broadcasted_iota(jnp.int32, (span, span), 0) <= lax.broadcasted_iota(jnp.int32, (span, span), 1)
    k_t = k_ref[...].T
    one = jnp.bfloat16(1)
    for h in range(heads):
        kt_h = jnp.where(sub == h, k_t, one)
        mine = lane == h
        for b in range(length // span):
            lo, hi = b * span, (b + 1) * span
            q = q_ref[lo:hi, :] * jnp.bfloat16(scale)
            qz = jnp.where(mine, q, jnp.bfloat16(0))
            q1 = jnp.where(mine, q, one)
            do = do_ref[lo:hi, :]
            doz = jnp.where(mine, do, jnp.bfloat16(0))
            row = row_ref[0, h:h+1, lo:hi] - lse_ref[0, h:h+1, lo:hi]
            s = second_contract(k_ref[lo:hi, :], qz) + row - col_ref[0, lo:hi, h:h+1]
            p = jnp.exp(jnp.where(below, s, -1e30))
            dp = second_contract(v_ref[lo:hi, :], doz)
            centre = jnp.sum(p * dp, axis=0, keepdims=True)
            if lo:
                s0 = second_contract(k_ref[:lo, :], qz) + row - col_ref[0, :lo, h:h+1]
                p0 = jnp.exp(s0)
                dp0 = second_contract(v_ref[:lo, :], doz)
                centre = centre + jnp.sum(p0 * dp0, axis=0, keepdims=True)
            ds = lower(p * (dp - centre))
            dqt = matmul(kt_h[:, lo:hi], ds)
            dv_acc[h, lo:hi, :] = matmul(lower(p), do)
            dk_acc[h, lo:hi, :] = matmul(ds, q1)
            if lo:
                ds0 = lower(p0 * (dp0 - centre))
                dqt = dqt + matmul(kt_h[:, :lo], ds0)
                dv_acc[h, :lo, :] = dv_acc[h, :lo, :] + matmul(lower(p0), do)
                dk_acc[h, :lo, :] = dk_acc[h, :lo, :] + matmul(ds0, q1)
            dq_t[h*head:(h+1)*head, lo:hi] = dqt[h*head:(h+1)*head] * scale
            other = ((h + 1) % heads) * head
            drow_ref[0, h:h+1, lo:hi] = dqt[other:other+1]
    lane_all = lax.broadcasted_iota(jnp.int32, (length, lanes), 1) // head
    dk, dv = dk_acc[0], dv_acc[0]
    for h in range(1, heads):
        dk = jnp.where(lane_all == h, dk_acc[h], dk)
        dv = jnp.where(lane_all == h, dv_acc[h], dv)
    for h in range(heads):
        other = ((h + 1) % heads) * head
        dcol_ref[0, :, h:h+1] = dk_acc[h][:, other:other+1]
    dq_ref[...] = lower(dq_t[...].T)
    dk_ref[...] = lower(dk)
    dv_ref[...] = lower(dv)


def pair_specs(length, groups, per):
    def block(offset):
        return pl.BlockSpec((length, LANES), lambda group: (0, group + offset))

    column = pl.BlockSpec((1, length, per), lambda group: (group, 0, 0))
    row = pl.BlockSpec((1, per, length), lambda group: (group, 0, 0))
    return block, column, row


def attention_cost(length, width, head, products):
    return small_cost(products * 6 * length * length * width, 16 * length * width)


def attend(qk, values, column, row, head):
    length, width = values.shape[0], qk.shape[1] // 2
    groups, per, _ = row.shape
    block, column_spec, row_spec = pair_specs(length, groups, per)
    return pl.pallas_call(
        functools.partial(fwd_kernel, head**-0.5, head),
        grid=(groups,),
        in_specs=[block(0), block(groups), block(0), column_spec, row_spec],
        out_specs=[block(0), row_spec],
        out_shape=[
            jax.ShapeDtypeStruct((length, width), jnp.float32),
            jax.ShapeDtypeStruct(row.shape, jnp.float32),
        ],
        scratch_shapes=[pltpu.VMEM((LANES, length), jnp.float32)],
        cost_estimate=attention_cost(length, width, head, 2),
        compiler_params=pltpu.CompilerParams(vmem_limit_bytes=VMEM_LIMIT),
    )(qk, qk, values, column, row)


def attend_backward(qk, values, grad, column, row, logsum, head):
    length, width = values.shape[0], qk.shape[1] // 2
    groups, per, _ = row.shape
    block, column_spec, row_spec = pair_specs(length, groups, per)
    wide_out = jax.ShapeDtypeStruct((length, width), jnp.bfloat16)
    return pl.pallas_call(
        functools.partial(bwd_kernel, head**-0.5, head),
        grid=(groups,),
        in_specs=[block(0), block(groups), block(0), block(0), column_spec, row_spec, row_spec],
        out_specs=[block(0), block(0), block(0), row_spec, column_spec],
        out_shape=[
            wide_out,
            wide_out,
            wide_out,
            jax.ShapeDtypeStruct(row.shape, jnp.float32),
            jax.ShapeDtypeStruct(column.shape, jnp.float32),
        ],
        scratch_shapes=[
            pltpu.VMEM((LANES, length), jnp.float32),
            pltpu.VMEM((per, length, LANES), jnp.float32),
            pltpu.VMEM((per, length, LANES), jnp.float32),
        ],
        cost_estimate=attention_cost(length, width, head, 5),
        compiler_params=pltpu.CompilerParams(vmem_limit_bytes=VMEM_LIMIT),
    )(qk, qk, values, grad, column, row, logsum)


def per_device(
    tokens,
    w_query,
    w_key,
    w_value,
    w_gate_attn,
    w_forget,
    forget_bias,
    w_out,
    norm_attn,
    norm_mlp,
    w_gate,
    w_up,
    w_down,
    cotangent,
):
    grid = Grid()
    side = lax.axis_index("tensor")
    heads_here = forget_bias.shape[0]
    width = w_query.shape[1]
    head_size = width // heads_here
    hidden_here = w_gate.shape[1]
    scale = head_size ** (-0.5)
    rows_here = tokens.shape[0]

    load_qk = Gather(grid, jnp.concatenate([lower(w_query), lower(w_key)], axis=1))
    own_gains = jnp.stack([norm_attn, norm_mlp])
    other_gains = partner(own_gains)
    gains = jnp.where(
        side == 0,
        jnp.concatenate([own_gains, other_gains], axis=1),
        jnp.concatenate([other_gains, own_gains], axis=1),
    )[None]
    gain_codes = [0]
    for number in range(len(grid.line_bits) + 2):
        gains = jnp.concatenate([gains, grid.swap(gains, number)], axis=0)
        gain_codes = gain_codes + [code ^ (1 << number) for code in gain_codes]
        if number == 1:
            load_qk.line_end(gains)
    (all_gains,) = grid.place([(gain_codes, gains)], [gains.shape[2]])
    all_gains = all_gains.reshape(grid.count, 2, all_gains.shape[1])
    gain_attn = all_gains[:, 0].reshape(-1)
    gain_mlp = all_gains[:, 1].reshape(-1)
    load_qk.plane(fine=True)
    other_cotangent = partner(tie(cotangent, gains))

    padding = jnp.zeros((w_forget.shape[0], LANES - heads_here), jnp.bfloat16)
    forget_lanes = jnp.concatenate([lower(w_forget), padding], axis=1)
    load_vf = Gather(
        grid, jnp.concatenate([lower(w_value), forget_lanes], axis=1), load_qk.far, gains
    )
    load_vf.line_end(*load_qk.corner_parts).plane(*load_qk.corners)
    load_go = Gather(
        grid, jnp.concatenate([lower(w_gate_attn), lower(w_out).T], axis=1), load_vf.far
    )
    load_go.line_end(load_vf.block)
    gain_attn, gain_mlp = gain_attn[None], gain_mlp[None]
    low = jnp.bfloat16
    columns = tokens.shape[1]
    rounded_outs = [(columns, low), (columns // 2, low), (columns // 2, low)]

    def exchanged(parts):
        return [partner(part) for part in parts]

    own_attn, *sent = row_kernel(
        lambda rows, gain: halves(lower(statistics(wide(rows))[0] * gain)),
        [tokens, gain_attn],
        rounded_outs,
    )
    normed_attn, normed_attn_t = joined_rows(own_attn, exchanged(sent), True)
    grad_output, grad_output_t = joined_rows(cotangent, [other_cotangent], False)

    load_go.plane(*load_vf.corners, normed_attn)
    load_gate = Gather(grid, lower(w_gate), load_go.far).line_end(load_go.block)
    load_up = Gather(grid, lower(w_up), load_gate.far, load_go.corners[0])
    value_w, forget_w = load_vf.weight.part(0, width), load_vf.weight.part(width, LANES)
    query_w, key_w = load_qk.weight.part(0, width), load_qk.weight.part(width, width)
    gate_w, out_w = load_go.weight.part(0, width), load_go.weight.part(width, width)

    (qk,) = multiply(
        normed_attn, load_qk.weight, 3, lambda p: (lower(p),), [], [(2 * width, low)]
    )
    values_all, forget_logit = multiply(
        normed_attn,
        load_vf.weight,
        1,
        lambda p: (lower(p[:, :width]), p[:, width:]),
        [],
        [(width, low), (LANES, jnp.float32)],
    )
    bias_lanes = jnp.pad(forget_bias, (0, LANES - heads_here))[None]
    decay_row, decay_column = decays(forget_logit, bias_lanes, heads_here, LANES // head_size)
    load_gate.plane(*load_go.corners, decay_row, qk)
    load_up.line_end(load_gate.block)
    qk = tie(qk, load_gate.block)
    attended, logsum = attend(qk, values_all, decay_column, decay_row, head_size)
    load_up.plane(*load_gate.corners, attended)
    load_down = Gather(grid, lower(w_down).T, load_up.far, load_gate.corners[0])
    load_down.line_end(load_up.block)
    mlp_gate, mlp_up = load_gate.weight, load_up.weight

    def gate_output(product, attended):
        sigmoid = jax.nn.sigmoid(product)
        return sigmoid, lower(attended * sigmoid)

    gate_sig, gated = multiply(
        normed_attn, gate_w, 2, gate_output, [attended], [(width, jnp.float32), (width, low)]
    )
    arrived = exchanged(multiply_back([(gated, out_w)], 1 - side, low, 2))
    (own_part,) = multiply_back([(gated, out_w)], side)
    middle, own_normed, *sent = row_kernel(
        norm_forward,
        [tokens, own_part, *arrived, gain_mlp],
        [(columns, jnp.float32)] + rounded_outs,
    )
    normed_mlp, normed_mlp_t = joined_rows(own_normed, exchanged(sent), False)
    (gate_act,) = multiply(
        normed_mlp, mlp_gate, 4, lambda p: (lower(p),), [], [(hidden_here, low)]
    )

    load_down.plane(*load_up.corners, gate_act)
    mlp_down = load_down.weight

    def hidden_units(up, gate):
        gate = wide(gate)
        return lower(up), lower(gate * jax.nn.sigmoid(gate) * up)

    up_act, hidden = multiply(
        normed_mlp, mlp_up, 4, hidden_units, [gate_act], [(hidden_here, low)] * 2
    )
    sum_down = weight_gradient(grid, [(grad_output_t, hidden)], 4, "line").start()

    def hidden_backward(grad, gate, up):
        gate, up = wide(gate), wide(up)
        sigmoid = jax.nn.sigmoid(gate)
        return (
            lower(grad * (gate * sigmoid)),
            lower(grad * up * sigmoid * (1.0 + gate * (1.0 - sigmoid))),
        )

    grad_up, grad_gate = multiply(
        tie(grad_output, sum_down.sent),
        mlp_down,
        4,
        hidden_backward,
        [gate_act, up_act],
        [(hidden_here, low)] * 2,
    )
    sum_up = weight_gradient(grid, [(normed_mlp_t, grad_up)], 4, 0)
    sum_up.start()
    grad_gate = tie(grad_gate, *sum_up.sent)
    sum_gate = weight_gradient(grid, [(normed_mlp_t, grad_gate)], 4, 1).start()
    grad_gate = tie(grad_gate, *sum_gate.sent)
    back = [(grad_gate, mlp_gate), (grad_up, mlp_up)]
    arrived = exchanged(multiply_back(back, jnp.int32(1), low, 2))
    (own_part,) = multiply_back(back, jnp.int32(0))
    sum_down.line(own_part)
    own_part = tie(own_part, sum_down.sent)
    grad_middle, own_branch, *sent, gain_mlp_part = row_kernel(
        norm_gradient_halves,
        [middle, own_part, *arrived, cotangent, gain_mlp],
        [(columns, jnp.float32)] + rounded_outs,
        sums=1,
    )
    other_branch = exchanged(sent)
    grad_branch, grad_branch_t = joined_rows(own_branch, other_branch, True)

    def gate_backward(grad, sigmoid, attended):
        return lower(grad * sigmoid), lower(grad * attended * sigmoid * (1.0 - sigmoid))

    grad_attended, grad_gate_logit = multiply(
        grad_branch,
        out_w,
        2,
        gate_backward,
        [gate_sig, attended],
        [(width, low)] * 2,
    )
    sum_up.second(grad_attended)
    sum_gate.second(grad_attended)
    grad_gate_logit = tie(grad_gate_logit, *sum_up.sent, *sum_gate.sent)
    sum_go = weight_gradient(
        grid, [(normed_attn_t, grad_gate_logit), (grad_branch_t, gated)], 4, "halves"
    ).start()
    grad_attended = tie(grad_attended, *sum_go.sent)
    grad_queries, grad_keys, grad_values, row_total, column_total = attend_backward(
        qk, values_all, grad_attended, decay_column, decay_row, logsum, head_size
    )
    line_mlp = LineSum(grid, [sum_gate, sum_up]).third(grad_queries)
    sum_down.step(1, grad_queries)
    grad_queries = tie(grad_queries, line_mlp.sent, sum_down.sent)
    sum_qk = weight_gradient(
        grid, [(normed_attn_t, grad_queries), (normed_attn_t, grad_keys)], 4, "halves"
    )
    sum_qk.start()
    sum_go.second(*sum_qk.sent)
    grad_forget, bias_part = forget_backward(
        row_total, column_total, forget_logit, bias_lanes, heads_here
    )
    grad_values = tie(grad_values, *sum_qk.sent, *sum_go.sent)
    sum_vf = weight_gradient(
        grid, [(normed_attn_t, grad_values), (normed_attn_t, grad_forget)], 1, "halves"
    )
    sum_down.step(0, *sum_vf.sent)
    hidden = tie(hidden, sum_down.sent)
    other_down = multiply_back([(hidden, mlp_down)], jnp.int32(1), low, 2)
    arrived_down = exchanged(other_down)
    back = [
        (tie(grad_gate_logit, *other_down), gate_w),
        (grad_queries, query_w),
        (grad_keys, key_w),
        (grad_values, value_w),
        (grad_forget, forget_w),
    ]
    other_part = multiply_back(back, 1 - side, low, 2)
    arrived = exchanged(other_part)
    sum_qk.second(*other_part)
    line_mlp.fourth(*other_part)
    back[1] = (tie(grad_queries, line_mlp.sent, *sum_qk.sent), query_w)
    (own_part,) = multiply_back(back, side)
    (own_down,) = multiply_back([(tie(hidden, own_part), mlp_down)], jnp.int32(0))
    (mixed,) = row_kernel(
        lambda middle, own, *parts: (lower(middle + (own + both_parts(*parts))),),
        [middle, own_down, *arrived_down],
        [(columns, low)],
    )
    line_go = LineSum(grid, [sum_go]).third(own_part)
    sum_vf.start(own_part, line_go.sent)
    _, tokens_grad, gain_attn_part = row_kernel(
        norm_gradient,
        [tokens, own_part, *arrived, grad_middle, gain_attn],
        [(columns, jnp.float32), (columns, low)],
        sums=1,
    )
    small = jnp.concatenate(
        [
            gain_attn_part.reshape(grid.count, -1),
            gain_mlp_part.reshape(grid.count, -1),
            jnp.broadcast_to(bias_part[:, :heads_here], (grid.count, heads_here)),
        ],
        axis=1,
    )
    sum_vf.second(gain_attn_part)
    line_qkv = LineSum(grid, [sum_qk, sum_vf]).third(gain_attn_part)
    line_go.fourth(line_qkv.sent)
    sum_small = SmallSum(grid, small).step(0, line_qkv.sent).step(1)
    line_qkv.fourth(sum_small.sent)
    for number in grid.line_bits:
        sum_small.step(number, line_qkv.sent)
    down_grad, go_grad, qkv_grad = sum_down.result().T, line_go.result(), line_qkv.result()
    mlp_grad = line_mlp.result()
    small_sum = sum_small.result().reshape(-1)
    share = norm_attn.shape[0]
    gain_sums = small_sum[: 4 * share].reshape(2, 2, share)
    other_sums = lax.dynamic_index_in_dim(gain_sums, 1 - side, 1, keepdims=False)
    own_sums = lax.dynamic_index_in_dim(gain_sums, side, 1, keepdims=False)
    gain_grads = own_sums + partner(other_sums)
    return (
        mixed,
        tokens_grad,
        qkv_grad[:, :width],
        qkv_grad[:, width : 2 * width],
        qkv_grad[:, 2 * width : 3 * width],
        go_grad[:, :width],
        qkv_grad[:, 3 * width : 3 * width + heads_here],
        small_sum[4 * share :],
        go_grad[:, width:].T,
        gain_grads[0],
        gain_grads[1],
        mlp_grad[:, :hidden_here],
        mlp_grad[:, hidden_here:],
        down_grad,
    )


def solution(mesh):
    return jax.shard_map(
        per_device,
        mesh=mesh,
        in_specs=(
            P(("dp", "tensor"), None),
            P("dp", "tensor"),
            P("dp", "tensor"),
            P("dp", "tensor"),
            P("dp", "tensor"),
            P("dp", "tensor"),
            P("tensor"),
            P("tensor", "dp"),
            P(("dp", "tensor")),
            P(("dp", "tensor")),
            P("dp", "tensor"),
            P("dp", "tensor"),
            P("tensor", "dp"),
            P(("dp", "tensor"), None),
        ),
        out_specs=(
            P(("dp", "tensor"), None),
            P(("dp", "tensor"), None),
            P("dp", "tensor"),
            P("dp", "tensor"),
            P("dp", "tensor"),
            P("dp", "tensor"),
            P("dp", "tensor"),
            P("tensor"),
            P("tensor", "dp"),
            P(("dp", "tensor")),
            P(("dp", "tensor")),
            P("dp", "tensor"),
            P("dp", "tensor"),
            P("tensor", "dp"),
        ),
        check_vma=False,
    )
```

```python
import functools

import jax
import jax.numpy as jnp
from jax import lax
from jax.experimental import pallas as pl
from jax.experimental.pallas import tpu as pltpu
from jax.sharding import PartitionSpec as P

EPSILON = 1e-06
LANES = 128
VMEM_LIMIT = 50 * 2**20
COST_SCALE = 0.02


def lower(values):
    return values.astype(jnp.bfloat16)


def wide(values):
    return values.astype(jnp.float32)


def matmul(left, right):
    return jnp.dot(left, right, preferred_element_type=jnp.float32)


def first_contract(left, right):
    return lax.dot_general(
        left, right, (((0,), (0,)), ((), ())), preferred_element_type=jnp.float32
    )


def second_contract(left, right):
    return lax.dot_general(
        left, right, (((1,), (1,)), ((), ())), preferred_element_type=jnp.float32
    )


def statistics(values):
    inverse = lax.rsqrt(jnp.mean(values * values, axis=-1, keepdims=True) + EPSILON)
    return (values * inverse, inverse)


def norm_backward(unit, inverse, gain, grad):
    scaled = gain * grad
    return inverse * (scaled - unit * jnp.mean(scaled * unit, axis=-1, keepdims=True))


def partner(values):
    return lax.ppermute(values, "tensor", [(0, 1), (1, 0)])


def tie(value, *others):
    if not others:
        return value
    return lax.optimization_barrier((value, *others))[0]


def small_cost(flops, size):
    return pl.CostEstimate(
        flops=int(COST_SCALE * flops), bytes_accessed=int(COST_SCALE * size), transcendentals=0
    )


class Grid:
    def __init__(self):
        self.count = lax.axis_size("dp")
        self.index = lax.axis_index("dp")
        bits = self.count.bit_length() - 1
        self.line_bits = list(range(2, bits))

    def bit(self, number):
        return (self.index >> number) & 1

    def swap(self, values, number):
        pairs = [(i, i ^ (1 << number)) for i in range(self.count)]
        return lax.ppermute(values, "dp", pairs)

    def place(self, pieces, splits):
        rows = pieces[0][1].shape[1]
        arrays = [piece for _, piece in pieces]
        codes = [code for found, _ in pieces for code in found]
        kind = arrays[0].dtype

        def body(*refs):
            inputs, results, sem = refs[: len(arrays)], refs[len(arrays) : -1], refs[-1]
            here = lax.axis_index("dp")
            copies = []
            for (found, _), ref in zip(pieces, inputs):
                for number, code in enumerate(found):
                    start = 0
                    for width, result in zip(splits, results):
                        copies.append(
                            pltpu.make_async_copy(
                                ref.at[number, :, pl.ds(start, width)],
                                result.at[here ^ code],
                                sem.at[len(copies)],
                            )
                        )
                        start += width
            for copy in copies:
                copy.start()
            for copy in copies:
                copy.wait()

        size = self.count * rows * sum(splits) * kind.itemsize
        results = pl.pallas_call(
            body,
            out_shape=[jax.ShapeDtypeStruct((self.count, rows, w), kind) for w in splits],
            in_specs=[pl.BlockSpec(memory_space=pl.ANY)] * len(arrays),
            out_specs=[pl.BlockSpec(memory_space=pltpu.VMEM)] * len(splits),
            scratch_shapes=[pltpu.SemaphoreType.DMA((len(codes) * len(splits),))],
            compiler_params=pltpu.CompilerParams(vmem_limit_bytes=VMEM_LIMIT),
            cost_estimate=small_cost(0, 2 * size),
        )(*arrays)
        return [r.reshape(self.count * rows, w) for r, w in zip(results, splits)]


class Weight:
    def __init__(self, grid, pieces, first=0, width=None):
        self.grid, self.pieces, self.first = grid, pieces, first
        self.rows = pieces[0][1].shape[1]
        self.width = width or pieces[0][1].shape[2]
        self.in_kernel = self.rows % 16 == 0

    def part(self, first, width):
        return Weight(self.grid, self.pieces, self.first + first, width)

    def arrays(self):
        return [piece for _, piece in self.pieces]

    def assembled(self):
        pieces = [
            (codes, piece[:, :, self.first : self.first + self.width])
            for codes, piece in self.pieces
        ]
        return self.grid.place(pieces, [self.width])[0]

    def copies(self, refs, target, sem, tiles):
        here = lax.axis_index("dp")
        tile = self.width // tiles
        found = []
        for step in range(tiles):
            for (codes, _), ref in zip(self.pieces, refs):
                for number, code in enumerate(codes):
                    block = here ^ code
                    source = ref.at[number, :, pl.ds(self.first + step * tile, tile)]
                    found.append(
                        pltpu.make_async_copy(source, target(step, block), sem.at[step, block])
                    )
        return found


def multiply(left, weight, tiles, epilogue, extras, outs):
    if not weight.in_kernel:
        return epilogue(matmul(left, weight.assembled()), *extras)
    grid, rows = weight.grid, weight.rows
    length, depth = left.shape
    tile = weight.width // tiles
    arrays = weight.arrays()

    def body(*refs):
        left_ref, refs = refs[0], refs[1:]
        piece_refs, refs = refs[: len(arrays)], refs[len(arrays) :]
        extra_refs, refs = refs[: len(extras)], refs[len(extras) :]
        out_refs, (held, sem) = refs[: len(outs)], refs[len(outs) :]
        step = pl.program_id(0)

        def target(place, block):
            return held.at[place, pl.ds(pl.multiple_of(block * rows, 16), rows)]

        @pl.when(step == 0)
        def _():
            for copy in weight.copies(piece_refs, target, sem, tiles):
                copy.start()

        for block in range(grid.count):
            there = target(step, block)
            pltpu.make_async_copy(there, there, sem.at[step, block]).wait()
        results = epilogue(matmul(left_ref[...], held[step]), *[ref[...] for ref in extra_refs])
        for ref, result in zip(out_refs, results):
            ref[...] = result

    def column_block(width):
        return pl.BlockSpec((length, width // tiles), lambda step: (0, step))

    size = (
        left.size * 2
        + depth * weight.width * 2
        + sum(e.size * e.dtype.itemsize for e in extras)
        + sum(length * w * jnp.dtype(kind).itemsize for w, kind in outs)
    )
    return pl.pallas_call(
        body,
        grid=(tiles,),
        in_specs=[pl.BlockSpec((length, depth), lambda step: (0, 0))]
        + [pl.BlockSpec(memory_space=pl.ANY)] * len(arrays)
        + [column_block(extra.shape[1]) for extra in extras],
        out_specs=[column_block(width) for width, _ in outs],
        out_shape=[jax.ShapeDtypeStruct((length, width), kind) for width, kind in outs],
        scratch_shapes=[
            pltpu.VMEM((tiles, depth, tile), jnp.bfloat16),
            pltpu.SemaphoreType.DMA((tiles, grid.count)),
        ],
        cost_estimate=small_cost(2 * length * depth * weight.width, size),
        compiler_params=pltpu.CompilerParams(vmem_limit_bytes=VMEM_LIMIT),
    )(left, *arrays, *extras)


def multiply_back(terms, half, kind=jnp.float32, parts=1, tiles=4):
    grid, rows = terms[0][1].grid, terms[0][1].rows
    length = terms[0][0].shape[0] // 2
    if not terms[0][1].in_kernel:
        total = sum(
            second_contract(
                lax.dynamic_slice_in_dim(left, half * length, length, 0), weight.assembled()
            )
            for left, weight in terms
        )
        return jnp.split(total.astype(kind), parts, axis=1)
    depth = grid.count * rows
    tile, share = depth // tiles, grid.count // tiles
    run = tiles // parts

    def part_spec(number):
        return pl.BlockSpec(
            (length, tile), lambda step, which: (0, jnp.clip(step - number * run, 0, run - 1))
        )

    sources, counts = [], []
    for _, weight in terms:
        sources = sources + weight.arrays()
        counts.append(len(weight.pieces))

    def body(half_ref, *refs):
        left_refs, refs = refs[: len(terms)], refs[len(terms) :]
        piece_refs, refs = refs[: len(sources)], refs[len(sources) :]
        out_refs, refs = refs[:parts], refs[parts:]
        held, sems = refs[: len(terms)], refs[len(terms) :]
        step = pl.program_id(0)

        def target(number):
            def found(_, block):
                return held[number].at[pl.ds(pl.multiple_of(block * rows, 16), rows)]

            return found

        @pl.when(step == 0)
        def _():
            first = 0
            for number, (_, weight) in enumerate(terms):
                mine = piece_refs[first : first + counts[number]]
                first += counts[number]
                for copy in weight.copies(mine, target(number), sems[number], 1):
                    copy.start()

        total = None
        for number in range(len(terms)):
            for part in range(share):
                block = step * share + part
                there = target(number)(0, block)
                pltpu.make_async_copy(there, there, sems[number].at[0, block]).wait()
            found = held[number][pl.ds(pl.multiple_of(step * tile, 16), tile), :]
            product = second_contract(left_refs[number][...], found)
            total = product if total is None else total + product
        for number, out_ref in enumerate(out_refs):

            @pl.when(step // run == number)
            def _():
                out_ref[...] = total.astype(kind)

    size = length * depth * 4 + sum(l.size + depth * w.width * 2 for l, w in terms)
    flops = sum(2 * length * depth * w.width for _, w in terms)
    return pl.pallas_call(
        body,
        grid_spec=pltpu.PrefetchScalarGridSpec(
            num_scalar_prefetch=1,
            grid=(tiles,),
            in_specs=[
                pl.BlockSpec((length, left.shape[1]), lambda step, which: (which[0], 0))
                for left, _ in terms
            ]
            + [pl.BlockSpec(memory_space=pl.ANY)] * len(sources),
            out_specs=[part_spec(number) for number in range(parts)],
            scratch_shapes=[pltpu.VMEM((depth, w.width), jnp.bfloat16) for _, w in terms]
            + [pltpu.SemaphoreType.DMA((1, grid.count)) for _ in terms],
        ),
        out_shape=[jax.ShapeDtypeStruct((length, depth // parts), kind)] * parts,
        cost_estimate=small_cost(flops, size),
        compiler_params=pltpu.CompilerParams(vmem_limit_bytes=VMEM_LIMIT),
    )(jnp.reshape(half, (1,)).astype(jnp.int32), *[left for left, _ in terms], *sources)


class Gather:
    def __init__(self, grid, shard, *after):
        near, codes = tie(shard[None], *after), [0]
        for number in reversed(grid.line_bits[1:]):
            found = grid.swap(near, number)
            near = jnp.concatenate([near, found], axis=0)
            codes = codes + self.moved(codes, 1 << number)
        self.grid, self.near, self.codes = grid, near, codes

    def moved(self, found, plane):
        return [code ^ plane for code in found]

    def line_end(self, *after):
        last = self.grid.line_bits[0]
        self.near = tie(self.near, *after)
        self.far = self.grid.swap(self.near, last)
        self.far_codes = self.moved(self.codes, 1 << last)
        return self

    def plane(self, *after, fine=False, to_end=True):
        grid, near, far, codes, far_codes = (
            self.grid,
            self.near,
            self.far,
            self.codes,
            self.far_codes,
        )
        moved, both, half = self.moved, self.codes + self.far_codes, len(self.codes)
        if fine:
            near_x, near_y = grid.swap(near, 0), grid.swap(near, 1)
            far_x, far_y = grid.swap(far, 0), grid.swap(far, 1)
            sides = [
                (codes, near),
                (far_codes, far),
                (moved(codes, 1), near_x),
                (moved(codes, 2), near_y),
                (moved(far_codes, 1), far_x),
                (moved(far_codes, 2), far_y),
            ]
            received = (near_y, far_x)
        else:
            block = tie(jnp.concatenate([near, far], axis=0), *after)
            side_x, side_y = grid.swap(block, 0), grid.swap(block, 1)
            near_x, far_y = side_x[:half], side_y[half:]
            sides = [(both, block), (moved(both, 1), side_x), (moved(both, 2), side_y)]
            received = ()
            self.block = block
        self.corner_parts, self.received, self.sides = (near_x, far_y), received, sides
        return self.plane_end() if to_end else self

    def plane_end(self, *after):
        grid, codes, far_codes = self.grid, self.codes, self.far_codes
        moved, sides = self.moved, self.sides
        near_x, far_y = [tie(part, *after) for part in self.corner_parts]
        near_corner, far_corner = grid.swap(near_x, 1), grid.swap(far_y, 0)
        self.corners = (near_corner, far_corner, *self.received)
        corners = [(moved(codes, 3), near_corner), (moved(far_codes, 3), far_corner)]
        self.weight = Weight(grid, sides + corners)
        return self


def gradient_parts(grid, pairs, tiles, form, extra=None):
    depth, length = pairs[0][0].shape
    rows, line = depth // grid.count, grid.count // 4
    width = sum(right.shape[1] for _, right in pairs)
    lefts = []
    for left, _ in pairs:
        if not any(left is other for other in lefts):
            lefts.append(left)
    which = [[left is other for other in lefts].index(True) for left, _ in pairs]
    tile = width // tiles
    starts, first = [], 0
    for _, right in pairs:
        starts.append(first)
        first += right.shape[1]

    def body(*refs):
        left_refs, refs = refs[: len(lefts)], refs[len(lefts) :]
        right_refs, refs = refs[: len(pairs)], refs[len(pairs) :]
        if extra is not None:
            extra_ref, refs = refs[0], refs[1:]
        outs, total = refs[:-1], refs[-1]
        step = pl.program_id(0)
        if tiles == 1:
            for place in range(len(pairs)):
                ahead = starts[place]
                total[:, ahead : ahead + pairs[place][1].shape[1]] = matmul(
                    left_refs[which[place]][...], right_refs[place][...]
                )
        elif len(pairs) == 1:
            total[...] = matmul(left_refs[0][...], right_refs[0][...])
        else:
            for place in range(len(pairs)):
                low = starts[place] // tile
                high = low + pairs[place][1].shape[1] // tile

                @pl.when((step >= low) & (step < high))
                def _():
                    total[...] = matmul(left_refs[which[place]][...], right_refs[place][...])

        if extra is not None:
            total[:, tile - extra.shape[1] :] += extra_ref[...]
        index = lax.axis_index("dp")

        def block(place):
            return lower(total[pl.ds(pl.multiple_of(place * rows, 8), rows), :])

        if form == "line":
            here = (index >> 2) & 1
            for place in range(half):
                for plane in range(4):
                    outs[0][place, plane] = block((2 * place + 1 - here) * 4 + plane)
                    outs[1][place, plane] = block((2 * place + here) * 4 + plane)
            return

        for number, first, count, away, own in (
            [(form, 0, line, *outs)]
            if form in (0, 1)
            else [(1, 0, half, outs[0], outs[2]), (0, half, half, outs[1], outs[3])]
        ):
            here = (index >> number) & 1
            for place in range(count):
                for side in range(2):
                    base = (first + place) * 4 + side * (3 - (1 << number))
                    away[place, side] = block(base + ((1 - here) << number))
                    own[place, side] = block(base + (here << number))

    def right_spec(place):
        columns = pairs[place][1].shape[1]
        if tiles == 1:
            return pl.BlockSpec((length, columns), lambda step: (0, 0))
        low, count = starts[place] // tile, columns // tile
        return pl.BlockSpec((length, tile), lambda step: (0, jnp.clip(step - low, 0, count - 1)))

    half = line // 2
    cut, parts = {"line": ((half, 4), 2), "halves": ((half, 2), 4)}.get(form, ((line, 2), 2))
    out = jax.ShapeDtypeStruct((*cut, rows, width), jnp.bfloat16)
    out_spec = pl.BlockSpec((*cut, rows, tile), lambda step: (0, 0, 0, step))
    size = depth * width * 2 + sum(l.size * 2 for l in lefts) + sum(r.size * 2 for _, r in pairs)
    return pl.pallas_call(
        body,
        grid=(tiles,),
        in_specs=[pl.BlockSpec((depth, length), lambda step: (0, 0))] * len(lefts)
        + [right_spec(place) for place in range(len(pairs))]
        + ([] if extra is None else [pl.BlockSpec(extra.shape, lambda step: (0, 0))]),
        out_specs=[out_spec] * parts,
        out_shape=[out] * parts,
        scratch_shapes=[pltpu.VMEM((depth, tile), jnp.float32)],
        cost_estimate=small_cost(2 * depth * length * width, size),
        compiler_params=pltpu.CompilerParams(vmem_limit_bytes=VMEM_LIMIT),
    )(*lefts, *[right for _, right in pairs], *([] if extra is None else [extra]))


def pick(array, axis, place):
    return lax.dynamic_index_in_dim(array, place, axis, keepdims=False)


def cut_parts(grid, array, form):
    line, rows = grid.count // 4, array.shape[0] // grid.count
    blocks = array.reshape(line, 2, 2, rows, array.shape[1])

    def cut(blocks, number):
        here, axis = grid.bit(number), 2 - number
        return pick(blocks, axis, 1 - here), pick(blocks, axis, here)

    if form in (0, 1):
        return cut(blocks, form)
    if form == "line":
        here, whole = grid.bit(2), array.reshape(line // 2, 2, 4, rows, array.shape[1])
        return pick(whole, 1, 1 - here), pick(whole, 1, here)
    low, high = cut(blocks[: line // 2], 1), cut(blocks[line // 2 :], 0)
    return low[0], high[0], low[1], high[1]


def weight_gradient(grid, pairs, tiles, form, extra=None):
    rows = pairs[0][0].shape[0] // grid.count
    if rows % 16 == 0:
        parts = gradient_parts(grid, pairs, tiles, form, extra)
    else:
        found = [matmul(left, right) for left, right in pairs]
        if extra is not None:
            found[-1] = found[-1] + extra
        parts = cut_parts(grid, lower(jnp.concatenate(found, axis=1)), form)
    return BitSum(grid, parts) if form == "line" else PlaneSum(grid, parts, form)


def add_halves(terms, number):
    count, _, rows, columns = terms[0].shape
    tile = next(t for t in (512, 384, 256, 128, columns) if columns % t == 0)

    def body(*refs):
        inputs, (away, kept) = refs[: len(terms)], refs[len(terms) :]
        side = (lax.axis_index("dp") >> number) & 1
        for place in range(count):
            away[place] = lower(sum(wide(ref[place, 1 - side]) for ref in inputs))
            kept[place] = lower(sum(wide(ref[place, side]) for ref in inputs))

    block = pl.BlockSpec((count, 2, rows, tile), lambda step: (0, 0, 0, step))
    half = pl.BlockSpec((count, rows, tile), lambda step: (0, 0, step))
    size = terms[0].size * (2 * len(terms) + 2)
    return pl.pallas_call(
        body,
        grid=(columns // tile,),
        in_specs=[block] * len(terms),
        out_specs=[half] * 2,
        out_shape=[jax.ShapeDtypeStruct((count, rows, columns), jnp.bfloat16)] * 2,
        cost_estimate=small_cost(0, size),
        compiler_params=pltpu.CompilerParams(vmem_limit_bytes=VMEM_LIMIT),
    )(*terms)


def add_joined(packs, number):
    rows = packs[0][0][0].shape[2]
    widths = [pack[0][0].shape[3] for pack in packs]
    count = sum(group[0].shape[0] for group in packs[0])
    flat = [term for pack in packs for group in pack for term in group]

    def body(*refs):
        inputs, (away, kept) = list(refs[: len(flat)]), refs[len(flat) :]
        side = (lax.axis_index("dp") >> number) & 1
        start = 0
        for pack, width in zip(packs, widths):
            place = 0
            for group in pack:
                terms = [inputs.pop(0) for _ in group]
                for row in range(group[0].shape[0]):
                    other = sum(wide(term[row, 1 - side]) for term in terms)
                    own = sum(wide(term[row, side]) for term in terms)
                    away[place, :, start : start + width] = lower(other)
                    kept[place, :, start : start + width] = lower(own)
                    place += 1
            start += width

    out = jax.ShapeDtypeStruct((count, rows, sum(widths)), jnp.bfloat16)
    return pl.pallas_call(
        body,
        out_shape=[out] * 2,
        cost_estimate=small_cost(0, 2 * sum(term.size for term in flat)),
        compiler_params=pltpu.CompilerParams(vmem_limit_bytes=VMEM_LIMIT),
    )(*flat)


def joined_rows(own, others, in_sequence):
    rows, columns = own.shape
    tile, run = columns // 4, 4 // len(others)

    def body(own_ref, *refs):
        other_refs, (rows_ref, turned_ref) = refs[: len(others)], refs[len(others) :]
        first, second = own_ref[...], other_refs[0][...]
        for number in range(1, len(others)):
            later = pl.program_id(0) >= number * run
            second = jnp.where(later, other_refs[number][...], second)
        if in_sequence:
            ahead = lax.axis_index("tensor") == 0
            first, second = jnp.where(ahead, first, second), jnp.where(ahead, second, first)
        rows_ref[:rows] = first
        rows_ref[rows:] = second
        turned_ref[:, :rows] = first.T
        turned_ref[:, rows:] = second.T

    def part_spec(number):
        return pl.BlockSpec(
            (rows, tile), lambda step: (0, jnp.clip(step - number * run, 0, run - 1))
        )

    return pl.pallas_call(
        body,
        grid=(4,),
        in_specs=[pl.BlockSpec((rows, tile), lambda step: (0, step))]
        + [part_spec(number) for number in range(len(others))],
        out_specs=[
            pl.BlockSpec((2 * rows, tile), lambda step: (0, step)),
            pl.BlockSpec((tile, 2 * rows), lambda step: (step, 0)),
        ],
        out_shape=[
            jax.ShapeDtypeStruct((2 * rows, columns), own.dtype),
            jax.ShapeDtypeStruct((columns, 2 * rows), own.dtype),
        ],
        cost_estimate=small_cost(0, 12 * rows * columns),
        compiler_params=pltpu.CompilerParams(vmem_limit_bytes=VMEM_LIMIT),
    )(own, *others)


def row_kernel(body, inputs, outs, sums=0):
    length, columns = inputs[0].shape
    tile = length // 4

    def spec(rows, width):
        if rows == 1:
            return pl.BlockSpec((1, width), lambda step: (0, 0))
        return pl.BlockSpec((tile, width), lambda step: (step, 0))

    def kernel(*refs):
        found = body(*[ref[...] for ref in refs[: len(inputs)]])
        out_refs = refs[len(inputs) :]
        for ref, value in zip(out_refs[: len(outs)], found):
            ref[...] = value
        for ref, value in zip(out_refs[len(outs) :], found[len(outs) :]):

            @pl.when(pl.program_id(0) == 0)
            def _():
                ref[...] = jnp.zeros_like(ref)

            ref[...] += value

    size = length * columns * (sum(i.dtype.itemsize for i in inputs) + 4 * len(outs))
    return pl.pallas_call(
        kernel,
        grid=(4,),
        in_specs=[spec(*i.shape) for i in inputs],
        out_specs=[spec(length, width) for width, _ in outs] + [spec(1, columns)] * sums,
        out_shape=[jax.ShapeDtypeStruct((length, width), kind) for width, kind in outs]
        + [jax.ShapeDtypeStruct((1, columns), jnp.float32)] * sums,
        cost_estimate=small_cost(0, size),
        compiler_params=pltpu.CompilerParams(vmem_limit_bytes=VMEM_LIMIT),
    )(*inputs)


def halves(values):
    half = values.shape[1] // 2
    return values, values[:, :half], values[:, half:]


def both_parts(first, second):
    return wide(jnp.concatenate([first, second], axis=1))


def norm_forward(residual, own, first, second, gain):
    middle = wide(residual) + (own + both_parts(first, second))
    unit, _ = statistics(middle)
    return middle, *halves(lower(unit * gain))


def norm_gradient(source, own, first, second, base, gain):
    unit, inverse = statistics(wide(source))
    grad = own + both_parts(first, second)
    total = wide(base) + norm_backward(unit, inverse, gain, grad)
    return total, lower(total)


def norm_gradient_halves(*values):
    total, rounded = norm_gradient(*values)
    return total, *halves(rounded)


class PlaneSum:
    def __init__(self, grid, parts, form):
        half = len(parts) // 2
        self.grid, self.sent, self.own = grid, tuple(parts[:half]), tuple(parts[half:])
        self.numbers = (form,) if form in (0, 1) else (1, 0)

    def start(self, *after):
        swaps = zip(self.sent, self.numbers)
        self.got = [self.grid.swap(tie(sent, *after), number) for sent, number in swaps]
        return self

    def second(self, *after):
        sent, self.groups = [], []
        for own, got, number in zip(self.own, self.got, self.numbers):
            away, kept = add_halves([own, tie(got, *after)], 1 - number)
            sent.append(away)
            self.groups.append([kept, self.grid.swap(away, 1 - number)])
        self.sent = tuple(sent)
        return self


class BitSum:
    def __init__(self, grid, parts):
        self.grid, self.sent, self.kept = grid, *parts

    def start(self, *after):
        self.got = self.grid.swap(tie(self.sent, *after), 2)
        return self

    def step(self, number, *after):
        def cut(array):
            rows, columns = array.shape[-2:]
            count = array.size // (rows * columns)
            if number >= 2:
                count, rows = count // 4, rows * 4
            else:
                count = 1
                rows = array.size // (2 * columns)
            return array.reshape(count if number < 2 else count // 2, 2, rows, columns)

        self.sent, self.kept = add_halves([cut(self.kept), cut(tie(self.got, *after))], number)
        self.got = self.grid.swap(self.sent, number)
        if number >= 2:
            shape = (self.sent.shape[0], 4, self.sent.shape[1] // 4, self.sent.shape[2])
            self.kept, self.got = self.kept.reshape(shape), self.got.reshape(shape)
        return self

    def line(self, *after):
        for number in self.grid.line_bits[1:]:
            self.step(number, *after)
        return self

    def result(self):
        return wide(self.kept[0]) + wide(self.got[0])


class LineSum:
    def __init__(self, grid, sums):
        self.grid, self.packs = grid, [found.groups for found in sums]

    def step(self, number, after):
        packs = [
            [
                [t.reshape((t.shape[0] // 2, 2) + t.shape[1:]) for t in (*kept, tie(got, *after))]
                for *kept, got in groups
            ]
            for groups in self.packs
        ]
        self.sent, kept = add_joined(packs, number)
        self.packs = [[[kept, self.grid.swap(self.sent, number)]]]
        return self

    def third(self, *after):
        return self.step(self.grid.line_bits[0], after)

    def fourth(self, *after):
        for number in self.grid.line_bits[1:]:
            self.step(number, after)
        return self

    def result(self):
        return sum(wide(term[0]) for term in self.packs[0][0])


def running_sum(values, reverse):
    length = values.shape[1]
    place = lax.broadcasted_iota(jnp.int32, values.shape, 1)
    shift = 1
    while shift < length:
        if reverse:
            moved = jnp.where(place < length - shift, pltpu.roll(values, length - shift, 1), 0.0)
        else:
            moved = jnp.where(place >= shift, pltpu.roll(values, shift, 1), 0.0)
        values = values + moved
        shift *= 2
    return values


def decay_kernel(heads, logit_ref, bias_ref, row_ref, column_ref):
    length, lanes = logit_ref.shape
    groups, per, _ = row_ref.shape
    padded = -(-heads // 8) * 8
    logit = (logit_ref[...] + bias_ref[...]).T[:padded]
    decay = running_sum(-jnp.log1p(jnp.exp(-logit)), False)
    columns = jnp.concatenate([decay, jnp.zeros((lanes - padded, length), jnp.float32)], axis=0).T
    for group in range(groups):
        row_ref[group] = decay[group * per : (group + 1) * per]
        column_ref[group] = columns[:, group * per : (group + 1) * per]


def decays(logit, bias, heads, per):
    length = logit.shape[0]
    groups = heads // per
    return pl.pallas_call(
        functools.partial(decay_kernel, heads),
        out_shape=[
            jax.ShapeDtypeStruct((groups, per, length), jnp.float32),
            jax.ShapeDtypeStruct((groups, length, per), jnp.float32),
        ],
        compiler_params=pltpu.CompilerParams(vmem_limit_bytes=VMEM_LIMIT),
    )(logit, bias)


def forget_kernel(heads, row_ref, column_ref, logit_ref, bias_ref, grad_ref, sum_ref):
    length, lanes = logit_ref.shape
    groups, per, _ = row_ref.shape
    padded = -(-heads // 8) * 8
    rows = [row_ref[group] for group in range(groups)]
    columns = [column_ref[group] for group in range(groups)]
    columns = jnp.concatenate(
        columns + [jnp.zeros((length, lanes - heads), jnp.float32)], axis=1
    ).T[:padded]
    if padded > heads:
        rows = rows + [jnp.zeros((padded - heads, length), jnp.float32)]
    grad_log = running_sum(jnp.concatenate(rows, axis=0) - columns, True)
    grad_log = jnp.concatenate([grad_log, jnp.zeros((lanes - padded, length), jnp.float32)], axis=0).T
    grad = lower(grad_log * jax.nn.sigmoid(-(logit_ref[...] + bias_ref[...])))
    lane = lax.broadcasted_iota(jnp.int32, grad.shape, 1)
    grad = jnp.where(lane < heads, grad, jnp.bfloat16(0))
    grad_ref[...] = grad
    sum_ref[...] = jnp.sum(wide(grad), axis=0, keepdims=True)


def forget_backward(row, column, logit, bias, heads):
    return pl.pallas_call(
        functools.partial(forget_kernel, heads),
        out_shape=[
            jax.ShapeDtypeStruct(logit.shape, jnp.bfloat16),
            jax.ShapeDtypeStruct(bias.shape, jnp.float32),
        ],
        compiler_params=pltpu.CompilerParams(vmem_limit_bytes=VMEM_LIMIT),
    )(row, column, logit, bias)


def fwd_kernel(scale, head, q_ref, k_ref, v_ref, col_ref, row_ref, o_ref, lse_ref, out_t):
    length, lanes = q_ref.shape
    span = min(256, length)
    lane = lax.broadcasted_iota(jnp.int32, (span, lanes), 1) // head
    below = lax.broadcasted_iota(jnp.int32, (span, span), 0) <= lax.broadcasted_iota(jnp.int32, (span, span), 1)
    v_t = v_ref[...].T
    for h in range(lanes // head):
        for b in range(length // span):
            lo, hi = b * span, (b + 1) * span
            q = jnp.where(lane == h, q_ref[lo:hi, :] * scale, 0).astype(jnp.bfloat16)
            row = row_ref[0, h:h+1, lo:hi]
            diag = second_contract(k_ref[lo:hi, :], q) + row - col_ref[0, lo:hi, h:h+1]
            diag = jnp.where(below, diag, -1e30)
            top = jnp.max(diag, axis=0, keepdims=True)
            if lo:
                off = second_contract(k_ref[:lo, :], q) + row - col_ref[0, :lo, h:h+1]
                top = jnp.maximum(top, jnp.max(off, axis=0, keepdims=True))
            e = jnp.exp(diag - top)
            total = jnp.sum(e, axis=0, keepdims=True)
            v_h = v_t[h*head:(h+1)*head]
            acc = matmul(v_h[:, lo:hi], lower(e))
            if lo:
                e = jnp.exp(off - top)
                total = total + jnp.sum(e, axis=0, keepdims=True)
                acc = acc + matmul(v_h[:, :lo], lower(e))
            out_t[h*head:(h+1)*head, lo:hi] = acc / total
            lse_ref[0, h:h+1, lo:hi] = top + jnp.log(total)
    o_ref[...] = out_t[...].T

def bwd_kernel(scale, head, q_ref, k_ref, v_ref, do_ref, col_ref, row_ref, lse_ref, dq_ref, dk_ref, dv_ref, drow_ref, dcol_ref, dq_t, dk_acc, dv_acc):
    length, lanes = q_ref.shape
    span = min(256, length)
    heads = lanes // head
    lane = lax.broadcasted_iota(jnp.int32, (span, lanes), 1) // head
    sub = lax.broadcasted_iota(jnp.int32, (lanes, length), 0) // head
    below = lax.broadcasted_iota(jnp.int32, (span, span), 0) <= lax.broadcasted_iota(jnp.int32, (span, span), 1)
    k_t = k_ref[...].T
    one = jnp.bfloat16(1)
    for h in range(heads):
        kt_h = jnp.where(sub == h, k_t, one)
        mine = lane == h
        for b in range(length // span):
            lo, hi = b * span, (b + 1) * span
            q = q_ref[lo:hi, :] * jnp.bfloat16(scale)
            qz = jnp.where(mine, q, jnp.bfloat16(0))
            q1 = jnp.where(mine, q, one)
            do = do_ref[lo:hi, :]
            doz = jnp.where(mine, do, jnp.bfloat16(0))
            row = row_ref[0, h:h+1, lo:hi] - lse_ref[0, h:h+1, lo:hi]
            s = second_contract(k_ref[lo:hi, :], qz) + row - col_ref[0, lo:hi, h:h+1]
            p = jnp.exp(jnp.where(below, s, -1e30))
            dp = second_contract(v_ref[lo:hi, :], doz)
            centre = jnp.sum(p * dp, axis=0, keepdims=True)
            if lo:
                s0 = second_contract(k_ref[:lo, :], qz) + row - col_ref[0, :lo, h:h+1]
                p0 = jnp.exp(s0)
                dp0 = second_contract(v_ref[:lo, :], doz)
                centre = centre + jnp.sum(p0 * dp0, axis=0, keepdims=True)
            ds = lower(p * (dp - centre))
            dqt = matmul(kt_h[:, lo:hi], ds)
            dv_acc[h, lo:hi, :] = matmul(lower(p), do)
            dk_acc[h, lo:hi, :] = matmul(ds, q1)
            if lo:
                ds0 = lower(p0 * (dp0 - centre))
                dqt = dqt + matmul(kt_h[:, :lo], ds0)
                dv_acc[h, :lo, :] = dv_acc[h, :lo, :] + matmul(lower(p0), do)
                dk_acc[h, :lo, :] = dk_acc[h, :lo, :] + matmul(ds0, q1)
            dq_t[h*head:(h+1)*head, lo:hi] = dqt[h*head:(h+1)*head] * scale
            other = ((h + 1) % heads) * head
            drow_ref[0, h:h+1, lo:hi] = dqt[other:other+1]
    lane_all = lax.broadcasted_iota(jnp.int32, (length, lanes), 1) // head
    dk, dv = dk_acc[0], dv_acc[0]
    for h in range(1, heads):
        dk = jnp.where(lane_all == h, dk_acc[h], dk)
        dv = jnp.where(lane_all == h, dv_acc[h], dv)
    for h in range(heads):
        other = ((h + 1) % heads) * head
        dcol_ref[0, :, h:h+1] = dk_acc[h][:, other:other+1]
    dq_ref[...] = lower(dq_t[...].T)
    dk_ref[...] = lower(dk)
    dv_ref[...] = lower(dv)


def pair_specs(length, groups, per):
    def block(offset):
        return pl.BlockSpec((length, LANES), lambda group: (0, group + offset))

    column = pl.BlockSpec((1, length, per), lambda group: (group, 0, 0))
    row = pl.BlockSpec((1, per, length), lambda group: (group, 0, 0))
    return block, column, row


def attention_cost(length, width, head, products):
    return small_cost(products * 6 * length * length * width, 16 * length * width)


def attend(qk, values, column, row, head):
    length, width = values.shape[0], qk.shape[1] // 2
    groups, per, _ = row.shape
    block, column_spec, row_spec = pair_specs(length, groups, per)
    return pl.pallas_call(
        functools.partial(fwd_kernel, head**-0.5, head),
        grid=(groups,),
        in_specs=[block(0), block(groups), block(0), column_spec, row_spec],
        out_specs=[block(0), row_spec],
        out_shape=[
            jax.ShapeDtypeStruct((length, width), jnp.float32),
            jax.ShapeDtypeStruct(row.shape, jnp.float32),
        ],
        scratch_shapes=[pltpu.VMEM((LANES, length), jnp.float32)],
        cost_estimate=attention_cost(length, width, head, 2),
        compiler_params=pltpu.CompilerParams(vmem_limit_bytes=VMEM_LIMIT),
    )(qk, qk, values, column, row)


def attend_backward(qk, values, grad, column, row, logsum, head):
    length, width = values.shape[0], qk.shape[1] // 2
    groups, per, _ = row.shape
    block, column_spec, row_spec = pair_specs(length, groups, per)
    wide_out = jax.ShapeDtypeStruct((length, width), jnp.bfloat16)
    return pl.pallas_call(
        functools.partial(bwd_kernel, head**-0.5, head),
        grid=(groups,),
        in_specs=[block(0), block(groups), block(0), block(0), column_spec, row_spec, row_spec],
        out_specs=[block(0), block(0), block(0), row_spec, column_spec],
        out_shape=[
            wide_out,
            wide_out,
            wide_out,
            jax.ShapeDtypeStruct(row.shape, jnp.float32),
            jax.ShapeDtypeStruct(column.shape, jnp.float32),
        ],
        scratch_shapes=[
            pltpu.VMEM((LANES, length), jnp.float32),
            pltpu.VMEM((per, length, LANES), jnp.float32),
            pltpu.VMEM((per, length, LANES), jnp.float32),
        ],
        cost_estimate=attention_cost(length, width, head, 5),
        compiler_params=pltpu.CompilerParams(vmem_limit_bytes=VMEM_LIMIT),
    )(qk, qk, values, grad, column, row, logsum)


def per_device(
    tokens,
    w_query,
    w_key,
    w_value,
    w_gate_attn,
    w_forget,
    forget_bias,
    w_out,
    norm_attn,
    norm_mlp,
    w_gate,
    w_up,
    w_down,
    cotangent,
):
    grid = Grid()
    side = lax.axis_index("tensor")
    heads_here = forget_bias.shape[0]
    width = w_query.shape[1]
    head_size = width // heads_here
    hidden_here = w_gate.shape[1]
    scale = head_size ** (-0.5)
    rows_here = tokens.shape[0]

    load_qk = Gather(grid, jnp.concatenate([lower(w_query), lower(w_key)], axis=1))
    own_gains = jnp.stack([norm_attn, norm_mlp])
    other_gains = partner(own_gains)
    gains = jnp.where(
        side == 0,
        jnp.concatenate([own_gains, other_gains], axis=1),
        jnp.concatenate([other_gains, own_gains], axis=1),
    )[None]
    pair_gains, gain_codes = gains[0], [0]
    for number in range(len(grid.line_bits) + 2):
        gains = jnp.concatenate([gains, grid.swap(gains, number)], axis=0)
        gain_codes = gain_codes + [code ^ (1 << number) for code in gain_codes]
        if number == 1:
            load_qk.line_end(gains)
    (all_gains,) = grid.place([(gain_codes, gains)], [gains.shape[2]])
    all_gains = all_gains.reshape(grid.count, 2, all_gains.shape[1])
    gain_attn = all_gains[:, 0].reshape(-1)
    gain_mlp = all_gains[:, 1].reshape(-1)
    load_qk.plane(fine=True)
    other_cotangent = partner(tie(cotangent, gains))

    padding = jnp.zeros((w_forget.shape[0], LANES - heads_here), jnp.bfloat16)
    forget_lanes = jnp.concatenate([lower(w_forget), padding], axis=1)
    load_vf = Gather(
        grid, jnp.concatenate([lower(w_value), forget_lanes], axis=1), load_qk.far, gains
    )
    load_vf.line_end(*load_qk.corner_parts).plane(*load_qk.corners)
    load_go = Gather(
        grid, jnp.concatenate([lower(w_gate_attn), lower(w_out).T], axis=1), load_vf.far
    )
    load_go.line_end(load_vf.block)
    gain_attn, gain_mlp = gain_attn[None], gain_mlp[None]
    low = jnp.bfloat16
    columns = tokens.shape[1]
    rounded_outs = [(columns, low), (columns // 2, low), (columns // 2, low)]

    def exchanged(parts):
        return [partner(part) for part in parts]

    own_attn, *sent = row_kernel(
        lambda rows, gain: halves(lower(statistics(wide(rows))[0] * gain)),
        [tokens, gain_attn],
        rounded_outs,
    )
    normed_attn, normed_attn_t = joined_rows(own_attn, exchanged(sent), True)
    grad_output, grad_output_t = joined_rows(cotangent, [other_cotangent], False)

    load_go.plane(*load_vf.corners, normed_attn)
    load_gate = Gather(grid, lower(w_gate), load_go.far).line_end(load_go.block)
    load_up = Gather(grid, lower(w_up), load_gate.far, load_go.corners[0])
    value_w, forget_w = load_vf.weight.part(0, width), load_vf.weight.part(width, LANES)
    query_w, key_w = load_qk.weight.part(0, width), load_qk.weight.part(width, width)
    gate_w, out_w = load_go.weight.part(0, width), load_go.weight.part(width, width)

    (qk,) = multiply(
        normed_attn, load_qk.weight, 3, lambda p: (lower(p),), [], [(2 * width, low)]
    )
    values_all, forget_logit = multiply(
        normed_attn,
        load_vf.weight,
        1,
        lambda p: (lower(p[:, :width]), p[:, width:]),
        [],
        [(width, low), (LANES, jnp.float32)],
    )
    bias_lanes = jnp.pad(forget_bias, (0, LANES - heads_here))[None]
    decay_row, decay_column = decays(forget_logit, bias_lanes, heads_here, LANES // head_size)
    load_gate.plane(*load_go.corners, qk, to_end=False)
    load_up.line_end(load_gate.block, decay_row, values_all)
    qk = tie(qk, load_gate.block)
    attended, logsum = attend(qk, values_all, decay_column, decay_row, head_size)
    load_gate.plane_end(attended)
    load_up.plane(*load_gate.corners)
    load_down = Gather(grid, lower(w_down).T, load_up.far, load_gate.corners[0])
    load_down.line_end(load_up.block)
    mlp_gate, mlp_up = load_gate.weight, load_up.weight

    def gate_output(product, attended):
        sigmoid = jax.nn.sigmoid(product)
        return sigmoid, lower(attended * sigmoid)

    gate_sig, gated = multiply(
        normed_attn, gate_w, 2, gate_output, [attended], [(width, jnp.float32), (width, low)]
    )
    arrived = exchanged(multiply_back([(gated, out_w)], 1 - side, low, 2))
    (own_part,) = multiply_back([(gated, out_w)], side)
    middle, own_normed, *sent = row_kernel(
        norm_forward,
        [tokens, own_part, *arrived, gain_mlp],
        [(columns, jnp.float32)] + rounded_outs,
    )
    normed_mlp, normed_mlp_t = joined_rows(own_normed, exchanged(sent), False)
    (gate_act,) = multiply(
        normed_mlp, mlp_gate, 4, lambda p: (lower(p),), [], [(hidden_here, low)]
    )

    load_down.plane(*load_up.corners, gate_act)
    mlp_down = load_down.weight

    def hidden_units(up, gate):
        gate = wide(gate)
        return lower(up), lower(gate * jax.nn.sigmoid(gate) * up)

    up_act, hidden = multiply(
        normed_mlp, mlp_up, 4, hidden_units, [gate_act], [(hidden_here, low)] * 2
    )
    sum_down = weight_gradient(grid, [(grad_output_t, hidden)], 4, "line").start()

    def hidden_backward(grad, gate, up):
        gate, up = wide(gate), wide(up)
        sigmoid = jax.nn.sigmoid(gate)
        return (
            lower(grad * (gate * sigmoid)),
            lower(grad * up * sigmoid * (1.0 + gate * (1.0 - sigmoid))),
        )

    grad_up, grad_gate = multiply(
        tie(grad_output, sum_down.sent),
        mlp_down,
        4,
        hidden_backward,
        [gate_act, up_act],
        [(hidden_here, low)] * 2,
    )
    sum_up = weight_gradient(grid, [(normed_mlp_t, grad_up)], 4, 0)
    sum_up.start()
    grad_gate = tie(grad_gate, *sum_up.sent)
    sum_gate = weight_gradient(grid, [(normed_mlp_t, grad_gate)], 4, 1).start()
    grad_gate = tie(grad_gate, *sum_gate.sent)
    back = [(grad_gate, mlp_gate), (grad_up, mlp_up)]
    arrived = exchanged(multiply_back(back, jnp.int32(1), low, 2))
    (own_part,) = multiply_back(back, jnp.int32(0))
    sum_down.line(own_part)
    own_part = tie(own_part, sum_down.sent)
    grad_middle, own_branch, *sent = row_kernel(
        norm_gradient_halves,
        [middle, own_part, *arrived, cotangent, gain_mlp],
        [(columns, jnp.float32)] + rounded_outs,
    )
    other_branch = exchanged(sent)
    grad_branch, grad_branch_t = joined_rows(own_branch, other_branch, True)

    def gate_backward(grad, sigmoid, attended):
        return lower(grad * sigmoid), lower(grad * attended * sigmoid * (1.0 - sigmoid))

    grad_attended, grad_gate_logit = multiply(
        grad_branch,
        out_w,
        2,
        gate_backward,
        [gate_sig, attended],
        [(width, low)] * 2,
    )
    sum_up.second(grad_attended)
    sum_gate.second(grad_attended)
    grad_gate_logit = tie(grad_gate_logit, *sum_up.sent, *sum_gate.sent)
    sum_go = weight_gradient(
        grid, [(normed_attn_t, grad_gate_logit), (grad_branch_t, gated)], 4, "halves"
    ).start()
    grad_attended = tie(grad_attended, *sum_go.sent)
    grad_queries, grad_keys, grad_values, row_total, column_total = attend_backward(
        qk, values_all, grad_attended, decay_column, decay_row, logsum, head_size
    )
    line_mlp = LineSum(grid, [sum_gate, sum_up]).third(grad_queries)
    sum_down.step(1, grad_queries)
    grad_queries = tie(grad_queries, line_mlp.sent, sum_down.sent)
    sum_qk = weight_gradient(
        grid, [(normed_attn_t, grad_queries), (normed_attn_t, grad_keys)], 4, "halves"
    )
    sum_qk.start()
    sum_go.second(*sum_qk.sent)
    grad_forget, bias_part = forget_backward(
        row_total, column_total, forget_logit, bias_lanes, heads_here
    )
    bias_block = jnp.pad(
        bias_part[0, :heads_here, None],
        ((0, w_forget.shape[0] - heads_here), (heads_here, LANES - heads_here - 1)),
    )
    bias_extra = jnp.tile(bias_block, (grid.count, 1))
    grad_values = tie(grad_values, *sum_qk.sent, *sum_go.sent)
    sum_vf = weight_gradient(
        grid,
        [(normed_attn_t, grad_values), (normed_attn_t, grad_forget)],
        1,
        "halves",
        bias_extra,
    )
    back = [
        (tie(grad_gate_logit, *sum_vf.sent), gate_w),
        (grad_queries, query_w),
        (grad_keys, key_w),
        (grad_values, value_w),
        (grad_forget, forget_w),
    ]
    other_part = multiply_back(back, 1 - side, low, 2)
    arrived = exchanged(other_part)
    hidden = tie(hidden, *other_part)
    other_down = multiply_back([(hidden, mlp_down)], jnp.int32(1), low, 2)
    arrived_down = exchanged(other_down)
    sum_qk.second(*other_down)
    line_mlp.fourth(*other_down)
    sum_vf.start(*sum_qk.sent)
    back[1] = (tie(grad_queries, line_mlp.sent, *sum_qk.sent), query_w)
    (own_part,) = multiply_back(back, side)
    line_go = LineSum(grid, [sum_go]).third(own_part)
    own_part = tie(own_part, line_go.sent)
    _, tokens_grad = row_kernel(
        norm_gradient,
        [tokens, own_part, *arrived, grad_middle, gain_attn],
        [(columns, jnp.float32), (columns, low)],
    )
    sum_vf.second(tokens_grad)
    line_qkv = LineSum(grid, [sum_qk, sum_vf]).third()
    (own_down,) = multiply_back([(tie(hidden, line_qkv.sent), mlp_down)], jnp.int32(0))
    (mixed,) = row_kernel(
        lambda middle, own, *parts: (lower(middle + (own + both_parts(*parts))),),
        [middle, own_down, *arrived_down],
        [(columns, low)],
    )
    line_qkv.fourth(own_down)
    line_go.fourth(line_qkv.sent)
    sum_down.step(0, line_qkv.sent)
    down_grad, go_grad, qkv_grad = sum_down.result().T, line_go.result(), line_qkv.result()
    mlp_grad = line_mlp.result()

    def gain_gradient(gain, *pairs):
        return sum(jnp.sum(wide(lower(w)) * grad, axis=1) for w, grad in pairs) / gain

    forget_at = 3 * width
    parts = jnp.stack(
        [
            gain_gradient(
                pair_gains[0],
                (w_query, qkv_grad[:, :width]),
                (w_key, qkv_grad[:, width : 2 * width]),
                (w_value, qkv_grad[:, 2 * width : forget_at]),
                (w_forget, qkv_grad[:, forget_at : forget_at + heads_here]),
                (w_gate_attn, go_grad[:, :width]),
            ),
            gain_gradient(
                pair_gains[1], (w_gate, mlp_grad[:, :hidden_here]), (w_up, mlp_grad[:, hidden_here:])
            ),
        ]
    ).reshape(2, 2, norm_attn.shape[0])
    gain_grads = pick(parts, 1, side) + partner(pick(parts, 1, 1 - side))
    return (
        mixed,
        tokens_grad,
        qkv_grad[:, :width],
        qkv_grad[:, width : 2 * width],
        qkv_grad[:, 2 * width : 3 * width],
        go_grad[:, :width],
        qkv_grad[:, 3 * width : 3 * width + heads_here],
        qkv_grad[:heads_here, forget_at + heads_here],
        go_grad[:, width:].T,
        gain_grads[0],
        gain_grads[1],
        mlp_grad[:, :hidden_here],
        mlp_grad[:, hidden_here:],
        down_grad,
    )


def solution(mesh):
    return jax.shard_map(
        per_device,
        mesh=mesh,
        in_specs=(
            P(("dp", "tensor"), None),
            P("dp", "tensor"),
            P("dp", "tensor"),
            P("dp", "tensor"),
            P("dp", "tensor"),
            P("dp", "tensor"),
            P("tensor"),
            P("tensor", "dp"),
            P(("dp", "tensor")),
            P(("dp", "tensor")),
            P("dp", "tensor"),
            P("dp", "tensor"),
            P("tensor", "dp"),
            P(("dp", "tensor"), None),
        ),
        out_specs=(
            P(("dp", "tensor"), None),
            P(("dp", "tensor"), None),
            P("dp", "tensor"),
            P("dp", "tensor"),
            P("dp", "tensor"),
            P("dp", "tensor"),
            P("dp", "tensor"),
            P("tensor"),
            P("tensor", "dp"),
            P(("dp", "tensor")),
            P(("dp", "tensor")),
            P("dp", "tensor"),
            P("dp", "tensor"),
            P("tensor", "dp"),
        ),
        check_vma=False,
    )
```

```python
import functools

import jax
import jax.numpy as jnp
from jax import lax
from jax.experimental import pallas as pl
from jax.experimental.pallas import tpu as pltpu
from jax.sharding import PartitionSpec as P

EPSILON = 1e-06
LANES = 128
VMEM_LIMIT = 50 * 2**20
COST_SCALE = 0.02


def lower(values):
    return values.astype(jnp.bfloat16)


def wide(values):
    return values.astype(jnp.float32)


def matmul(left, right):
    return jnp.dot(left, right, preferred_element_type=jnp.float32)


def first_contract(left, right):
    return lax.dot_general(
        left, right, (((0,), (0,)), ((), ())), preferred_element_type=jnp.float32
    )


def second_contract(left, right):
    return lax.dot_general(
        left, right, (((1,), (1,)), ((), ())), preferred_element_type=jnp.float32
    )


def statistics(values):
    inverse = lax.rsqrt(jnp.mean(values * values, axis=-1, keepdims=True) + EPSILON)
    return (values * inverse, inverse)


def norm_backward(unit, inverse, gain, grad):
    scaled = gain * grad
    return inverse * (scaled - unit * jnp.mean(scaled * unit, axis=-1, keepdims=True))


def partner(values):
    return lax.ppermute(values, "tensor", [(0, 1), (1, 0)])


def tie(value, *others):
    if not others:
        return value
    return lax.optimization_barrier((value, *others))[0]


def small_cost(flops, size):
    return pl.CostEstimate(
        flops=int(COST_SCALE * flops), bytes_accessed=int(COST_SCALE * size), transcendentals=0
    )


class Grid:
    def __init__(self):
        self.count = lax.axis_size("dp")
        self.index = lax.axis_index("dp")
        bits = self.count.bit_length() - 1
        self.line_bits = list(range(2, bits))

    def bit(self, number):
        return (self.index >> number) & 1

    def swap(self, values, number):
        pairs = [(i, i ^ (1 << number)) for i in range(self.count)]
        return lax.ppermute(values, "dp", pairs)

    def place(self, pieces, splits):
        rows = pieces[0][1].shape[1]
        arrays = [piece for _, piece in pieces]
        codes = [code for found, _ in pieces for code in found]
        kind = arrays[0].dtype

        def body(*refs):
            inputs, results, sem = refs[: len(arrays)], refs[len(arrays) : -1], refs[-1]
            here = lax.axis_index("dp")
            copies = []
            for (found, _), ref in zip(pieces, inputs):
                for number, code in enumerate(found):
                    start = 0
                    for width, result in zip(splits, results):
                        copies.append(
                            pltpu.make_async_copy(
                                ref.at[number, :, pl.ds(start, width)],
                                result.at[here ^ code],
                                sem.at[len(copies)],
                            )
                        )
                        start += width
            for copy in copies:
                copy.start()
            for copy in copies:
                copy.wait()

        size = self.count * rows * sum(splits) * kind.itemsize
        results = pl.pallas_call(
            body,
            out_shape=[jax.ShapeDtypeStruct((self.count, rows, w), kind) for w in splits],
            in_specs=[pl.BlockSpec(memory_space=pl.ANY)] * len(arrays),
            out_specs=[pl.BlockSpec(memory_space=pltpu.VMEM)] * len(splits),
            scratch_shapes=[pltpu.SemaphoreType.DMA((len(codes) * len(splits),))],
            compiler_params=pltpu.CompilerParams(vmem_limit_bytes=VMEM_LIMIT),
            cost_estimate=small_cost(0, 2 * size),
        )(*arrays)
        return [r.reshape(self.count * rows, w) for r, w in zip(results, splits)]


class Weight:
    def __init__(self, grid, pieces, first=0, width=None):
        self.grid, self.pieces, self.first = grid, pieces, first
        self.rows = pieces[0][1].shape[1]
        self.width = width or pieces[0][1].shape[2]
        self.in_kernel = self.rows % 16 == 0

    def part(self, first, width):
        return Weight(self.grid, self.pieces, self.first + first, width)

    def arrays(self):
        return [piece for _, piece in self.pieces]

    def assembled(self):
        pieces = [
            (codes, piece[:, :, self.first : self.first + self.width])
            for codes, piece in self.pieces
        ]
        return self.grid.place(pieces, [self.width])[0]

    def copies(self, refs, target, sem, tiles):
        here = lax.axis_index("dp")
        tile = self.width // tiles
        found = []
        for step in range(tiles):
            for (codes, _), ref in zip(self.pieces, refs):
                for number, code in enumerate(codes):
                    block = here ^ code
                    source = ref.at[number, :, pl.ds(self.first + step * tile, tile)]
                    found.append(
                        pltpu.make_async_copy(source, target(step, block), sem.at[step, block])
                    )
        return found


def multiply(left, weight, tiles, epilogue, extras, outs):
    if not weight.in_kernel:
        return epilogue(matmul(left, weight.assembled()), *extras)
    grid, rows = weight.grid, weight.rows
    length, depth = left.shape
    tile = weight.width // tiles
    arrays = weight.arrays()

    def body(*refs):
        left_ref, refs = refs[0], refs[1:]
        piece_refs, refs = refs[: len(arrays)], refs[len(arrays) :]
        extra_refs, refs = refs[: len(extras)], refs[len(extras) :]
        out_refs, (held, sem) = refs[: len(outs)], refs[len(outs) :]
        step = pl.program_id(0)

        def target(place, block):
            return held.at[place, pl.ds(pl.multiple_of(block * rows, 16), rows)]

        @pl.when(step == 0)
        def _():
            for copy in weight.copies(piece_refs, target, sem, tiles):
                copy.start()

        for block in range(grid.count):
            there = target(step, block)
            pltpu.make_async_copy(there, there, sem.at[step, block]).wait()
        results = epilogue(matmul(left_ref[...], held[step]), *[ref[...] for ref in extra_refs])
        for ref, result in zip(out_refs, results):
            ref[...] = result

    def column_block(width):
        return pl.BlockSpec((length, width // tiles), lambda step: (0, step))

    size = (
        left.size * 2
        + depth * weight.width * 2
        + sum(e.size * e.dtype.itemsize for e in extras)
        + sum(length * w * jnp.dtype(kind).itemsize for w, kind in outs)
    )
    return pl.pallas_call(
        body,
        grid=(tiles,),
        in_specs=[pl.BlockSpec((length, depth), lambda step: (0, 0))]
        + [pl.BlockSpec(memory_space=pl.ANY)] * len(arrays)
        + [column_block(extra.shape[1]) for extra in extras],
        out_specs=[column_block(width) for width, _ in outs],
        out_shape=[jax.ShapeDtypeStruct((length, width), kind) for width, kind in outs],
        scratch_shapes=[
            pltpu.VMEM((tiles, depth, tile), jnp.bfloat16),
            pltpu.SemaphoreType.DMA((tiles, grid.count)),
        ],
        cost_estimate=small_cost(2 * length * depth * weight.width, size),
        compiler_params=pltpu.CompilerParams(vmem_limit_bytes=VMEM_LIMIT),
    )(left, *arrays, *extras)


def multiply_back(terms, half, kind=jnp.float32, parts=1, tiles=4):
    grid, rows = terms[0][1].grid, terms[0][1].rows
    length = terms[0][0].shape[0] // 2
    if not terms[0][1].in_kernel:
        total = sum(
            second_contract(
                lax.dynamic_slice_in_dim(left, half * length, length, 0), weight.assembled()
            )
            for left, weight in terms
        )
        return jnp.split(total.astype(kind), parts, axis=1)
    depth = grid.count * rows
    tile, share = depth // tiles, grid.count // tiles
    run = tiles // parts

    def part_spec(number):
        return pl.BlockSpec(
            (length, tile), lambda step, which: (0, jnp.clip(step - number * run, 0, run - 1))
        )

    sources, counts = [], []
    for _, weight in terms:
        sources = sources + weight.arrays()
        counts.append(len(weight.pieces))

    def body(half_ref, *refs):
        left_refs, refs = refs[: len(terms)], refs[len(terms) :]
        piece_refs, refs = refs[: len(sources)], refs[len(sources) :]
        out_refs, refs = refs[:parts], refs[parts:]
        held, sems = refs[: len(terms)], refs[len(terms) :]
        step = pl.program_id(0)

        def target(number):
            def found(_, block):
                return held[number].at[pl.ds(pl.multiple_of(block * rows, 16), rows)]

            return found

        @pl.when(step == 0)
        def _():
            first = 0
            for number, (_, weight) in enumerate(terms):
                mine = piece_refs[first : first + counts[number]]
                first += counts[number]
                for copy in weight.copies(mine, target(number), sems[number], 1):
                    copy.start()

        total = None
        for number in range(len(terms)):
            for part in range(share):
                block = step * share + part
                there = target(number)(0, block)
                pltpu.make_async_copy(there, there, sems[number].at[0, block]).wait()
            found = held[number][pl.ds(pl.multiple_of(step * tile, 16), tile), :]
            product = second_contract(left_refs[number][...], found)
            total = product if total is None else total + product
        for number, out_ref in enumerate(out_refs):

            @pl.when(step // run == number)
            def _():
                out_ref[...] = total.astype(kind)

    size = length * depth * 4 + sum(l.size + depth * w.width * 2 for l, w in terms)
    flops = sum(2 * length * depth * w.width for _, w in terms)
    return pl.pallas_call(
        body,
        grid_spec=pltpu.PrefetchScalarGridSpec(
            num_scalar_prefetch=1,
            grid=(tiles,),
            in_specs=[
                pl.BlockSpec((length, left.shape[1]), lambda step, which: (which[0], 0))
                for left, _ in terms
            ]
            + [pl.BlockSpec(memory_space=pl.ANY)] * len(sources),
            out_specs=[part_spec(number) for number in range(parts)],
            scratch_shapes=[pltpu.VMEM((depth, w.width), jnp.bfloat16) for _, w in terms]
            + [pltpu.SemaphoreType.DMA((1, grid.count)) for _ in terms],
        ),
        out_shape=[jax.ShapeDtypeStruct((length, depth // parts), kind)] * parts,
        cost_estimate=small_cost(flops, size),
        compiler_params=pltpu.CompilerParams(vmem_limit_bytes=VMEM_LIMIT),
    )(jnp.reshape(half, (1,)).astype(jnp.int32), *[left for left, _ in terms], *sources)


class Gather:
    def __init__(self, grid, shard, *after):
        near, codes = tie(shard[None], *after), [0]
        for number in reversed(grid.line_bits[1:]):
            found = grid.swap(near, number)
            near = jnp.concatenate([near, found], axis=0)
            codes = codes + self.moved(codes, 1 << number)
        self.grid, self.near, self.codes = grid, near, codes

    def moved(self, found, plane):
        return [code ^ plane for code in found]

    def line_end(self, *after):
        last = self.grid.line_bits[0]
        self.near = tie(self.near, *after)
        self.far = self.grid.swap(self.near, last)
        self.far_codes = self.moved(self.codes, 1 << last)
        return self

    def plane(self, *after, fine=False, to_end=True):
        grid, near, far, codes, far_codes = (
            self.grid,
            self.near,
            self.far,
            self.codes,
            self.far_codes,
        )
        moved, both, half = self.moved, self.codes + self.far_codes, len(self.codes)
        if fine:
            near_x, near_y = grid.swap(near, 0), grid.swap(near, 1)
            far_x, far_y = grid.swap(far, 0), grid.swap(far, 1)
            sides = [
                (codes, near),
                (far_codes, far),
                (moved(codes, 1), near_x),
                (moved(codes, 2), near_y),
                (moved(far_codes, 1), far_x),
                (moved(far_codes, 2), far_y),
            ]
            received = (near_y, far_x)
        else:
            block = tie(jnp.concatenate([near, far], axis=0), *after)
            side_x, side_y = grid.swap(block, 0), grid.swap(block, 1)
            near_x, far_y = side_x[:half], side_y[half:]
            sides = [(both, block), (moved(both, 1), side_x), (moved(both, 2), side_y)]
            received = ()
            self.block = block
        self.corner_parts, self.received, self.sides = (near_x, far_y), received, sides
        return self.plane_end() if to_end else self

    def plane_end(self, *after):
        grid, codes, far_codes = self.grid, self.codes, self.far_codes
        moved, sides = self.moved, self.sides
        near_x, far_y = [tie(part, *after) for part in self.corner_parts]
        near_corner, far_corner = grid.swap(near_x, 1), grid.swap(far_y, 0)
        self.corners = (near_corner, far_corner, *self.received)
        corners = [(moved(codes, 3), near_corner), (moved(far_codes, 3), far_corner)]
        self.weight = Weight(grid, sides + corners)
        return self


def gradient_parts(grid, pairs, tiles, form, extra=None):
    depth, length = pairs[0][0].shape
    rows, line = depth // grid.count, grid.count // 4
    width = sum(right.shape[1] for _, right in pairs)
    lefts = []
    for left, _ in pairs:
        if not any(left is other for other in lefts):
            lefts.append(left)
    which = [[left is other for other in lefts].index(True) for left, _ in pairs]
    tile = width // tiles
    starts, first = [], 0
    for _, right in pairs:
        starts.append(first)
        first += right.shape[1]

    def body(*refs):
        left_refs, refs = refs[: len(lefts)], refs[len(lefts) :]
        right_refs, refs = refs[: len(pairs)], refs[len(pairs) :]
        if extra is not None:
            extra_ref, refs = refs[0], refs[1:]
        outs, total = refs[:-1], refs[-1]
        step = pl.program_id(0)
        if tiles == 1:
            for place in range(len(pairs)):
                ahead = starts[place]
                total[:, ahead : ahead + pairs[place][1].shape[1]] = matmul(
                    left_refs[which[place]][...], right_refs[place][...]
                )
        elif len(pairs) == 1:
            total[...] = matmul(left_refs[0][...], right_refs[0][...])
        else:
            for place in range(len(pairs)):
                low = starts[place] // tile
                high = low + pairs[place][1].shape[1] // tile

                @pl.when((step >= low) & (step < high))
                def _():
                    total[...] = matmul(left_refs[which[place]][...], right_refs[place][...])

        if extra is not None:
            total[:, tile - extra.shape[1] :] += extra_ref[...]
        index = lax.axis_index("dp")

        def block(place):
            return lower(total[pl.ds(pl.multiple_of(place * rows, 8), rows), :])

        if form == "line":
            here = (index >> 2) & 1
            for place in range(half):
                for plane in range(4):
                    outs[0][place, plane] = block((2 * place + 1 - here) * 4 + plane)
                    outs[1][place, plane] = block((2 * place + here) * 4 + plane)
            return

        for number, first, count, away, own in (
            [(form, 0, line, *outs)]
            if form in (0, 1)
            else [(1, 0, half, outs[0], outs[2]), (0, half, half, outs[1], outs[3])]
        ):
            here = (index >> number) & 1
            for place in range(count):
                for side in range(2):
                    base = (first + place) * 4 + side * (3 - (1 << number))
                    away[place, side] = block(base + ((1 - here) << number))
                    own[place, side] = block(base + (here << number))

    def right_spec(place):
        columns = pairs[place][1].shape[1]
        if tiles == 1:
            return pl.BlockSpec((length, columns), lambda step: (0, 0))
        low, count = starts[place] // tile, columns // tile
        return pl.BlockSpec((length, tile), lambda step: (0, jnp.clip(step - low, 0, count - 1)))

    half = line // 2
    cut, parts = {"line": ((half, 4), 2), "halves": ((half, 2), 4)}.get(form, ((line, 2), 2))
    out = jax.ShapeDtypeStruct((*cut, rows, width), jnp.bfloat16)
    out_spec = pl.BlockSpec((*cut, rows, tile), lambda step: (0, 0, 0, step))
    size = depth * width * 2 + sum(l.size * 2 for l in lefts) + sum(r.size * 2 for _, r in pairs)
    return pl.pallas_call(
        body,
        grid=(tiles,),
        in_specs=[pl.BlockSpec((depth, length), lambda step: (0, 0))] * len(lefts)
        + [right_spec(place) for place in range(len(pairs))]
        + ([] if extra is None else [pl.BlockSpec(extra.shape, lambda step: (0, 0))]),
        out_specs=[out_spec] * parts,
        out_shape=[out] * parts,
        scratch_shapes=[pltpu.VMEM((depth, tile), jnp.float32)],
        cost_estimate=small_cost(2 * depth * length * width, size),
        compiler_params=pltpu.CompilerParams(vmem_limit_bytes=VMEM_LIMIT),
    )(*lefts, *[right for _, right in pairs], *([] if extra is None else [extra]))


def pick(array, axis, place):
    return lax.dynamic_index_in_dim(array, place, axis, keepdims=False)


def cut_parts(grid, array, form):
    line, rows = grid.count // 4, array.shape[0] // grid.count
    blocks = array.reshape(line, 2, 2, rows, array.shape[1])

    def cut(blocks, number):
        here, axis = grid.bit(number), 2 - number
        return pick(blocks, axis, 1 - here), pick(blocks, axis, here)

    if form in (0, 1):
        return cut(blocks, form)
    if form == "line":
        here, whole = grid.bit(2), array.reshape(line // 2, 2, 4, rows, array.shape[1])
        return pick(whole, 1, 1 - here), pick(whole, 1, here)
    low, high = cut(blocks[: line // 2], 1), cut(blocks[line // 2 :], 0)
    return low[0], high[0], low[1], high[1]


def weight_gradient(grid, pairs, tiles, form, extra=None):
    rows = pairs[0][0].shape[0] // grid.count
    if rows % 16 == 0:
        parts = gradient_parts(grid, pairs, tiles, form, extra)
    else:
        found = [matmul(left, right) for left, right in pairs]
        if extra is not None:
            found[-1] = found[-1] + extra
        parts = cut_parts(grid, lower(jnp.concatenate(found, axis=1)), form)
    return BitSum(grid, parts) if form == "line" else PlaneSum(grid, parts, form)


def add_halves(terms, number):
    count, _, rows, columns = terms[0].shape
    tile = next(t for t in (512, 384, 256, 128, columns) if columns % t == 0)

    def body(*refs):
        inputs, (away, kept) = refs[: len(terms)], refs[len(terms) :]
        side = (lax.axis_index("dp") >> number) & 1
        for place in range(count):
            away[place] = lower(sum(wide(ref[place, 1 - side]) for ref in inputs))
            kept[place] = lower(sum(wide(ref[place, side]) for ref in inputs))

    block = pl.BlockSpec((count, 2, rows, tile), lambda step: (0, 0, 0, step))
    half = pl.BlockSpec((count, rows, tile), lambda step: (0, 0, step))
    size = terms[0].size * (2 * len(terms) + 2)
    return pl.pallas_call(
        body,
        grid=(columns // tile,),
        in_specs=[block] * len(terms),
        out_specs=[half] * 2,
        out_shape=[jax.ShapeDtypeStruct((count, rows, columns), jnp.bfloat16)] * 2,
        cost_estimate=small_cost(0, size),
        compiler_params=pltpu.CompilerParams(vmem_limit_bytes=VMEM_LIMIT),
    )(*terms)


def add_joined(packs, number):
    rows = packs[0][0][0].shape[2]
    widths = [pack[0][0].shape[3] for pack in packs]
    count = sum(group[0].shape[0] for group in packs[0])
    flat = [term for pack in packs for group in pack for term in group]

    def body(*refs):
        inputs, (away, kept) = list(refs[: len(flat)]), refs[len(flat) :]
        side = (lax.axis_index("dp") >> number) & 1
        start = 0
        for pack, width in zip(packs, widths):
            place = 0
            for group in pack:
                terms = [inputs.pop(0) for _ in group]
                for row in range(group[0].shape[0]):
                    other = sum(wide(term[row, 1 - side]) for term in terms)
                    own = sum(wide(term[row, side]) for term in terms)
                    away[place, :, start : start + width] = lower(other)
                    kept[place, :, start : start + width] = lower(own)
                    place += 1
            start += width

    out = jax.ShapeDtypeStruct((count, rows, sum(widths)), jnp.bfloat16)
    return pl.pallas_call(
        body,
        out_shape=[out] * 2,
        cost_estimate=small_cost(0, 2 * sum(term.size for term in flat)),
        compiler_params=pltpu.CompilerParams(vmem_limit_bytes=VMEM_LIMIT),
    )(*flat)


def joined_rows(own, others, in_sequence):
    rows, columns = own.shape
    tile, run = columns // 4, 4 // len(others)

    def body(own_ref, *refs):
        other_refs, (rows_ref, turned_ref) = refs[: len(others)], refs[len(others) :]
        first, second = own_ref[...], other_refs[0][...]
        for number in range(1, len(others)):
            later = pl.program_id(0) >= number * run
            second = jnp.where(later, other_refs[number][...], second)
        if in_sequence:
            ahead = lax.axis_index("tensor") == 0
            first, second = jnp.where(ahead, first, second), jnp.where(ahead, second, first)
        rows_ref[:rows] = first
        rows_ref[rows:] = second
        turned_ref[:, :rows] = first.T
        turned_ref[:, rows:] = second.T

    def part_spec(number):
        return pl.BlockSpec(
            (rows, tile), lambda step: (0, jnp.clip(step - number * run, 0, run - 1))
        )

    return pl.pallas_call(
        body,
        grid=(4,),
        in_specs=[pl.BlockSpec((rows, tile), lambda step: (0, step))]
        + [part_spec(number) for number in range(len(others))],
        out_specs=[
            pl.BlockSpec((2 * rows, tile), lambda step: (0, step)),
            pl.BlockSpec((tile, 2 * rows), lambda step: (step, 0)),
        ],
        out_shape=[
            jax.ShapeDtypeStruct((2 * rows, columns), own.dtype),
            jax.ShapeDtypeStruct((columns, 2 * rows), own.dtype),
        ],
        cost_estimate=small_cost(0, 12 * rows * columns),
        compiler_params=pltpu.CompilerParams(vmem_limit_bytes=VMEM_LIMIT),
    )(own, *others)


def row_kernel(body, inputs, outs, sums=0):
    length, columns = inputs[0].shape
    tile = length // 4

    def spec(rows, width):
        if rows == 1:
            return pl.BlockSpec((1, width), lambda step: (0, 0))
        return pl.BlockSpec((tile, width), lambda step: (step, 0))

    def kernel(*refs):
        found = body(*[ref[...] for ref in refs[: len(inputs)]])
        out_refs = refs[len(inputs) :]
        for ref, value in zip(out_refs[: len(outs)], found):
            ref[...] = value
        for ref, value in zip(out_refs[len(outs) :], found[len(outs) :]):

            @pl.when(pl.program_id(0) == 0)
            def _():
                ref[...] = jnp.zeros_like(ref)

            ref[...] += value

    size = length * columns * (sum(i.dtype.itemsize for i in inputs) + 4 * len(outs))
    return pl.pallas_call(
        kernel,
        grid=(4,),
        in_specs=[spec(*i.shape) for i in inputs],
        out_specs=[spec(length, width) for width, _ in outs] + [spec(1, columns)] * sums,
        out_shape=[jax.ShapeDtypeStruct((length, width), kind) for width, kind in outs]
        + [jax.ShapeDtypeStruct((1, columns), jnp.float32)] * sums,
        cost_estimate=small_cost(0, size),
        compiler_params=pltpu.CompilerParams(vmem_limit_bytes=VMEM_LIMIT),
    )(*inputs)


def halves(values):
    half = values.shape[1] // 2
    return values, values[:, :half], values[:, half:]


def both_parts(first, second):
    return wide(jnp.concatenate([first, second], axis=1))


def norm_forward(residual, own, first, second, gain):
    middle = wide(residual) + (own + both_parts(first, second))
    unit, _ = statistics(middle)
    return middle, *halves(lower(unit * gain))


def norm_gradient(source, own, first, second, base, gain):
    unit, inverse = statistics(wide(source))
    grad = own + both_parts(first, second)
    total = wide(base) + norm_backward(unit, inverse, gain, grad)
    return total, lower(total)


def norm_gradient_halves(*values):
    total, rounded = norm_gradient(*values)
    return total, *halves(rounded)


class PlaneSum:
    def __init__(self, grid, parts, form):
        half = len(parts) // 2
        self.grid, self.sent, self.own = grid, tuple(parts[:half]), tuple(parts[half:])
        self.numbers = (form,) if form in (0, 1) else (1, 0)

    def start(self, *after):
        swaps = zip(self.sent, self.numbers)
        self.got = [self.grid.swap(tie(sent, *after), number) for sent, number in swaps]
        return self

    def second(self, *after):
        sent, self.groups = [], []
        for own, got, number in zip(self.own, self.got, self.numbers):
            away, kept = add_halves([own, tie(got, *after)], 1 - number)
            sent.append(away)
            self.groups.append([kept, self.grid.swap(away, 1 - number)])
        self.sent = tuple(sent)
        return self


class BitSum:
    def __init__(self, grid, parts):
        self.grid, self.sent, self.kept = grid, *parts

    def start(self, *after):
        self.got = self.grid.swap(tie(self.sent, *after), 2)
        return self

    def step(self, number, *after):
        def cut(array):
            rows, columns = array.shape[-2:]
            count = array.size // (rows * columns)
            if number >= 2:
                count, rows = count // 4, rows * 4
            else:
                count = 1
                rows = array.size // (2 * columns)
            return array.reshape(count if number < 2 else count // 2, 2, rows, columns)

        self.sent, self.kept = add_halves([cut(self.kept), cut(tie(self.got, *after))], number)
        self.got = self.grid.swap(self.sent, number)
        if number >= 2:
            shape = (self.sent.shape[0], 4, self.sent.shape[1] // 4, self.sent.shape[2])
            self.kept, self.got = self.kept.reshape(shape), self.got.reshape(shape)
        return self

    def line(self, *after):
        for number in self.grid.line_bits[1:]:
            self.step(number, *after)
        return self

    def result(self):
        return wide(self.kept[0]) + wide(self.got[0])


class LineSum:
    def __init__(self, grid, sums):
        self.grid, self.packs = grid, [found.groups for found in sums]

    def step(self, number, after):
        packs = [
            [
                [t.reshape((t.shape[0] // 2, 2) + t.shape[1:]) for t in (*kept, tie(got, *after))]
                for *kept, got in groups
            ]
            for groups in self.packs
        ]
        self.sent, kept = add_joined(packs, number)
        self.packs = [[[kept, self.grid.swap(self.sent, number)]]]
        return self

    def third(self, *after):
        return self.step(self.grid.line_bits[0], after)

    def fourth(self, *after):
        for number in self.grid.line_bits[1:]:
            self.step(number, after)
        return self

    def result(self):
        return sum(wide(term[0]) for term in self.packs[0][0])


def running_sum(values, reverse):
    length = values.shape[1]
    place = lax.broadcasted_iota(jnp.int32, values.shape, 1)
    shift = 1
    while shift < length:
        if reverse:
            moved = jnp.where(place < length - shift, pltpu.roll(values, length - shift, 1), 0.0)
        else:
            moved = jnp.where(place >= shift, pltpu.roll(values, shift, 1), 0.0)
        values = values + moved
        shift *= 2
    return values


def decay_kernel(heads, logit_ref, bias_ref, row_ref, column_ref):
    length, lanes = logit_ref.shape
    groups, per, _ = row_ref.shape
    padded = -(-heads // 8) * 8
    logit = (logit_ref[...] + bias_ref[...]).T[:padded]
    decay = running_sum(-jnp.log1p(jnp.exp(-logit)), False)
    columns = jnp.concatenate([decay, jnp.zeros((lanes - padded, length), jnp.float32)], axis=0).T
    for group in range(groups):
        row_ref[group] = decay[group * per : (group + 1) * per]
        column_ref[group] = columns[:, group * per : (group + 1) * per]


def decays(logit, bias, heads, per):
    length = logit.shape[0]
    groups = heads // per
    return pl.pallas_call(
        functools.partial(decay_kernel, heads),
        out_shape=[
            jax.ShapeDtypeStruct((groups, per, length), jnp.float32),
            jax.ShapeDtypeStruct((groups, length, per), jnp.float32),
        ],
        compiler_params=pltpu.CompilerParams(vmem_limit_bytes=VMEM_LIMIT),
    )(logit, bias)


def forget_kernel(heads, row_ref, column_ref, logit_ref, bias_ref, grad_ref, sum_ref):
    length, lanes = logit_ref.shape
    groups, per, _ = row_ref.shape
    padded = -(-heads // 8) * 8
    rows = [row_ref[group] for group in range(groups)]
    columns = [column_ref[group] for group in range(groups)]
    columns = jnp.concatenate(
        columns + [jnp.zeros((length, lanes - heads), jnp.float32)], axis=1
    ).T[:padded]
    if padded > heads:
        rows = rows + [jnp.zeros((padded - heads, length), jnp.float32)]
    grad_log = running_sum(jnp.concatenate(rows, axis=0) - columns, True)
    grad_log = jnp.concatenate([grad_log, jnp.zeros((lanes - padded, length), jnp.float32)], axis=0).T
    grad = lower(grad_log * jax.nn.sigmoid(-(logit_ref[...] + bias_ref[...])))
    lane = lax.broadcasted_iota(jnp.int32, grad.shape, 1)
    grad = jnp.where(lane < heads, grad, jnp.bfloat16(0))
    grad_ref[...] = grad
    sum_ref[...] = jnp.sum(wide(grad), axis=0, keepdims=True)


def forget_backward(row, column, logit, bias, heads):
    return pl.pallas_call(
        functools.partial(forget_kernel, heads),
        out_shape=[
            jax.ShapeDtypeStruct(logit.shape, jnp.bfloat16),
            jax.ShapeDtypeStruct(bias.shape, jnp.float32),
        ],
        compiler_params=pltpu.CompilerParams(vmem_limit_bytes=VMEM_LIMIT),
    )(row, column, logit, bias)


def fwd_kernel(scale, head, q_ref, k_ref, v_ref, col_ref, row_ref, o_ref, lse_ref, out_t):
    length, lanes = q_ref.shape
    span = min(256, length)
    lane = lax.broadcasted_iota(jnp.int32, (span, lanes), 1) // head
    below = lax.broadcasted_iota(jnp.int32, (span, span), 0) <= lax.broadcasted_iota(jnp.int32, (span, span), 1)
    v_t = v_ref[...].T
    for h in range(lanes // head):
        for b in range(length // span):
            lo, hi = b * span, (b + 1) * span
            q = jnp.where(lane == h, q_ref[lo:hi, :] * scale, 0).astype(jnp.bfloat16)
            row = row_ref[0, h:h+1, lo:hi]
            diag = second_contract(k_ref[lo:hi, :], q) + row - col_ref[0, lo:hi, h:h+1]
            diag = jnp.where(below, diag, -1e30)
            top = jnp.max(diag, axis=0, keepdims=True)
            if lo:
                off = second_contract(k_ref[:lo, :], q) + row - col_ref[0, :lo, h:h+1]
                top = jnp.maximum(top, jnp.max(off, axis=0, keepdims=True))
            e = jnp.exp(diag - top)
            total = jnp.sum(e, axis=0, keepdims=True)
            v_h = v_t[h*head:(h+1)*head]
            acc = matmul(v_h[:, lo:hi], lower(e))
            if lo:
                e = jnp.exp(off - top)
                total = total + jnp.sum(e, axis=0, keepdims=True)
                acc = acc + matmul(v_h[:, :lo], lower(e))
            out_t[h*head:(h+1)*head, lo:hi] = acc / total
            lse_ref[0, h:h+1, lo:hi] = top + jnp.log(total)
    o_ref[...] = out_t[...].T

def bwd_kernel(scale, head, q_ref, k_ref, v_ref, do_ref, col_ref, row_ref, lse_ref, dq_ref, dk_ref, dv_ref, drow_ref, dcol_ref, dq_t, dk_acc, dv_acc):
    length, lanes = q_ref.shape
    span = min(256, length)
    heads = lanes // head
    lane = lax.broadcasted_iota(jnp.int32, (span, lanes), 1) // head
    sub = lax.broadcasted_iota(jnp.int32, (lanes, length), 0) // head
    below = lax.broadcasted_iota(jnp.int32, (span, span), 0) <= lax.broadcasted_iota(jnp.int32, (span, span), 1)
    k_t = k_ref[...].T
    one = jnp.bfloat16(1)
    for h in range(heads):
        kt_h = jnp.where(sub == h, k_t, one)
        mine = lane == h
        for b in range(length // span):
            lo, hi = b * span, (b + 1) * span
            q = q_ref[lo:hi, :] * jnp.bfloat16(scale)
            qz = jnp.where(mine, q, jnp.bfloat16(0))
            q1 = jnp.where(mine, q, one)
            do = do_ref[lo:hi, :]
            doz = jnp.where(mine, do, jnp.bfloat16(0))
            row = row_ref[0, h:h+1, lo:hi] - lse_ref[0, h:h+1, lo:hi]
            s = second_contract(k_ref[lo:hi, :], qz) + row - col_ref[0, lo:hi, h:h+1]
            p = jnp.exp(jnp.where(below, s, -1e30))
            dp = second_contract(v_ref[lo:hi, :], doz)
            centre = jnp.sum(p * dp, axis=0, keepdims=True)
            if lo:
                s0 = second_contract(k_ref[:lo, :], qz) + row - col_ref[0, :lo, h:h+1]
                p0 = jnp.exp(s0)
                dp0 = second_contract(v_ref[:lo, :], doz)
                centre = centre + jnp.sum(p0 * dp0, axis=0, keepdims=True)
            ds = lower(p * (dp - centre))
            dqt = matmul(kt_h[:, lo:hi], ds)
            dv_acc[h, lo:hi, :] = matmul(lower(p), do)
            dk_acc[h, lo:hi, :] = matmul(ds, q1)
            if lo:
                ds0 = lower(p0 * (dp0 - centre))
                dqt = dqt + matmul(kt_h[:, :lo], ds0)
                dv_acc[h, :lo, :] = dv_acc[h, :lo, :] + matmul(lower(p0), do)
                dk_acc[h, :lo, :] = dk_acc[h, :lo, :] + matmul(ds0, q1)
            dq_t[h*head:(h+1)*head, lo:hi] = dqt[h*head:(h+1)*head] * scale
            other = ((h + 1) % heads) * head
            drow_ref[0, h:h+1, lo:hi] = dqt[other:other+1]
    lane_all = lax.broadcasted_iota(jnp.int32, (length, lanes), 1) // head
    dk, dv = dk_acc[0], dv_acc[0]
    for h in range(1, heads):
        dk = jnp.where(lane_all == h, dk_acc[h], dk)
        dv = jnp.where(lane_all == h, dv_acc[h], dv)
    for h in range(heads):
        other = ((h + 1) % heads) * head
        dcol_ref[0, :, h:h+1] = dk_acc[h][:, other:other+1]
    dq_ref[...] = lower(dq_t[...].T)
    dk_ref[...] = lower(dk)
    dv_ref[...] = lower(dv)


def pair_specs(length, groups, per):
    def block(offset):
        return pl.BlockSpec((length, LANES), lambda group: (0, group + offset))

    column = pl.BlockSpec((1, length, per), lambda group: (group, 0, 0))
    row = pl.BlockSpec((1, per, length), lambda group: (group, 0, 0))
    return block, column, row


def attention_cost(length, width, head, products):
    return small_cost(products * 6 * length * length * width, 16 * length * width)


def attend(qk, values, column, row, head):
    length, width = values.shape[0], qk.shape[1] // 2
    groups, per, _ = row.shape
    block, column_spec, row_spec = pair_specs(length, groups, per)
    return pl.pallas_call(
        functools.partial(fwd_kernel, head**-0.5, head),
        grid=(groups,),
        in_specs=[block(0), block(groups), block(0), column_spec, row_spec],
        out_specs=[block(0), row_spec],
        out_shape=[
            jax.ShapeDtypeStruct((length, width), jnp.float32),
            jax.ShapeDtypeStruct(row.shape, jnp.float32),
        ],
        scratch_shapes=[pltpu.VMEM((LANES, length), jnp.float32)],
        cost_estimate=attention_cost(length, width, head, 2),
        compiler_params=pltpu.CompilerParams(vmem_limit_bytes=VMEM_LIMIT),
    )(qk, qk, values, column, row)


def attend_backward(qk, values, grad, column, row, logsum, head):
    length, width = values.shape[0], qk.shape[1] // 2
    groups, per, _ = row.shape
    block, column_spec, row_spec = pair_specs(length, groups, per)
    wide_out = jax.ShapeDtypeStruct((length, width), jnp.bfloat16)
    return pl.pallas_call(
        functools.partial(bwd_kernel, head**-0.5, head),
        grid=(groups,),
        in_specs=[block(0), block(groups), block(0), block(0), column_spec, row_spec, row_spec],
        out_specs=[block(0), block(0), block(0), row_spec, column_spec],
        out_shape=[
            wide_out,
            wide_out,
            wide_out,
            jax.ShapeDtypeStruct(row.shape, jnp.float32),
            jax.ShapeDtypeStruct(column.shape, jnp.float32),
        ],
        scratch_shapes=[
            pltpu.VMEM((LANES, length), jnp.float32),
            pltpu.VMEM((per, length, LANES), jnp.float32),
            pltpu.VMEM((per, length, LANES), jnp.float32),
        ],
        cost_estimate=attention_cost(length, width, head, 5),
        compiler_params=pltpu.CompilerParams(vmem_limit_bytes=VMEM_LIMIT),
    )(qk, qk, values, grad, column, row, logsum)


def per_device(
    tokens,
    w_query,
    w_key,
    w_value,
    w_gate_attn,
    w_forget,
    forget_bias,
    w_out,
    norm_attn,
    norm_mlp,
    w_gate,
    w_up,
    w_down,
    cotangent,
):
    grid = Grid()
    side = lax.axis_index("tensor")
    heads_here = forget_bias.shape[0]
    width = w_query.shape[1]
    head_size = width // heads_here
    hidden_here = w_gate.shape[1]
    scale = head_size ** (-0.5)
    rows_here = tokens.shape[0]

    load_qk = Gather(grid, jnp.concatenate([lower(w_query), lower(w_key)], axis=1))
    own_gains = jnp.stack([norm_attn, norm_mlp])
    other_gains = partner(own_gains)
    gains = jnp.where(
        side == 0,
        jnp.concatenate([own_gains, other_gains], axis=1),
        jnp.concatenate([other_gains, own_gains], axis=1),
    )[None]
    pair_gains, gain_codes = gains[0], [0]
    for number in range(len(grid.line_bits) + 2):
        gains = jnp.concatenate([gains, grid.swap(gains, number)], axis=0)
        gain_codes = gain_codes + [code ^ (1 << number) for code in gain_codes]
        if number == 1:
            load_qk.line_end(gains)
    (all_gains,) = grid.place([(gain_codes, gains)], [gains.shape[2]])
    all_gains = all_gains.reshape(grid.count, 2, all_gains.shape[1])
    gain_attn = all_gains[:, 0].reshape(-1)
    gain_mlp = all_gains[:, 1].reshape(-1)
    load_qk.plane(fine=True)
    other_cotangent = partner(tie(cotangent, gains))

    padding = jnp.zeros((w_forget.shape[0], LANES - heads_here), jnp.bfloat16)
    forget_lanes = jnp.concatenate([lower(w_forget), padding], axis=1)
    load_vf = Gather(
        grid, jnp.concatenate([lower(w_value), forget_lanes], axis=1), load_qk.far, gains
    )
    load_vf.line_end(*load_qk.corner_parts).plane(*load_qk.corners)
    load_go = Gather(
        grid, jnp.concatenate([lower(w_gate_attn), lower(w_out).T], axis=1), load_vf.far
    )
    load_go.line_end(load_vf.block)
    gain_attn, gain_mlp = gain_attn[None], gain_mlp[None]
    low = jnp.bfloat16
    columns = tokens.shape[1]
    rounded_outs = [(columns, low), (columns // 2, low), (columns // 2, low)]

    def exchanged(parts):
        return [partner(part) for part in parts]

    own_attn, *sent = row_kernel(
        lambda rows, gain: halves(lower(statistics(wide(rows))[0] * gain)),
        [tokens, gain_attn],
        rounded_outs,
    )
    normed_attn, normed_attn_t = joined_rows(own_attn, exchanged(sent), True)
    grad_output, grad_output_t = joined_rows(cotangent, [other_cotangent], False)

    load_go.plane(*load_vf.corners, normed_attn)
    load_gate = Gather(grid, lower(w_gate), load_go.far).line_end(load_go.block)
    load_up = Gather(grid, lower(w_up), load_gate.far, load_go.corners[0])
    value_w, forget_w = load_vf.weight.part(0, width), load_vf.weight.part(width, LANES)
    query_w, key_w = load_qk.weight.part(0, width), load_qk.weight.part(width, width)
    gate_w, out_w = load_go.weight.part(0, width), load_go.weight.part(width, width)

    (qk,) = multiply(
        normed_attn, load_qk.weight, 3, lambda p: (lower(p),), [], [(2 * width, low)]
    )
    values_all, forget_logit = multiply(
        normed_attn,
        load_vf.weight,
        1,
        lambda p: (lower(p[:, :width]), p[:, width:]),
        [],
        [(width, low), (LANES, jnp.float32)],
    )
    bias_lanes = jnp.pad(forget_bias, (0, LANES - heads_here))[None]
    decay_row, decay_column = decays(forget_logit, bias_lanes, heads_here, LANES // head_size)
    load_gate.plane(*load_go.corners, qk, to_end=False)
    load_up.line_end(load_gate.block, decay_row, values_all)
    qk = tie(qk, load_gate.block)
    attended, logsum = attend(qk, values_all, decay_column, decay_row, head_size)
    load_gate.plane_end(attended)
    load_up.plane(*load_gate.corners)
    load_down = Gather(grid, lower(w_down).T, load_up.far, load_gate.corners[0])
    load_down.line_end(load_up.block)
    mlp_gate, mlp_up = load_gate.weight, load_up.weight

    def gate_output(product, attended):
        sigmoid = jax.nn.sigmoid(product)
        return sigmoid, lower(attended * sigmoid)

    gate_sig, gated = multiply(
        normed_attn, gate_w, 2, gate_output, [attended], [(width, jnp.float32), (width, low)]
    )
    arrived = exchanged(multiply_back([(gated, out_w)], 1 - side, low, 2))
    (own_part,) = multiply_back([(gated, out_w)], side)
    middle, own_normed, *sent = row_kernel(
        norm_forward,
        [tokens, own_part, *arrived, gain_mlp],
        [(columns, jnp.float32)] + rounded_outs,
    )
    normed_mlp, normed_mlp_t = joined_rows(own_normed, exchanged(sent), False)
    (gate_act,) = multiply(
        normed_mlp, mlp_gate, 4, lambda p: (lower(p),), [], [(hidden_here, low)]
    )

    load_down.plane(*load_up.corners, gate_act, to_end=False)

    def hidden_units(up, gate):
        gate = wide(gate)
        return lower(up), lower(gate * jax.nn.sigmoid(gate) * up)

    up_act, hidden = multiply(
        normed_mlp, mlp_up, 4, hidden_units, [gate_act], [(hidden_here, low)] * 2
    )
    sum_down = weight_gradient(grid, [(grad_output_t, hidden)], 4, "line").start()
    mlp_down = load_down.plane_end(sum_down.sent).weight

    def hidden_backward(grad, gate, up):
        gate, up = wide(gate), wide(up)
        sigmoid = jax.nn.sigmoid(gate)
        return (
            lower(grad * (gate * sigmoid)),
            lower(grad * up * sigmoid * (1.0 + gate * (1.0 - sigmoid))),
        )

    grad_up, grad_gate = multiply(
        tie(grad_output, sum_down.sent),
        mlp_down,
        4,
        hidden_backward,
        [gate_act, up_act],
        [(hidden_here, low)] * 2,
    )
    sum_up = weight_gradient(grid, [(normed_mlp_t, grad_up)], 4, 0)
    sum_up.start()
    grad_gate = tie(grad_gate, *sum_up.sent)
    sum_gate = weight_gradient(grid, [(normed_mlp_t, grad_gate)], 4, 1).start()
    grad_gate = tie(grad_gate, *sum_gate.sent)
    back = [(grad_gate, mlp_gate), (grad_up, mlp_up)]
    arrived = exchanged(multiply_back(back, jnp.int32(1), low, 2))
    (own_part,) = multiply_back(back, jnp.int32(0))
    sum_down.line(own_part)
    own_part = tie(own_part, sum_down.sent)
    grad_middle, own_branch, *sent = row_kernel(
        norm_gradient_halves,
        [middle, own_part, *arrived, cotangent, gain_mlp],
        [(columns, jnp.float32)] + rounded_outs,
    )
    other_branch = exchanged(sent)
    grad_branch, grad_branch_t = joined_rows(own_branch, other_branch, True)

    def gate_backward(grad, sigmoid, attended):
        return lower(grad * sigmoid), lower(grad * attended * sigmoid * (1.0 - sigmoid))

    grad_attended, grad_gate_logit = multiply(
        grad_branch,
        out_w,
        2,
        gate_backward,
        [gate_sig, attended],
        [(width, low)] * 2,
    )
    sum_up.second(grad_attended)
    sum_gate.second(grad_attended)
    grad_gate_logit = tie(grad_gate_logit, *sum_up.sent, *sum_gate.sent)
    sum_go = weight_gradient(
        grid, [(normed_attn_t, grad_gate_logit), (grad_branch_t, gated)], 4, "halves"
    ).start()
    grad_attended = tie(grad_attended, *sum_go.sent)
    grad_queries, grad_keys, grad_values, row_total, column_total = attend_backward(
        qk, values_all, grad_attended, decay_column, decay_row, logsum, head_size
    )
    line_mlp = LineSum(grid, [sum_gate, sum_up]).third(grad_queries)
    sum_down.step(1, grad_queries)
    grad_queries = tie(grad_queries, line_mlp.sent, sum_down.sent)
    sum_qk = weight_gradient(
        grid, [(normed_attn_t, grad_queries), (normed_attn_t, grad_keys)], 4, "halves"
    )
    sum_qk.start()
    sum_go.second(*sum_qk.sent)
    grad_forget, bias_part = forget_backward(
        row_total, column_total, forget_logit, bias_lanes, heads_here
    )
    bias_block = jnp.pad(
        bias_part[0, :heads_here, None],
        ((0, w_forget.shape[0] - heads_here), (heads_here, LANES - heads_here - 1)),
    )
    bias_extra = jnp.tile(bias_block, (grid.count, 1))
    grad_values = tie(grad_values, *sum_qk.sent, *sum_go.sent)
    sum_vf = weight_gradient(
        grid,
        [(normed_attn_t, grad_values), (normed_attn_t, grad_forget)],
        1,
        "halves",
        bias_extra,
    )
    back = [
        (tie(grad_gate_logit, *sum_vf.sent), gate_w),
        (grad_queries, query_w),
        (grad_keys, key_w),
        (grad_values, value_w),
        (grad_forget, forget_w),
    ]
    other_part = multiply_back(back, 1 - side, low, 2)
    arrived = exchanged(other_part)
    hidden = tie(hidden, *other_part)
    other_down = multiply_back([(hidden, mlp_down)], jnp.int32(1), low, 2)
    arrived_down = exchanged(other_down)
    sum_qk.second(*other_down)
    line_mlp.fourth(*other_down)
    sum_vf.start(*sum_qk.sent)
    back[1] = (tie(grad_queries, line_mlp.sent, *sum_qk.sent), query_w)
    (own_part,) = multiply_back(back, side)
    line_go = LineSum(grid, [sum_go]).third(own_part)
    own_part = tie(own_part, line_go.sent)
    _, tokens_grad = row_kernel(
        norm_gradient,
        [tokens, own_part, *arrived, grad_middle, gain_attn],
        [(columns, jnp.float32), (columns, low)],
    )
    sum_vf.second(tokens_grad)
    line_qkv = LineSum(grid, [sum_qk, sum_vf]).third()
    (own_down,) = multiply_back([(tie(hidden, line_qkv.sent), mlp_down)], jnp.int32(0))
    (mixed,) = row_kernel(
        lambda middle, own, *parts: (lower(middle + (own + both_parts(*parts))),),
        [middle, own_down, *arrived_down],
        [(columns, low)],
    )
    line_qkv.fourth(own_down)
    line_go.fourth(line_qkv.sent)
    sum_down.step(0, line_qkv.sent)
    down_grad, go_grad, qkv_grad = sum_down.result().T, line_go.result(), line_qkv.result()
    mlp_grad = line_mlp.result()

    def gain_gradient(gain, *pairs):
        return sum(jnp.sum(wide(lower(w)) * grad, axis=1) for w, grad in pairs) / gain

    forget_at = 3 * width
    parts = jnp.stack(
        [
            gain_gradient(
                pair_gains[0],
                (w_query, qkv_grad[:, :width]),
                (w_key, qkv_grad[:, width : 2 * width]),
                (w_value, qkv_grad[:, 2 * width : forget_at]),
                (w_forget, qkv_grad[:, forget_at : forget_at + heads_here]),
                (w_gate_attn, go_grad[:, :width]),
            ),
            gain_gradient(
                pair_gains[1], (w_gate, mlp_grad[:, :hidden_here]), (w_up, mlp_grad[:, hidden_here:])
            ),
        ]
    ).reshape(2, 2, norm_attn.shape[0])
    gain_grads = pick(parts, 1, side) + partner(pick(parts, 1, 1 - side))
    return (
        mixed,
        tokens_grad,
        qkv_grad[:, :width],
        qkv_grad[:, width : 2 * width],
        qkv_grad[:, 2 * width : 3 * width],
        go_grad[:, :width],
        qkv_grad[:, 3 * width : 3 * width + heads_here],
        qkv_grad[:heads_here, forget_at + heads_here],
        go_grad[:, width:].T,
        gain_grads[0],
        gain_grads[1],
        mlp_grad[:, :hidden_here],
        mlp_grad[:, hidden_here:],
        down_grad,
    )


def solution(mesh):
    return jax.shard_map(
        per_device,
        mesh=mesh,
        in_specs=(
            P(("dp", "tensor"), None),
            P("dp", "tensor"),
            P("dp", "tensor"),
            P("dp", "tensor"),
            P("dp", "tensor"),
            P("dp", "tensor"),
            P("tensor"),
            P("tensor", "dp"),
            P(("dp", "tensor")),
            P(("dp", "tensor")),
            P("dp", "tensor"),
            P("dp", "tensor"),
            P("tensor", "dp"),
            P(("dp", "tensor"), None),
        ),
        out_specs=(
            P(("dp", "tensor"), None),
            P(("dp", "tensor"), None),
            P("dp", "tensor"),
            P("dp", "tensor"),
            P("dp", "tensor"),
            P("dp", "tensor"),
            P("dp", "tensor"),
            P("tensor"),
            P("tensor", "dp"),
            P(("dp", "tensor")),
            P(("dp", "tensor")),
            P("dp", "tensor"),
            P("dp", "tensor"),
            P("tensor", "dp"),
        ),
        check_vma=False,
    )
```

```python
import functools

import jax
import jax.numpy as jnp
from jax import lax
from jax.experimental import pallas as pl
from jax.experimental.pallas import tpu as pltpu
from jax.sharding import PartitionSpec as P

EPSILON = 1e-06
LANES = 128
VMEM_LIMIT = 50 * 2**20
COST_SCALE = 0.02


def lower(values):
    return values.astype(jnp.bfloat16)


def wide(values):
    return values.astype(jnp.float32)


def matmul(left, right):
    return jnp.dot(left, right, preferred_element_type=jnp.float32)


def first_contract(left, right):
    return lax.dot_general(
        left, right, (((0,), (0,)), ((), ())), preferred_element_type=jnp.float32
    )


def second_contract(left, right):
    return lax.dot_general(
        left, right, (((1,), (1,)), ((), ())), preferred_element_type=jnp.float32
    )


def statistics(values):
    inverse = lax.rsqrt(jnp.mean(values * values, axis=-1, keepdims=True) + EPSILON)
    return (values * inverse, inverse)


def norm_backward(unit, inverse, gain, grad):
    scaled = gain * grad
    return inverse * (scaled - unit * jnp.mean(scaled * unit, axis=-1, keepdims=True))


def partner(values):
    return lax.ppermute(values, "tensor", [(0, 1), (1, 0)])


def tie(value, *others):
    if not others:
        return value
    return lax.optimization_barrier((value, *others))[0]


def small_cost(flops, size):
    return pl.CostEstimate(
        flops=int(COST_SCALE * flops), bytes_accessed=int(COST_SCALE * size), transcendentals=0
    )


class Grid:
    def __init__(self):
        self.count = lax.axis_size("dp")
        self.index = lax.axis_index("dp")
        bits = self.count.bit_length() - 1
        self.line_bits = list(range(2, bits))

    def bit(self, number):
        return (self.index >> number) & 1

    def swap(self, values, number):
        pairs = [(i, i ^ (1 << number)) for i in range(self.count)]
        return lax.ppermute(values, "dp", pairs)

    def place(self, pieces, splits):
        rows = pieces[0][1].shape[1]
        arrays = [piece for _, piece in pieces]
        codes = [code for found, _ in pieces for code in found]
        kind = arrays[0].dtype

        def body(*refs):
            inputs, results, sem = refs[: len(arrays)], refs[len(arrays) : -1], refs[-1]
            here = lax.axis_index("dp")
            copies = []
            for (found, _), ref in zip(pieces, inputs):
                for number, code in enumerate(found):
                    start = 0
                    for width, result in zip(splits, results):
                        copies.append(
                            pltpu.make_async_copy(
                                ref.at[number, :, pl.ds(start, width)],
                                result.at[here ^ code],
                                sem.at[len(copies)],
                            )
                        )
                        start += width
            for copy in copies:
                copy.start()
            for copy in copies:
                copy.wait()

        size = self.count * rows * sum(splits) * kind.itemsize
        results = pl.pallas_call(
            body,
            out_shape=[jax.ShapeDtypeStruct((self.count, rows, w), kind) for w in splits],
            in_specs=[pl.BlockSpec(memory_space=pl.ANY)] * len(arrays),
            out_specs=[pl.BlockSpec(memory_space=pltpu.VMEM)] * len(splits),
            scratch_shapes=[pltpu.SemaphoreType.DMA((len(codes) * len(splits),))],
            compiler_params=pltpu.CompilerParams(vmem_limit_bytes=VMEM_LIMIT),
            cost_estimate=small_cost(0, 2 * size),
        )(*arrays)
        return [r.reshape(self.count * rows, w) for r, w in zip(results, splits)]


class Weight:
    def __init__(self, grid, pieces, first=0, width=None):
        self.grid, self.pieces, self.first = grid, pieces, first
        self.rows = pieces[0][1].shape[1]
        self.width = width or pieces[0][1].shape[2]
        self.in_kernel = self.rows % 16 == 0

    def part(self, first, width):
        return Weight(self.grid, self.pieces, self.first + first, width)

    def arrays(self):
        return [piece for _, piece in self.pieces]

    def assembled(self):
        pieces = [
            (codes, piece[:, :, self.first : self.first + self.width])
            for codes, piece in self.pieces
        ]
        return self.grid.place(pieces, [self.width])[0]

    def copies(self, refs, target, sem, tiles):
        here = lax.axis_index("dp")
        tile = self.width // tiles
        found = []
        for step in range(tiles):
            for (codes, _), ref in zip(self.pieces, refs):
                for number, code in enumerate(codes):
                    block = here ^ code
                    source = ref.at[number, :, pl.ds(self.first + step * tile, tile)]
                    found.append(
                        pltpu.make_async_copy(source, target(step, block), sem.at[step, block])
                    )
        return found


def multiply(left, weight, tiles, epilogue, extras, outs):
    if not weight.in_kernel:
        return epilogue(matmul(left, weight.assembled()), *extras)
    grid, rows = weight.grid, weight.rows
    length, depth = left.shape
    tile = weight.width // tiles
    arrays = weight.arrays()

    def body(*refs):
        left_ref, refs = refs[0], refs[1:]
        piece_refs, refs = refs[: len(arrays)], refs[len(arrays) :]
        extra_refs, refs = refs[: len(extras)], refs[len(extras) :]
        out_refs, (held, sem) = refs[: len(outs)], refs[len(outs) :]
        step = pl.program_id(0)

        def target(place, block):
            return held.at[place, pl.ds(pl.multiple_of(block * rows, 16), rows)]

        @pl.when(step == 0)
        def _():
            for copy in weight.copies(piece_refs, target, sem, tiles):
                copy.start()

        for block in range(grid.count):
            there = target(step, block)
            pltpu.make_async_copy(there, there, sem.at[step, block]).wait()
        results = epilogue(matmul(left_ref[...], held[step]), *[ref[...] for ref in extra_refs])
        for ref, result in zip(out_refs, results):
            ref[...] = result

    def column_block(width):
        return pl.BlockSpec((length, width // tiles), lambda step: (0, step))

    size = (
        left.size * 2
        + depth * weight.width * 2
        + sum(e.size * e.dtype.itemsize for e in extras)
        + sum(length * w * jnp.dtype(kind).itemsize for w, kind in outs)
    )
    return pl.pallas_call(
        body,
        grid=(tiles,),
        in_specs=[pl.BlockSpec((length, depth), lambda step: (0, 0))]
        + [pl.BlockSpec(memory_space=pl.ANY)] * len(arrays)
        + [column_block(extra.shape[1]) for extra in extras],
        out_specs=[column_block(width) for width, _ in outs],
        out_shape=[jax.ShapeDtypeStruct((length, width), kind) for width, kind in outs],
        scratch_shapes=[
            pltpu.VMEM((tiles, depth, tile), jnp.bfloat16),
            pltpu.SemaphoreType.DMA((tiles, grid.count)),
        ],
        cost_estimate=small_cost(2 * length * depth * weight.width, size),
        compiler_params=pltpu.CompilerParams(vmem_limit_bytes=VMEM_LIMIT),
    )(left, *arrays, *extras)


def multiply_back(terms, half, kind=jnp.float32, parts=1, tiles=4):
    grid, rows = terms[0][1].grid, terms[0][1].rows
    length = terms[0][0].shape[0] // 2
    if not terms[0][1].in_kernel:
        total = sum(
            second_contract(
                lax.dynamic_slice_in_dim(left, half * length, length, 0), weight.assembled()
            )
            for left, weight in terms
        )
        return jnp.split(total.astype(kind), parts, axis=1)
    depth = grid.count * rows
    tile, share = depth // tiles, grid.count // tiles
    run = tiles // parts

    def part_spec(number):
        return pl.BlockSpec(
            (length, tile), lambda step, which: (0, jnp.clip(step - number * run, 0, run - 1))
        )

    sources, counts = [], []
    for _, weight in terms:
        sources = sources + weight.arrays()
        counts.append(len(weight.pieces))

    def body(half_ref, *refs):
        left_refs, refs = refs[: len(terms)], refs[len(terms) :]
        piece_refs, refs = refs[: len(sources)], refs[len(sources) :]
        out_refs, refs = refs[:parts], refs[parts:]
        held, sems = refs[: len(terms)], refs[len(terms) :]
        step = pl.program_id(0)

        def target(number):
            def found(_, block):
                return held[number].at[pl.ds(pl.multiple_of(block * rows, 16), rows)]

            return found

        @pl.when(step == 0)
        def _():
            first = 0
            for number, (_, weight) in enumerate(terms):
                mine = piece_refs[first : first + counts[number]]
                first += counts[number]
                for copy in weight.copies(mine, target(number), sems[number], 1):
                    copy.start()

        total = None
        for number in range(len(terms)):
            for part in range(share):
                block = step * share + part
                there = target(number)(0, block)
                pltpu.make_async_copy(there, there, sems[number].at[0, block]).wait()
            found = held[number][pl.ds(pl.multiple_of(step * tile, 16), tile), :]
            product = second_contract(left_refs[number][...], found)
            total = product if total is None else total + product
        for number, out_ref in enumerate(out_refs):

            @pl.when(step // run == number)
            def _():
                out_ref[...] = total.astype(kind)

    size = length * depth * 4 + sum(l.size + depth * w.width * 2 for l, w in terms)
    flops = sum(2 * length * depth * w.width for _, w in terms)
    return pl.pallas_call(
        body,
        grid_spec=pltpu.PrefetchScalarGridSpec(
            num_scalar_prefetch=1,
            grid=(tiles,),
            in_specs=[
                pl.BlockSpec((length, left.shape[1]), lambda step, which: (which[0], 0))
                for left, _ in terms
            ]
            + [pl.BlockSpec(memory_space=pl.ANY)] * len(sources),
            out_specs=[part_spec(number) for number in range(parts)],
            scratch_shapes=[pltpu.VMEM((depth, w.width), jnp.bfloat16) for _, w in terms]
            + [pltpu.SemaphoreType.DMA((1, grid.count)) for _ in terms],
        ),
        out_shape=[jax.ShapeDtypeStruct((length, depth // parts), kind)] * parts,
        cost_estimate=small_cost(flops, size),
        compiler_params=pltpu.CompilerParams(vmem_limit_bytes=VMEM_LIMIT),
    )(jnp.reshape(half, (1,)).astype(jnp.int32), *[left for left, _ in terms], *sources)


class Gather:
    def __init__(self, grid, shard, *after):
        near, codes = tie(shard[None], *after), [0]
        for number in reversed(grid.line_bits[1:]):
            found = grid.swap(near, number)
            near = jnp.concatenate([near, found], axis=0)
            codes = codes + self.moved(codes, 1 << number)
        self.grid, self.near, self.codes = grid, near, codes

    def moved(self, found, plane):
        return [code ^ plane for code in found]

    def line_end(self, *after):
        last = self.grid.line_bits[0]
        self.near = tie(self.near, *after)
        self.far = self.grid.swap(self.near, last)
        self.far_codes = self.moved(self.codes, 1 << last)
        return self

    def plane(self, *after, fine=False, to_end=True):
        grid, near, far, codes, far_codes = (
            self.grid,
            self.near,
            self.far,
            self.codes,
            self.far_codes,
        )
        moved, both, half = self.moved, self.codes + self.far_codes, len(self.codes)
        if fine:
            near_x, near_y = grid.swap(near, 0), grid.swap(near, 1)
            far_x, far_y = grid.swap(far, 0), grid.swap(far, 1)
            sides = [
                (codes, near),
                (far_codes, far),
                (moved(codes, 1), near_x),
                (moved(codes, 2), near_y),
                (moved(far_codes, 1), far_x),
                (moved(far_codes, 2), far_y),
            ]
            received = (near_y, far_x)
        else:
            block = tie(jnp.concatenate([near, far], axis=0), *after)
            side_x, side_y = grid.swap(block, 0), grid.swap(block, 1)
            near_x, far_y = side_x[:half], side_y[half:]
            sides = [(both, block), (moved(both, 1), side_x), (moved(both, 2), side_y)]
            received = ()
            self.block = block
        self.corner_parts, self.received, self.sides = (near_x, far_y), received, sides
        return self.plane_end() if to_end else self

    def plane_end(self, *after):
        grid, codes, far_codes = self.grid, self.codes, self.far_codes
        moved, sides = self.moved, self.sides
        near_x, far_y = [tie(part, *after) for part in self.corner_parts]
        near_corner, far_corner = grid.swap(near_x, 1), grid.swap(far_y, 0)
        self.corners = (near_corner, far_corner, *self.received)
        corners = [(moved(codes, 3), near_corner), (moved(far_codes, 3), far_corner)]
        self.weight = Weight(grid, sides + corners)
        return self


def gradient_parts(grid, pairs, tiles, form, extra=None):
    depth, length = pairs[0][0].shape
    rows, line = depth // grid.count, grid.count // 4
    width = sum(right.shape[1] for _, right in pairs)
    lefts = []
    for left, _ in pairs:
        if not any(left is other for other in lefts):
            lefts.append(left)
    which = [[left is other for other in lefts].index(True) for left, _ in pairs]
    tile = width // tiles
    starts, first = [], 0
    for _, right in pairs:
        starts.append(first)
        first += right.shape[1]

    def body(*refs):
        left_refs, refs = refs[: len(lefts)], refs[len(lefts) :]
        right_refs, refs = refs[: len(pairs)], refs[len(pairs) :]
        if extra is not None:
            extra_ref, refs = refs[0], refs[1:]
        outs, total = refs[:-1], refs[-1]
        step = pl.program_id(0)
        if tiles == 1:
            for place in range(len(pairs)):
                ahead = starts[place]
                total[:, ahead : ahead + pairs[place][1].shape[1]] = matmul(
                    left_refs[which[place]][...], right_refs[place][...]
                )
        elif len(pairs) == 1:
            total[...] = matmul(left_refs[0][...], right_refs[0][...])
        else:
            for place in range(len(pairs)):
                low = starts[place] // tile
                high = low + pairs[place][1].shape[1] // tile

                @pl.when((step >= low) & (step < high))
                def _():
                    total[...] = matmul(left_refs[which[place]][...], right_refs[place][...])

        if extra is not None:
            total[:, tile - extra.shape[1] :] += extra_ref[...]
        index = lax.axis_index("dp")

        def block(place):
            return lower(total[pl.ds(pl.multiple_of(place * rows, 8), rows), :])

        if form == "line":
            here = (index >> 2) & 1
            for place in range(half):
                for plane in range(4):
                    outs[0][place, plane] = block((2 * place + 1 - here) * 4 + plane)
                    outs[1][place, plane] = block((2 * place + here) * 4 + plane)
            return

        for number, first, count, away, own in (
            [(form, 0, line, *outs)]
            if form in (0, 1)
            else [(1, 0, half, outs[0], outs[2]), (0, half, half, outs[1], outs[3])]
        ):
            here = (index >> number) & 1
            for place in range(count):
                for side in range(2):
                    base = (first + place) * 4 + side * (3 - (1 << number))
                    away[place, side] = block(base + ((1 - here) << number))
                    own[place, side] = block(base + (here << number))

    def right_spec(place):
        columns = pairs[place][1].shape[1]
        if tiles == 1:
            return pl.BlockSpec((length, columns), lambda step: (0, 0))
        low, count = starts[place] // tile, columns // tile
        return pl.BlockSpec((length, tile), lambda step: (0, jnp.clip(step - low, 0, count - 1)))

    half = line // 2
    cut, parts = {"line": ((half, 4), 2), "halves": ((half, 2), 4)}.get(form, ((line, 2), 2))
    out = jax.ShapeDtypeStruct((*cut, rows, width), jnp.bfloat16)
    out_spec = pl.BlockSpec((*cut, rows, tile), lambda step: (0, 0, 0, step))
    size = depth * width * 2 + sum(l.size * 2 for l in lefts) + sum(r.size * 2 for _, r in pairs)
    return pl.pallas_call(
        body,
        grid=(tiles,),
        in_specs=[pl.BlockSpec((depth, length), lambda step: (0, 0))] * len(lefts)
        + [right_spec(place) for place in range(len(pairs))]
        + ([] if extra is None else [pl.BlockSpec(extra.shape, lambda step: (0, 0))]),
        out_specs=[out_spec] * parts,
        out_shape=[out] * parts,
        scratch_shapes=[pltpu.VMEM((depth, tile), jnp.float32)],
        cost_estimate=small_cost(2 * depth * length * width, size),
        compiler_params=pltpu.CompilerParams(vmem_limit_bytes=VMEM_LIMIT),
    )(*lefts, *[right for _, right in pairs], *([] if extra is None else [extra]))


def pick(array, axis, place):
    return lax.dynamic_index_in_dim(array, place, axis, keepdims=False)


def cut_parts(grid, array, form):
    line, rows = grid.count // 4, array.shape[0] // grid.count
    blocks = array.reshape(line, 2, 2, rows, array.shape[1])

    def cut(blocks, number):
        here, axis = grid.bit(number), 2 - number
        return pick(blocks, axis, 1 - here), pick(blocks, axis, here)

    if form in (0, 1):
        return cut(blocks, form)
    if form == "line":
        here, whole = grid.bit(2), array.reshape(line // 2, 2, 4, rows, array.shape[1])
        return pick(whole, 1, 1 - here), pick(whole, 1, here)
    low, high = cut(blocks[: line // 2], 1), cut(blocks[line // 2 :], 0)
    return low[0], high[0], low[1], high[1]


def weight_gradient(grid, pairs, tiles, form, extra=None):
    rows = pairs[0][0].shape[0] // grid.count
    if rows % 16 == 0:
        parts = gradient_parts(grid, pairs, tiles, form, extra)
    else:
        found = [matmul(left, right) for left, right in pairs]
        if extra is not None:
            found[-1] = found[-1] + extra
        parts = cut_parts(grid, lower(jnp.concatenate(found, axis=1)), form)
    return BitSum(grid, parts) if form == "line" else PlaneSum(grid, parts, form)


def add_halves(terms, number):
    count, _, rows, columns = terms[0].shape
    tile = next(t for t in (512, 384, 256, 128, columns) if columns % t == 0)

    def body(*refs):
        inputs, (away, kept) = refs[: len(terms)], refs[len(terms) :]
        side = (lax.axis_index("dp") >> number) & 1
        for place in range(count):
            away[place] = lower(sum(wide(ref[place, 1 - side]) for ref in inputs))
            kept[place] = lower(sum(wide(ref[place, side]) for ref in inputs))

    block = pl.BlockSpec((count, 2, rows, tile), lambda step: (0, 0, 0, step))
    half = pl.BlockSpec((count, rows, tile), lambda step: (0, 0, step))
    size = terms[0].size * (2 * len(terms) + 2)
    return pl.pallas_call(
        body,
        grid=(columns // tile,),
        in_specs=[block] * len(terms),
        out_specs=[half] * 2,
        out_shape=[jax.ShapeDtypeStruct((count, rows, columns), jnp.bfloat16)] * 2,
        cost_estimate=small_cost(0, size),
        compiler_params=pltpu.CompilerParams(vmem_limit_bytes=VMEM_LIMIT),
    )(*terms)


def add_joined(packs, number):
    rows = packs[0][0][0].shape[2]
    widths = [pack[0][0].shape[3] for pack in packs]
    count = sum(group[0].shape[0] for group in packs[0])
    flat = [term for pack in packs for group in pack for term in group]

    def body(*refs):
        inputs, (away, kept) = list(refs[: len(flat)]), refs[len(flat) :]
        side = (lax.axis_index("dp") >> number) & 1
        start = 0
        for pack, width in zip(packs, widths):
            place = 0
            for group in pack:
                terms = [inputs.pop(0) for _ in group]
                for row in range(group[0].shape[0]):
                    other = sum(wide(term[row, 1 - side]) for term in terms)
                    own = sum(wide(term[row, side]) for term in terms)
                    away[place, :, start : start + width] = lower(other)
                    kept[place, :, start : start + width] = lower(own)
                    place += 1
            start += width

    out = jax.ShapeDtypeStruct((count, rows, sum(widths)), jnp.bfloat16)
    return pl.pallas_call(
        body,
        out_shape=[out] * 2,
        cost_estimate=small_cost(0, 2 * sum(term.size for term in flat)),
        compiler_params=pltpu.CompilerParams(vmem_limit_bytes=VMEM_LIMIT),
    )(*flat)


def joined_rows(own, others, in_sequence):
    rows, columns = own.shape
    tile, run = columns // 4, 4 // len(others)

    def body(own_ref, *refs):
        other_refs, (rows_ref, turned_ref) = refs[: len(others)], refs[len(others) :]
        first, second = own_ref[...], other_refs[0][...]
        for number in range(1, len(others)):
            later = pl.program_id(0) >= number * run
            second = jnp.where(later, other_refs[number][...], second)
        if in_sequence:
            ahead = lax.axis_index("tensor") == 0
            first, second = jnp.where(ahead, first, second), jnp.where(ahead, second, first)
        rows_ref[:rows] = first
        rows_ref[rows:] = second
        turned_ref[:, :rows] = first.T
        turned_ref[:, rows:] = second.T

    def part_spec(number):
        return pl.BlockSpec(
            (rows, tile), lambda step: (0, jnp.clip(step - number * run, 0, run - 1))
        )

    return pl.pallas_call(
        body,
        grid=(4,),
        in_specs=[pl.BlockSpec((rows, tile), lambda step: (0, step))]
        + [part_spec(number) for number in range(len(others))],
        out_specs=[
            pl.BlockSpec((2 * rows, tile), lambda step: (0, step)),
            pl.BlockSpec((tile, 2 * rows), lambda step: (step, 0)),
        ],
        out_shape=[
            jax.ShapeDtypeStruct((2 * rows, columns), own.dtype),
            jax.ShapeDtypeStruct((columns, 2 * rows), own.dtype),
        ],
        cost_estimate=small_cost(0, 12 * rows * columns),
        compiler_params=pltpu.CompilerParams(vmem_limit_bytes=VMEM_LIMIT),
    )(own, *others)


def row_kernel(body, inputs, outs, sums=0):
    length, columns = inputs[0].shape
    tile = length // 4

    def spec(rows, width):
        if rows == 1:
            return pl.BlockSpec((1, width), lambda step: (0, 0))
        return pl.BlockSpec((tile, width), lambda step: (step, 0))

    def kernel(*refs):
        found = body(*[ref[...] for ref in refs[: len(inputs)]])
        out_refs = refs[len(inputs) :]
        for ref, value in zip(out_refs[: len(outs)], found):
            ref[...] = value
        for ref, value in zip(out_refs[len(outs) :], found[len(outs) :]):

            @pl.when(pl.program_id(0) == 0)
            def _():
                ref[...] = jnp.zeros_like(ref)

            ref[...] += value

    size = length * columns * (sum(i.dtype.itemsize for i in inputs) + 4 * len(outs))
    return pl.pallas_call(
        kernel,
        grid=(4,),
        in_specs=[spec(*i.shape) for i in inputs],
        out_specs=[spec(length, width) for width, _ in outs] + [spec(1, columns)] * sums,
        out_shape=[jax.ShapeDtypeStruct((length, width), kind) for width, kind in outs]
        + [jax.ShapeDtypeStruct((1, columns), jnp.float32)] * sums,
        cost_estimate=small_cost(0, size),
        compiler_params=pltpu.CompilerParams(vmem_limit_bytes=VMEM_LIMIT),
    )(*inputs)


def halves(values):
    half = values.shape[1] // 2
    return values, values[:, :half], values[:, half:]


def both_parts(first, second):
    return wide(jnp.concatenate([first, second], axis=1))


def norm_forward(residual, own, first, second, gain):
    middle = wide(residual) + (own + both_parts(first, second))
    unit, _ = statistics(middle)
    return middle, *halves(lower(unit * gain))


def norm_gradient(source, own, first, second, base, gain):
    unit, inverse = statistics(wide(source))
    grad = own + both_parts(first, second)
    total = wide(base) + norm_backward(unit, inverse, gain, grad)
    return total, lower(total)


def norm_gradient_halves(*values):
    total, rounded = norm_gradient(*values)
    return total, *halves(rounded)


class PlaneSum:
    def __init__(self, grid, parts, form):
        half = len(parts) // 2
        self.grid, self.sent, self.own = grid, tuple(parts[:half]), tuple(parts[half:])
        self.numbers = (form,) if form in (0, 1) else (1, 0)

    def start(self, *after):
        swaps = zip(self.sent, self.numbers)
        self.got = [self.grid.swap(tie(sent, *after), number) for sent, number in swaps]
        return self

    def second(self, *after):
        sent, self.groups = [], []
        for own, got, number in zip(self.own, self.got, self.numbers):
            away, kept = add_halves([own, tie(got, *after)], 1 - number)
            sent.append(away)
            self.groups.append([kept, self.grid.swap(away, 1 - number)])
        self.sent = tuple(sent)
        return self


class BitSum:
    def __init__(self, grid, parts):
        self.grid, self.sent, self.kept = grid, *parts

    def start(self, *after):
        self.got = self.grid.swap(tie(self.sent, *after), 2)
        return self

    def step(self, number, *after):
        def cut(array):
            rows, columns = array.shape[-2:]
            count = array.size // (rows * columns)
            if number >= 2:
                count, rows = count // 4, rows * 4
            else:
                count = 1
                rows = array.size // (2 * columns)
            return array.reshape(count if number < 2 else count // 2, 2, rows, columns)

        self.sent, self.kept = add_halves([cut(self.kept), cut(tie(self.got, *after))], number)
        self.got = self.grid.swap(self.sent, number)
        if number >= 2:
            shape = (self.sent.shape[0], 4, self.sent.shape[1] // 4, self.sent.shape[2])
            self.kept, self.got = self.kept.reshape(shape), self.got.reshape(shape)
        return self

    def line(self, *after):
        for number in self.grid.line_bits[1:]:
            self.step(number, *after)
        return self

    def result(self):
        return wide(self.kept[0]) + wide(self.got[0])


class LineSum:
    def __init__(self, grid, sums):
        self.grid, self.packs = grid, [found.groups for found in sums]

    def step(self, number, after):
        packs = [
            [
                [t.reshape((t.shape[0] // 2, 2) + t.shape[1:]) for t in (*kept, tie(got, *after))]
                for *kept, got in groups
            ]
            for groups in self.packs
        ]
        self.sent, kept = add_joined(packs, number)
        self.packs = [[[kept, self.grid.swap(self.sent, number)]]]
        return self

    def third(self, *after):
        return self.step(self.grid.line_bits[0], after)

    def fourth(self, *after):
        for number in self.grid.line_bits[1:]:
            self.step(number, after)
        return self

    def result(self):
        return sum(wide(term[0]) for term in self.packs[0][0])


def running_sum(values, reverse):
    length = values.shape[1]
    place = lax.broadcasted_iota(jnp.int32, values.shape, 1)
    shift = 1
    while shift < length:
        if reverse:
            moved = jnp.where(place < length - shift, pltpu.roll(values, length - shift, 1), 0.0)
        else:
            moved = jnp.where(place >= shift, pltpu.roll(values, shift, 1), 0.0)
        values = values + moved
        shift *= 2
    return values


def decay_kernel(heads, logit_ref, bias_ref, row_ref, column_ref):
    length, lanes = logit_ref.shape
    groups, per, _ = row_ref.shape
    padded = -(-heads // 8) * 8
    logit = (logit_ref[...] + bias_ref[...]).T[:padded]
    decay = running_sum(-jnp.log1p(jnp.exp(-logit)), False)
    columns = jnp.concatenate([decay, jnp.zeros((lanes - padded, length), jnp.float32)], axis=0).T
    for group in range(groups):
        row_ref[group] = decay[group * per : (group + 1) * per]
        column_ref[group] = columns[:, group * per : (group + 1) * per]


def decays(logit, bias, heads, per):
    length = logit.shape[0]
    groups = heads // per
    return pl.pallas_call(
        functools.partial(decay_kernel, heads),
        out_shape=[
            jax.ShapeDtypeStruct((groups, per, length), jnp.float32),
            jax.ShapeDtypeStruct((groups, length, per), jnp.float32),
        ],
        compiler_params=pltpu.CompilerParams(vmem_limit_bytes=VMEM_LIMIT),
    )(logit, bias)


def forget_kernel(heads, row_ref, column_ref, logit_ref, bias_ref, grad_ref, sum_ref):
    length, lanes = logit_ref.shape
    groups, per, _ = row_ref.shape
    padded = -(-heads // 8) * 8
    rows = [row_ref[group] for group in range(groups)]
    columns = [column_ref[group] for group in range(groups)]
    columns = jnp.concatenate(
        columns + [jnp.zeros((length, lanes - heads), jnp.float32)], axis=1
    ).T[:padded]
    if padded > heads:
        rows = rows + [jnp.zeros((padded - heads, length), jnp.float32)]
    grad_log = running_sum(jnp.concatenate(rows, axis=0) - columns, True)
    grad_log = jnp.concatenate([grad_log, jnp.zeros((lanes - padded, length), jnp.float32)], axis=0).T
    grad = lower(grad_log * jax.nn.sigmoid(-(logit_ref[...] + bias_ref[...])))
    lane = lax.broadcasted_iota(jnp.int32, grad.shape, 1)
    grad = jnp.where(lane < heads, grad, jnp.bfloat16(0))
    grad_ref[...] = grad
    sum_ref[...] = jnp.sum(wide(grad), axis=0, keepdims=True)


def forget_backward(row, column, logit, bias, heads):
    return pl.pallas_call(
        functools.partial(forget_kernel, heads),
        out_shape=[
            jax.ShapeDtypeStruct(logit.shape, jnp.bfloat16),
            jax.ShapeDtypeStruct(bias.shape, jnp.float32),
        ],
        compiler_params=pltpu.CompilerParams(vmem_limit_bytes=VMEM_LIMIT),
    )(row, column, logit, bias)


def fwd_kernel(scale, head, q_ref, k_ref, v_ref, col_ref, row_ref, o_ref, lse_ref, out_t):
    length, lanes = q_ref.shape
    span = min(256, length)
    lane = lax.broadcasted_iota(jnp.int32, (span, lanes), 1) // head
    below = lax.broadcasted_iota(jnp.int32, (span, span), 0) <= lax.broadcasted_iota(jnp.int32, (span, span), 1)
    v_t = v_ref[...].T
    for h in range(lanes // head):
        for b in range(length // span):
            lo, hi = b * span, (b + 1) * span
            q = jnp.where(lane == h, q_ref[lo:hi, :] * scale, 0).astype(jnp.bfloat16)
            row = row_ref[0, h:h+1, lo:hi]
            diag = second_contract(k_ref[lo:hi, :], q) + row - col_ref[0, lo:hi, h:h+1]
            diag = jnp.where(below, diag, -1e30)
            top = jnp.max(diag, axis=0, keepdims=True)
            if lo:
                off = second_contract(k_ref[:lo, :], q) + row - col_ref[0, :lo, h:h+1]
                top = jnp.maximum(top, jnp.max(off, axis=0, keepdims=True))
            e = jnp.exp(diag - top)
            total = jnp.sum(e, axis=0, keepdims=True)
            v_h = v_t[h*head:(h+1)*head]
            acc = matmul(v_h[:, lo:hi], lower(e))
            if lo:
                e = jnp.exp(off - top)
                total = total + jnp.sum(e, axis=0, keepdims=True)
                acc = acc + matmul(v_h[:, :lo], lower(e))
            out_t[h*head:(h+1)*head, lo:hi] = acc / total
            lse_ref[0, h:h+1, lo:hi] = top + jnp.log(total)
    o_ref[...] = out_t[...].T

def bwd_kernel(scale, head, q_ref, k_ref, v_ref, do_ref, col_ref, row_ref, lse_ref, dq_ref, dk_ref, dv_ref, drow_ref, dcol_ref, dq_t, dk_acc, dv_acc):
    length, lanes = q_ref.shape
    span = min(256, length)
    heads = lanes // head
    lane = lax.broadcasted_iota(jnp.int32, (span, lanes), 1) // head
    sub = lax.broadcasted_iota(jnp.int32, (lanes, length), 0) // head
    below = lax.broadcasted_iota(jnp.int32, (span, span), 0) <= lax.broadcasted_iota(jnp.int32, (span, span), 1)
    k_t = k_ref[...].T
    one = jnp.bfloat16(1)
    for h in range(heads):
        kt_h = jnp.where(sub == h, k_t, one)
        mine = lane == h
        for b in range(length // span):
            lo, hi = b * span, (b + 1) * span
            q = q_ref[lo:hi, :] * jnp.bfloat16(scale)
            qz = jnp.where(mine, q, jnp.bfloat16(0))
            q1 = jnp.where(mine, q, one)
            do = do_ref[lo:hi, :]
            doz = jnp.where(mine, do, jnp.bfloat16(0))
            row = row_ref[0, h:h+1, lo:hi] - lse_ref[0, h:h+1, lo:hi]
            s = second_contract(k_ref[lo:hi, :], qz) + row - col_ref[0, lo:hi, h:h+1]
            p = jnp.exp(jnp.where(below, s, -1e30))
            dp = second_contract(v_ref[lo:hi, :], doz)
            centre = jnp.sum(p * dp, axis=0, keepdims=True)
            if lo:
                s0 = second_contract(k_ref[:lo, :], qz) + row - col_ref[0, :lo, h:h+1]
                p0 = jnp.exp(s0)
                dp0 = second_contract(v_ref[:lo, :], doz)
                centre = centre + jnp.sum(p0 * dp0, axis=0, keepdims=True)
            ds = lower(p * (dp - centre))
            dqt = matmul(kt_h[:, lo:hi], ds)
            dv_acc[h, lo:hi, :] = matmul(lower(p), do)
            dk_acc[h, lo:hi, :] = matmul(ds, q1)
            if lo:
                ds0 = lower(p0 * (dp0 - centre))
                dqt = dqt + matmul(kt_h[:, :lo], ds0)
                dv_acc[h, :lo, :] = dv_acc[h, :lo, :] + matmul(lower(p0), do)
                dk_acc[h, :lo, :] = dk_acc[h, :lo, :] + matmul(ds0, q1)
            dq_t[h*head:(h+1)*head, lo:hi] = dqt[h*head:(h+1)*head] * scale
            other = ((h + 1) % heads) * head
            drow_ref[0, h:h+1, lo:hi] = dqt[other:other+1]
    lane_all = lax.broadcasted_iota(jnp.int32, (length, lanes), 1) // head
    dk, dv = dk_acc[0], dv_acc[0]
    for h in range(1, heads):
        dk = jnp.where(lane_all == h, dk_acc[h], dk)
        dv = jnp.where(lane_all == h, dv_acc[h], dv)
    for h in range(heads):
        other = ((h + 1) % heads) * head
        dcol_ref[0, :, h:h+1] = dk_acc[h][:, other:other+1]
    dq_ref[...] = lower(dq_t[...].T)
    dk_ref[...] = lower(dk)
    dv_ref[...] = lower(dv)


def pair_specs(length, groups, per):
    def block(offset):
        return pl.BlockSpec((length, LANES), lambda group: (0, group + offset))

    column = pl.BlockSpec((1, length, per), lambda group: (group, 0, 0))
    row = pl.BlockSpec((1, per, length), lambda group: (group, 0, 0))
    return block, column, row


def attention_cost(length, width, head, products):
    return small_cost(products * 6 * length * length * width, 16 * length * width)


def attend(qk, values, column, row, head):
    length, width = values.shape[0], qk.shape[1] // 2
    groups, per, _ = row.shape
    block, column_spec, row_spec = pair_specs(length, groups, per)
    return pl.pallas_call(
        functools.partial(fwd_kernel, head**-0.5, head),
        grid=(groups,),
        in_specs=[block(0), block(groups), block(0), column_spec, row_spec],
        out_specs=[block(0), row_spec],
        out_shape=[
            jax.ShapeDtypeStruct((length, width), jnp.float32),
            jax.ShapeDtypeStruct(row.shape, jnp.float32),
        ],
        scratch_shapes=[pltpu.VMEM((LANES, length), jnp.float32)],
        cost_estimate=attention_cost(length, width, head, 2),
        compiler_params=pltpu.CompilerParams(vmem_limit_bytes=VMEM_LIMIT),
    )(qk, qk, values, column, row)


def attend_backward(qk, values, grad, column, row, logsum, head):
    length, width = values.shape[0], qk.shape[1] // 2
    groups, per, _ = row.shape
    block, column_spec, row_spec = pair_specs(length, groups, per)
    wide_out = jax.ShapeDtypeStruct((length, width), jnp.bfloat16)
    return pl.pallas_call(
        functools.partial(bwd_kernel, head**-0.5, head),
        grid=(groups,),
        in_specs=[block(0), block(groups), block(0), block(0), column_spec, row_spec, row_spec],
        out_specs=[block(0), block(0), block(0), row_spec, column_spec],
        out_shape=[
            wide_out,
            wide_out,
            wide_out,
            jax.ShapeDtypeStruct(row.shape, jnp.float32),
            jax.ShapeDtypeStruct(column.shape, jnp.float32),
        ],
        scratch_shapes=[
            pltpu.VMEM((LANES, length), jnp.float32),
            pltpu.VMEM((per, length, LANES), jnp.float32),
            pltpu.VMEM((per, length, LANES), jnp.float32),
        ],
        cost_estimate=attention_cost(length, width, head, 5),
        compiler_params=pltpu.CompilerParams(vmem_limit_bytes=VMEM_LIMIT),
    )(qk, qk, values, grad, column, row, logsum)


def per_device(
    tokens,
    w_query,
    w_key,
    w_value,
    w_gate_attn,
    w_forget,
    forget_bias,
    w_out,
    norm_attn,
    norm_mlp,
    w_gate,
    w_up,
    w_down,
    cotangent,
):
    grid = Grid()
    side = lax.axis_index("tensor")
    heads_here = forget_bias.shape[0]
    width = w_query.shape[1]
    head_size = width // heads_here
    hidden_here = w_gate.shape[1]
    scale = head_size ** (-0.5)
    rows_here = tokens.shape[0]

    load_qk = Gather(grid, jnp.concatenate([lower(w_query), lower(w_key)], axis=1))
    own_gains = jnp.stack([norm_attn, norm_mlp])
    other_gains = partner(own_gains)
    gains = jnp.where(
        side == 0,
        jnp.concatenate([own_gains, other_gains], axis=1),
        jnp.concatenate([other_gains, own_gains], axis=1),
    )[None]
    pair_gains, gain_codes = gains[0], [0]
    for number in range(len(grid.line_bits) + 2):
        gains = jnp.concatenate([gains, grid.swap(gains, number)], axis=0)
        gain_codes = gain_codes + [code ^ (1 << number) for code in gain_codes]
        if number == 1:
            load_qk.line_end(gains)
    (all_gains,) = grid.place([(gain_codes, gains)], [gains.shape[2]])
    all_gains = all_gains.reshape(grid.count, 2, all_gains.shape[1])
    gain_attn = all_gains[:, 0].reshape(-1)
    gain_mlp = all_gains[:, 1].reshape(-1)
    load_qk.plane(fine=True)
    other_cotangent = partner(tie(cotangent, gains))

    padding = jnp.zeros((w_forget.shape[0], LANES - heads_here), jnp.bfloat16)
    forget_lanes = jnp.concatenate([lower(w_forget), padding], axis=1)
    load_vf = Gather(
        grid, jnp.concatenate([lower(w_value), forget_lanes], axis=1), load_qk.far, gains
    )
    load_vf.line_end(*load_qk.corner_parts).plane(*load_qk.corners)
    load_go = Gather(
        grid, jnp.concatenate([lower(w_gate_attn), lower(w_out).T], axis=1), load_vf.far
    )
    load_go.line_end(load_vf.block)
    gain_attn, gain_mlp = gain_attn[None], gain_mlp[None]
    low = jnp.bfloat16
    columns = tokens.shape[1]
    rounded_outs = [(columns, low), (columns // 2, low), (columns // 2, low)]

    def exchanged(parts):
        return [partner(part) for part in parts]

    own_attn, *sent = row_kernel(
        lambda rows, gain: halves(lower(statistics(wide(rows))[0] * gain)),
        [tokens, gain_attn],
        rounded_outs,
    )
    normed_attn, normed_attn_t = joined_rows(own_attn, exchanged(sent), True)
    grad_output, grad_output_t = joined_rows(cotangent, [other_cotangent], False)

    load_go.plane(*load_vf.corners, normed_attn)
    load_gate = Gather(grid, lower(w_gate), load_go.far).line_end(load_go.block)
    load_up = Gather(grid, lower(w_up), load_gate.far, load_go.corners[0])
    value_w, forget_w = load_vf.weight.part(0, width), load_vf.weight.part(width, LANES)
    query_w, key_w = load_qk.weight.part(0, width), load_qk.weight.part(width, width)
    gate_w, out_w = load_go.weight.part(0, width), load_go.weight.part(width, width)

    (qk,) = multiply(
        normed_attn, load_qk.weight, 3, lambda p: (lower(p),), [], [(2 * width, low)]
    )
    values_all, forget_logit = multiply(
        normed_attn,
        load_vf.weight,
        1,
        lambda p: (lower(p[:, :width]), p[:, width:]),
        [],
        [(width, low), (LANES, jnp.float32)],
    )
    bias_lanes = jnp.pad(forget_bias, (0, LANES - heads_here))[None]
    decay_row, decay_column = decays(forget_logit, bias_lanes, heads_here, LANES // head_size)
    load_gate.plane(*load_go.corners, qk, to_end=False)
    load_up.line_end(load_gate.block, decay_row, values_all)
    qk = tie(qk, load_gate.block)
    attended, logsum = attend(qk, values_all, decay_column, decay_row, head_size)
    load_gate.plane_end(attended)
    load_up.plane(*load_gate.corners)
    load_down = Gather(grid, lower(w_down).T, load_up.far, load_gate.corners[0])
    load_down.line_end(load_up.block)
    mlp_gate, mlp_up = load_gate.weight, load_up.weight

    def gate_output(product, attended):
        sigmoid = jax.nn.sigmoid(product)
        return sigmoid, lower(attended * sigmoid)

    gate_sig, gated = multiply(
        normed_attn, gate_w, 2, gate_output, [attended], [(width, jnp.float32), (width, low)]
    )
    arrived = exchanged(multiply_back([(gated, out_w)], 1 - side, low, 2))
    (own_part,) = multiply_back([(gated, out_w)], side)
    middle, own_normed, *sent = row_kernel(
        norm_forward,
        [tokens, own_part, *arrived, gain_mlp],
        [(columns, jnp.float32)] + rounded_outs,
    )
    normed_mlp, normed_mlp_t = joined_rows(own_normed, exchanged(sent), False)
    (gate_act,) = multiply(
        normed_mlp, mlp_gate, 4, lambda p: (lower(p),), [], [(hidden_here, low)]
    )

    load_down.plane(*load_up.corners, gate_act, to_end=False)

    def hidden_units(up, gate):
        gate = wide(gate)
        return lower(up), lower(gate * jax.nn.sigmoid(gate) * up)

    up_act, hidden = multiply(
        normed_mlp, mlp_up, 4, hidden_units, [gate_act], [(hidden_here, low)] * 2
    )
    sum_down = weight_gradient(grid, [(grad_output_t, hidden)], 4, "line").start()
    mlp_down = load_down.plane_end(sum_down.sent).weight

    def hidden_backward(grad, gate, up):
        gate, up = wide(gate), wide(up)
        sigmoid = jax.nn.sigmoid(gate)
        return (
            lower(grad * (gate * sigmoid)),
            lower(grad * up * sigmoid * (1.0 + gate * (1.0 - sigmoid))),
        )

    grad_up, grad_gate = multiply(
        tie(grad_output, sum_down.sent),
        mlp_down,
        4,
        hidden_backward,
        [gate_act, up_act],
        [(hidden_here, low)] * 2,
    )
    sum_up = weight_gradient(grid, [(normed_mlp_t, grad_up)], 4, 0)
    sum_up.start()
    grad_gate = tie(grad_gate, *sum_up.sent)
    sum_gate = weight_gradient(grid, [(normed_mlp_t, grad_gate)], 4, 1).start()
    grad_gate = tie(grad_gate, *sum_gate.sent)
    back = [(grad_gate, mlp_gate), (grad_up, mlp_up)]
    arrived = exchanged(multiply_back(back, jnp.int32(1), low, 2))
    (own_part,) = multiply_back(back, jnp.int32(0))
    sum_down.line(own_part)
    own_part = tie(own_part, sum_down.sent)
    grad_middle, own_branch, *sent = row_kernel(
        norm_gradient_halves,
        [middle, own_part, *arrived, cotangent, gain_mlp],
        [(columns, jnp.float32)] + rounded_outs,
    )
    other_branch = exchanged(sent)
    grad_branch, grad_branch_t = joined_rows(own_branch, other_branch, True)

    def gate_backward(grad, sigmoid, attended):
        return lower(grad * sigmoid), lower(grad * attended * sigmoid * (1.0 - sigmoid))

    grad_attended, grad_gate_logit = multiply(
        grad_branch,
        out_w,
        2,
        gate_backward,
        [gate_sig, attended],
        [(width, low)] * 2,
    )
    sum_up.second(grad_attended)
    sum_gate.second(grad_attended)
    grad_gate_logit = tie(grad_gate_logit, *sum_up.sent, *sum_gate.sent)
    sum_go = weight_gradient(
        grid, [(normed_attn_t, grad_gate_logit), (grad_branch_t, gated)], 4, "halves"
    ).start()
    grad_attended = tie(grad_attended, *sum_go.sent)
    grad_queries, grad_keys, grad_values, row_total, column_total = attend_backward(
        qk, values_all, grad_attended, decay_column, decay_row, logsum, head_size
    )
    line_mlp = LineSum(grid, [sum_gate, sum_up]).third(grad_queries)
    sum_down.step(1, grad_queries)
    grad_queries = tie(grad_queries, line_mlp.sent, sum_down.sent)
    sum_qk = weight_gradient(
        grid, [(normed_attn_t, grad_queries), (normed_attn_t, grad_keys)], 4, "halves"
    )
    sum_qk.start()
    sum_go.second(*sum_qk.sent)
    grad_forget, bias_part = forget_backward(
        row_total, column_total, forget_logit, bias_lanes, heads_here
    )
    bias_block = jnp.pad(
        bias_part[0, :heads_here, None],
        ((0, w_forget.shape[0] - heads_here), (heads_here, LANES - heads_here - 1)),
    )
    bias_extra = jnp.tile(bias_block, (grid.count, 1))
    grad_values = tie(grad_values, *sum_qk.sent, *sum_go.sent)
    sum_vf = weight_gradient(
        grid,
        [(normed_attn_t, grad_values), (normed_attn_t, grad_forget)],
        1,
        "halves",
        bias_extra,
    )
    back = [
        (tie(grad_gate_logit, *sum_vf.sent), gate_w),
        (grad_queries, query_w),
        (grad_keys, key_w),
        (grad_values, value_w),
        (grad_forget, forget_w),
    ]
    other_part = multiply_back(back, 1 - side, low, 2)
    arrived = exchanged(other_part)
    hidden = tie(hidden, *other_part)
    other_down = multiply_back([(hidden, mlp_down)], jnp.int32(1), low)
    arrived_down = exchanged(other_down)
    sum_qk.second(*other_down)
    line_mlp.fourth(*other_down)
    sum_vf.start(*sum_qk.sent)
    back[1] = (tie(grad_queries, line_mlp.sent, *sum_qk.sent), query_w)
    (own_part,) = multiply_back(back, side)
    line_go = LineSum(grid, [sum_go]).third(own_part)
    own_part = tie(own_part, line_go.sent)
    _, tokens_grad = row_kernel(
        norm_gradient,
        [tokens, own_part, *arrived, grad_middle, gain_attn],
        [(columns, jnp.float32), (columns, low)],
    )
    sum_vf.second(tokens_grad)
    line_qkv = LineSum(grid, [sum_qk, sum_vf]).third()
    line_qkv.fourth()
    (own_down,) = multiply_back([(tie(hidden, line_qkv.sent), mlp_down)], jnp.int32(0))
    (mixed,) = row_kernel(
        lambda middle, own, part: (lower(middle + (own + wide(part))),),
        [middle, own_down, *arrived_down],
        [(columns, low)],
    )
    line_go.fourth(line_qkv.sent)
    sum_down.step(0, line_qkv.sent)
    down_grad, go_grad, qkv_grad = sum_down.result().T, line_go.result(), line_qkv.result()
    mlp_grad = line_mlp.result()

    def gain_gradient(gain, *pairs):
        return sum(jnp.sum(wide(lower(w)) * grad, axis=1) for w, grad in pairs) / gain

    forget_at = 3 * width
    parts = jnp.stack(
        [
            gain_gradient(
                pair_gains[0],
                (w_query, qkv_grad[:, :width]),
                (w_key, qkv_grad[:, width : 2 * width]),
                (w_value, qkv_grad[:, 2 * width : forget_at]),
                (w_forget, qkv_grad[:, forget_at : forget_at + heads_here]),
                (w_gate_attn, go_grad[:, :width]),
            ),
            gain_gradient(
                pair_gains[1], (w_gate, mlp_grad[:, :hidden_here]), (w_up, mlp_grad[:, hidden_here:])
            ),
        ]
    ).reshape(2, 2, norm_attn.shape[0])
    gain_grads = pick(parts, 1, side) + partner(pick(parts, 1, 1 - side))
    return (
        mixed,
        tokens_grad,
        qkv_grad[:, :width],
        qkv_grad[:, width : 2 * width],
        qkv_grad[:, 2 * width : 3 * width],
        go_grad[:, :width],
        qkv_grad[:, 3 * width : 3 * width + heads_here],
        qkv_grad[:heads_here, forget_at + heads_here],
        go_grad[:, width:].T,
        gain_grads[0],
        gain_grads[1],
        mlp_grad[:, :hidden_here],
        mlp_grad[:, hidden_here:],
        down_grad,
    )


def solution(mesh):
    return jax.shard_map(
        per_device,
        mesh=mesh,
        in_specs=(
            P(("dp", "tensor"), None),
            P("dp", "tensor"),
            P("dp", "tensor"),
            P("dp", "tensor"),
            P("dp", "tensor"),
            P("dp", "tensor"),
            P("tensor"),
            P("tensor", "dp"),
            P(("dp", "tensor")),
            P(("dp", "tensor")),
            P("dp", "tensor"),
            P("dp", "tensor"),
            P("tensor", "dp"),
            P(("dp", "tensor"), None),
        ),
        out_specs=(
            P(("dp", "tensor"), None),
            P(("dp", "tensor"), None),
            P("dp", "tensor"),
            P("dp", "tensor"),
            P("dp", "tensor"),
            P("dp", "tensor"),
            P("dp", "tensor"),
            P("tensor"),
            P("tensor", "dp"),
            P(("dp", "tensor")),
            P(("dp", "tensor")),
            P("dp", "tensor"),
            P("dp", "tensor"),
            P("tensor", "dp"),
        ),
        check_vma=False,
    )
```

```python
import functools

import jax
import jax.numpy as jnp
from jax import lax
from jax.experimental import pallas as pl
from jax.experimental.pallas import tpu as pltpu
from jax.sharding import PartitionSpec as P

EPSILON = 1e-06
LANES = 128
VMEM_LIMIT = 50 * 2**20
COST_SCALE = 0.02


def lower(values):
    return values.astype(jnp.bfloat16)


def wide(values):
    return values.astype(jnp.float32)


def matmul(left, right):
    return jnp.dot(left, right, preferred_element_type=jnp.float32)


def first_contract(left, right):
    return lax.dot_general(
        left, right, (((0,), (0,)), ((), ())), preferred_element_type=jnp.float32
    )


def second_contract(left, right):
    return lax.dot_general(
        left, right, (((1,), (1,)), ((), ())), preferred_element_type=jnp.float32
    )


def statistics(values):
    inverse = lax.rsqrt(jnp.mean(values * values, axis=-1, keepdims=True) + EPSILON)
    return (values * inverse, inverse)


def norm_backward(unit, inverse, gain, grad):
    scaled = gain * grad
    return inverse * (scaled - unit * jnp.mean(scaled * unit, axis=-1, keepdims=True))


def partner(values):
    return lax.ppermute(values, "tensor", [(0, 1), (1, 0)])


def tie(value, *others):
    if not others:
        return value
    return lax.optimization_barrier((value, *others))[0]


def small_cost(flops, size):
    return pl.CostEstimate(
        flops=int(COST_SCALE * flops), bytes_accessed=int(COST_SCALE * size), transcendentals=0
    )


class Grid:
    def __init__(self):
        self.count = lax.axis_size("dp")
        self.index = lax.axis_index("dp")
        bits = self.count.bit_length() - 1
        self.line_bits = list(range(2, bits))

    def bit(self, number):
        return (self.index >> number) & 1

    def swap(self, values, number):
        pairs = [(i, i ^ (1 << number)) for i in range(self.count)]
        return lax.ppermute(values, "dp", pairs)

    def place(self, pieces, splits):
        rows = pieces[0][1].shape[1]
        arrays = [piece for _, piece in pieces]
        codes = [code for found, _ in pieces for code in found]
        kind = arrays[0].dtype

        def body(*refs):
            inputs, results, sem = refs[: len(arrays)], refs[len(arrays) : -1], refs[-1]
            here = lax.axis_index("dp")
            copies = []
            for (found, _), ref in zip(pieces, inputs):
                for number, code in enumerate(found):
                    start = 0
                    for width, result in zip(splits, results):
                        copies.append(
                            pltpu.make_async_copy(
                                ref.at[number, :, pl.ds(start, width)],
                                result.at[here ^ code],
                                sem.at[len(copies)],
                            )
                        )
                        start += width
            for copy in copies:
                copy.start()
            for copy in copies:
                copy.wait()

        size = self.count * rows * sum(splits) * kind.itemsize
        results = pl.pallas_call(
            body,
            out_shape=[jax.ShapeDtypeStruct((self.count, rows, w), kind) for w in splits],
            in_specs=[pl.BlockSpec(memory_space=pl.ANY)] * len(arrays),
            out_specs=[pl.BlockSpec(memory_space=pltpu.VMEM)] * len(splits),
            scratch_shapes=[pltpu.SemaphoreType.DMA((len(codes) * len(splits),))],
            compiler_params=pltpu.CompilerParams(vmem_limit_bytes=VMEM_LIMIT),
            cost_estimate=small_cost(0, 2 * size),
        )(*arrays)
        return [r.reshape(self.count * rows, w) for r, w in zip(results, splits)]


class Weight:
    def __init__(self, grid, pieces, first=0, width=None):
        self.grid, self.pieces, self.first = grid, pieces, first
        self.rows = pieces[0][1].shape[1]
        self.width = width or pieces[0][1].shape[2]
        self.in_kernel = self.rows % 16 == 0

    def part(self, first, width):
        return Weight(self.grid, self.pieces, self.first + first, width)

    def arrays(self):
        return [piece for _, piece in self.pieces]

    def assembled(self):
        pieces = [
            (codes, piece[:, :, self.first : self.first + self.width])
            for codes, piece in self.pieces
        ]
        return self.grid.place(pieces, [self.width])[0]

    def copies(self, refs, target, sem, tiles):
        here = lax.axis_index("dp")
        tile = self.width // tiles
        found = []
        for step in range(tiles):
            for (codes, _), ref in zip(self.pieces, refs):
                for number, code in enumerate(codes):
                    block = here ^ code
                    source = ref.at[number, :, pl.ds(self.first + step * tile, tile)]
                    found.append(
                        pltpu.make_async_copy(source, target(step, block), sem.at[step, block])
                    )
        return found


def multiply(left, weight, tiles, epilogue, extras, outs):
    if not weight.in_kernel:
        return epilogue(matmul(left, weight.assembled()), *extras)
    grid, rows = weight.grid, weight.rows
    length, depth = left.shape
    tile = weight.width // tiles
    arrays = weight.arrays()

    def body(*refs):
        left_ref, refs = refs[0], refs[1:]
        piece_refs, refs = refs[: len(arrays)], refs[len(arrays) :]
        extra_refs, refs = refs[: len(extras)], refs[len(extras) :]
        out_refs, (held, sem) = refs[: len(outs)], refs[len(outs) :]
        step = pl.program_id(0)

        def target(place, block):
            return held.at[place, pl.ds(pl.multiple_of(block * rows, 16), rows)]

        @pl.when(step == 0)
        def _():
            for copy in weight.copies(piece_refs, target, sem, tiles):
                copy.start()

        for block in range(grid.count):
            there = target(step, block)
            pltpu.make_async_copy(there, there, sem.at[step, block]).wait()
        results = epilogue(matmul(left_ref[...], held[step]), *[ref[...] for ref in extra_refs])
        for ref, result in zip(out_refs, results):
            ref[...] = result

    def column_block(width):
        return pl.BlockSpec((length, width // tiles), lambda step: (0, step))

    size = (
        left.size * 2
        + depth * weight.width * 2
        + sum(e.size * e.dtype.itemsize for e in extras)
        + sum(length * w * jnp.dtype(kind).itemsize for w, kind in outs)
    )
    return pl.pallas_call(
        body,
        grid=(tiles,),
        in_specs=[pl.BlockSpec((length, depth), lambda step: (0, 0))]
        + [pl.BlockSpec(memory_space=pl.ANY)] * len(arrays)
        + [column_block(extra.shape[1]) for extra in extras],
        out_specs=[column_block(width) for width, _ in outs],
        out_shape=[jax.ShapeDtypeStruct((length, width), kind) for width, kind in outs],
        scratch_shapes=[
            pltpu.VMEM((tiles, depth, tile), jnp.bfloat16),
            pltpu.SemaphoreType.DMA((tiles, grid.count)),
        ],
        cost_estimate=small_cost(2 * length * depth * weight.width, size),
        compiler_params=pltpu.CompilerParams(vmem_limit_bytes=VMEM_LIMIT),
    )(left, *arrays, *extras)


def multiply_back(terms, half, kind=jnp.float32, parts=1, tiles=4):
    grid, rows = terms[0][1].grid, terms[0][1].rows
    length = terms[0][0].shape[0] // 2
    if not terms[0][1].in_kernel:
        total = sum(
            second_contract(
                lax.dynamic_slice_in_dim(left, half * length, length, 0), weight.assembled()
            )
            for left, weight in terms
        )
        return jnp.split(total.astype(kind), parts, axis=1)
    depth = grid.count * rows
    tile, share = depth // tiles, grid.count // tiles
    run = tiles // parts

    def part_spec(number):
        return pl.BlockSpec(
            (length, tile), lambda step, which: (0, jnp.clip(step - number * run, 0, run - 1))
        )

    sources, counts = [], []
    for _, weight in terms:
        sources = sources + weight.arrays()
        counts.append(len(weight.pieces))

    def body(half_ref, *refs):
        left_refs, refs = refs[: len(terms)], refs[len(terms) :]
        piece_refs, refs = refs[: len(sources)], refs[len(sources) :]
        out_refs, refs = refs[:parts], refs[parts:]
        held, sems = refs[: len(terms)], refs[len(terms) :]
        step = pl.program_id(0)

        def target(number):
            def found(_, block):
                return held[number].at[pl.ds(pl.multiple_of(block * rows, 16), rows)]

            return found

        @pl.when(step == 0)
        def _():
            first = 0
            for number, (_, weight) in enumerate(terms):
                mine = piece_refs[first : first + counts[number]]
                first += counts[number]
                for copy in weight.copies(mine, target(number), sems[number], 1):
                    copy.start()

        total = None
        for number in range(len(terms)):
            for part in range(share):
                block = step * share + part
                there = target(number)(0, block)
                pltpu.make_async_copy(there, there, sems[number].at[0, block]).wait()
            found = held[number][pl.ds(pl.multiple_of(step * tile, 16), tile), :]
            product = second_contract(left_refs[number][...], found)
            total = product if total is None else total + product
        for number, out_ref in enumerate(out_refs):

            @pl.when(step // run == number)
            def _():
                out_ref[...] = total.astype(kind)

    size = length * depth * 4 + sum(l.size + depth * w.width * 2 for l, w in terms)
    flops = sum(2 * length * depth * w.width for _, w in terms)
    return pl.pallas_call(
        body,
        grid_spec=pltpu.PrefetchScalarGridSpec(
            num_scalar_prefetch=1,
            grid=(tiles,),
            in_specs=[
                pl.BlockSpec((length, left.shape[1]), lambda step, which: (which[0], 0))
                for left, _ in terms
            ]
            + [pl.BlockSpec(memory_space=pl.ANY)] * len(sources),
            out_specs=[part_spec(number) for number in range(parts)],
            scratch_shapes=[pltpu.VMEM((depth, w.width), jnp.bfloat16) for _, w in terms]
            + [pltpu.SemaphoreType.DMA((1, grid.count)) for _ in terms],
        ),
        out_shape=[jax.ShapeDtypeStruct((length, depth // parts), kind)] * parts,
        cost_estimate=small_cost(flops, size),
        compiler_params=pltpu.CompilerParams(vmem_limit_bytes=VMEM_LIMIT),
    )(jnp.reshape(half, (1,)).astype(jnp.int32), *[left for left, _ in terms], *sources)


class Gather:
    def __init__(self, grid, shard, *after):
        near, codes = tie(shard[None], *after), [0]
        for number in reversed(grid.line_bits[1:]):
            found = grid.swap(near, number)
            near = jnp.concatenate([near, found], axis=0)
            codes = codes + self.moved(codes, 1 << number)
        self.grid, self.near, self.codes = grid, near, codes

    def moved(self, found, plane):
        return [code ^ plane for code in found]

    def line_end(self, *after):
        last = self.grid.line_bits[0]
        self.near = tie(self.near, *after)
        self.far = self.grid.swap(self.near, last)
        self.far_codes = self.moved(self.codes, 1 << last)
        return self

    def plane(self, *after, fine=False, to_end=True):
        grid, near, far, codes, far_codes = (
            self.grid,
            self.near,
            self.far,
            self.codes,
            self.far_codes,
        )
        moved, both, half = self.moved, self.codes + self.far_codes, len(self.codes)
        if fine:
            near_x, near_y = grid.swap(near, 0), grid.swap(near, 1)
            far_x, far_y = grid.swap(far, 0), grid.swap(far, 1)
            sides = [
                (codes, near),
                (far_codes, far),
                (moved(codes, 1), near_x),
                (moved(codes, 2), near_y),
                (moved(far_codes, 1), far_x),
                (moved(far_codes, 2), far_y),
            ]
            received = (near_y, far_x)
        else:
            block = tie(jnp.concatenate([near, far], axis=0), *after)
            side_x, side_y = grid.swap(block, 0), grid.swap(block, 1)
            near_x, far_y = side_x[:half], side_y[half:]
            sides = [(both, block), (moved(both, 1), side_x), (moved(both, 2), side_y)]
            received = ()
            self.block = block
        self.corner_parts, self.received, self.sides = (near_x, far_y), received, sides
        return self.plane_end() if to_end else self

    def plane_end(self, *after):
        grid, codes, far_codes = self.grid, self.codes, self.far_codes
        moved, sides = self.moved, self.sides
        near_x, far_y = [tie(part, *after) for part in self.corner_parts]
        near_corner, far_corner = grid.swap(near_x, 1), grid.swap(far_y, 0)
        self.corners = (near_corner, far_corner, *self.received)
        corners = [(moved(codes, 3), near_corner), (moved(far_codes, 3), far_corner)]
        self.weight = Weight(grid, sides + corners)
        return self


def gradient_parts(grid, pairs, tiles, form, extra=None):
    depth, length = pairs[0][0].shape
    rows, line = depth // grid.count, grid.count // 4
    width = sum(right.shape[1] for _, right in pairs)
    lefts = []
    for left, _ in pairs:
        if not any(left is other for other in lefts):
            lefts.append(left)
    which = [[left is other for other in lefts].index(True) for left, _ in pairs]
    tile = width // tiles
    starts, first = [], 0
    for _, right in pairs:
        starts.append(first)
        first += right.shape[1]

    def body(*refs):
        left_refs, refs = refs[: len(lefts)], refs[len(lefts) :]
        right_refs, refs = refs[: len(pairs)], refs[len(pairs) :]
        if extra is not None:
            extra_ref, refs = refs[0], refs[1:]
        outs, total = refs[:-1], refs[-1]
        step = pl.program_id(0)
        if tiles == 1:
            for place in range(len(pairs)):
                ahead = starts[place]
                total[:, ahead : ahead + pairs[place][1].shape[1]] = matmul(
                    left_refs[which[place]][...], right_refs[place][...]
                )
        elif len(pairs) == 1:
            total[...] = matmul(left_refs[0][...], right_refs[0][...])
        else:
            for place in range(len(pairs)):
                low = starts[place] // tile
                high = low + pairs[place][1].shape[1] // tile

                @pl.when((step >= low) & (step < high))
                def _():
                    total[...] = matmul(left_refs[which[place]][...], right_refs[place][...])

        if extra is not None:
            total[:, tile - extra.shape[1] :] += extra_ref[...]
        index = lax.axis_index("dp")

        def block(place):
            return lower(total[pl.ds(pl.multiple_of(place * rows, 8), rows), :])

        if form == "line":
            here = (index >> 2) & 1
            for place in range(half):
                for plane in range(4):
                    outs[0][place, plane] = block((2 * place + 1 - here) * 4 + plane)
                    outs[1][place, plane] = block((2 * place + here) * 4 + plane)
            return

        for number, first, count, away, own in (
            [(form, 0, line, *outs)]
            if form in (0, 1)
            else [(1, 0, half, outs[0], outs[2]), (0, half, half, outs[1], outs[3])]
        ):
            here = (index >> number) & 1
            for place in range(count):
                for side in range(2):
                    base = (first + place) * 4 + side * (3 - (1 << number))
                    away[place, side] = block(base + ((1 - here) << number))
                    own[place, side] = block(base + (here << number))

    def right_spec(place):
        columns = pairs[place][1].shape[1]
        if tiles == 1:
            return pl.BlockSpec((length, columns), lambda step: (0, 0))
        low, count = starts[place] // tile, columns // tile
        return pl.BlockSpec((length, tile), lambda step: (0, jnp.clip(step - low, 0, count - 1)))

    half = line // 2
    cut, parts = {"line": ((half, 4), 2), "halves": ((half, 2), 4)}.get(form, ((line, 2), 2))
    out = jax.ShapeDtypeStruct((*cut, rows, width), jnp.bfloat16)
    out_spec = pl.BlockSpec((*cut, rows, tile), lambda step: (0, 0, 0, step))
    size = depth * width * 2 + sum(l.size * 2 for l in lefts) + sum(r.size * 2 for _, r in pairs)
    return pl.pallas_call(
        body,
        grid=(tiles,),
        in_specs=[pl.BlockSpec((depth, length), lambda step: (0, 0))] * len(lefts)
        + [right_spec(place) for place in range(len(pairs))]
        + ([] if extra is None else [pl.BlockSpec(extra.shape, lambda step: (0, 0))]),
        out_specs=[out_spec] * parts,
        out_shape=[out] * parts,
        scratch_shapes=[pltpu.VMEM((depth, tile), jnp.float32)],
        cost_estimate=small_cost(2 * depth * length * width, size),
        compiler_params=pltpu.CompilerParams(vmem_limit_bytes=VMEM_LIMIT),
    )(*lefts, *[right for _, right in pairs], *([] if extra is None else [extra]))


def pick(array, axis, place):
    return lax.dynamic_index_in_dim(array, place, axis, keepdims=False)


def cut_parts(grid, array, form):
    line, rows = grid.count // 4, array.shape[0] // grid.count
    blocks = array.reshape(line, 2, 2, rows, array.shape[1])

    def cut(blocks, number):
        here, axis = grid.bit(number), 2 - number
        return pick(blocks, axis, 1 - here), pick(blocks, axis, here)

    if form in (0, 1):
        return cut(blocks, form)
    if form == "line":
        here, whole = grid.bit(2), array.reshape(line // 2, 2, 4, rows, array.shape[1])
        return pick(whole, 1, 1 - here), pick(whole, 1, here)
    low, high = cut(blocks[: line // 2], 1), cut(blocks[line // 2 :], 0)
    return low[0], high[0], low[1], high[1]


def weight_gradient(grid, pairs, tiles, form, extra=None):
    rows = pairs[0][0].shape[0] // grid.count
    if rows % 16 == 0:
        parts = gradient_parts(grid, pairs, tiles, form, extra)
    else:
        found = [matmul(left, right) for left, right in pairs]
        if extra is not None:
            found[-1] = found[-1] + extra
        parts = cut_parts(grid, lower(jnp.concatenate(found, axis=1)), form)
    return BitSum(grid, parts) if form == "line" else PlaneSum(grid, parts, form)


def add_halves(terms, number):
    count, _, rows, columns = terms[0].shape
    tile = next(t for t in (512, 384, 256, 128, columns) if columns % t == 0)

    def body(*refs):
        inputs, (away, kept) = refs[: len(terms)], refs[len(terms) :]
        side = (lax.axis_index("dp") >> number) & 1
        for place in range(count):
            away[place] = lower(sum(wide(ref[place, 1 - side]) for ref in inputs))
            kept[place] = lower(sum(wide(ref[place, side]) for ref in inputs))

    block = pl.BlockSpec((count, 2, rows, tile), lambda step: (0, 0, 0, step))
    half = pl.BlockSpec((count, rows, tile), lambda step: (0, 0, step))
    size = terms[0].size * (2 * len(terms) + 2)
    return pl.pallas_call(
        body,
        grid=(columns // tile,),
        in_specs=[block] * len(terms),
        out_specs=[half] * 2,
        out_shape=[jax.ShapeDtypeStruct((count, rows, columns), jnp.bfloat16)] * 2,
        cost_estimate=small_cost(0, size),
        compiler_params=pltpu.CompilerParams(vmem_limit_bytes=VMEM_LIMIT),
    )(*terms)


def add_joined(packs, number):
    rows = packs[0][0][0].shape[2]
    widths = [pack[0][0].shape[3] for pack in packs]
    count = sum(group[0].shape[0] for group in packs[0])
    flat = [term for pack in packs for group in pack for term in group]

    def body(*refs):
        inputs, (away, kept) = list(refs[: len(flat)]), refs[len(flat) :]
        side = (lax.axis_index("dp") >> number) & 1
        start = 0
        for pack, width in zip(packs, widths):
            place = 0
            for group in pack:
                terms = [inputs.pop(0) for _ in group]
                for row in range(group[0].shape[0]):
                    other = sum(wide(term[row, 1 - side]) for term in terms)
                    own = sum(wide(term[row, side]) for term in terms)
                    away[place, :, start : start + width] = lower(other)
                    kept[place, :, start : start + width] = lower(own)
                    place += 1
            start += width

    out = jax.ShapeDtypeStruct((count, rows, sum(widths)), jnp.bfloat16)
    return pl.pallas_call(
        body,
        out_shape=[out] * 2,
        cost_estimate=small_cost(0, 2 * sum(term.size for term in flat)),
        compiler_params=pltpu.CompilerParams(vmem_limit_bytes=VMEM_LIMIT),
    )(*flat)


def joined_rows(own, others, in_sequence):
    rows, columns = own.shape
    tile, run = columns // 4, 4 // len(others)

    def body(own_ref, *refs):
        other_refs, (rows_ref, turned_ref) = refs[: len(others)], refs[len(others) :]
        first, second = own_ref[...], other_refs[0][...]
        for number in range(1, len(others)):
            later = pl.program_id(0) >= number * run
            second = jnp.where(later, other_refs[number][...], second)
        if in_sequence:
            ahead = lax.axis_index("tensor") == 0
            first, second = jnp.where(ahead, first, second), jnp.where(ahead, second, first)
        rows_ref[:rows] = first
        rows_ref[rows:] = second
        turned_ref[:, :rows] = first.T
        turned_ref[:, rows:] = second.T

    def part_spec(number):
        return pl.BlockSpec(
            (rows, tile), lambda step: (0, jnp.clip(step - number * run, 0, run - 1))
        )

    return pl.pallas_call(
        body,
        grid=(4,),
        in_specs=[pl.BlockSpec((rows, tile), lambda step: (0, step))]
        + [part_spec(number) for number in range(len(others))],
        out_specs=[
            pl.BlockSpec((2 * rows, tile), lambda step: (0, step)),
            pl.BlockSpec((tile, 2 * rows), lambda step: (step, 0)),
        ],
        out_shape=[
            jax.ShapeDtypeStruct((2 * rows, columns), own.dtype),
            jax.ShapeDtypeStruct((columns, 2 * rows), own.dtype),
        ],
        cost_estimate=small_cost(0, 12 * rows * columns),
        compiler_params=pltpu.CompilerParams(vmem_limit_bytes=VMEM_LIMIT),
    )(own, *others)


def row_kernel(body, inputs, outs, sums=0):
    length, columns = inputs[0].shape
    tile = length // 4

    def spec(rows, width):
        if rows == 1:
            return pl.BlockSpec((1, width), lambda step: (0, 0))
        return pl.BlockSpec((tile, width), lambda step: (step, 0))

    def kernel(*refs):
        found = body(*[ref[...] for ref in refs[: len(inputs)]])
        out_refs = refs[len(inputs) :]
        for ref, value in zip(out_refs[: len(outs)], found):
            ref[...] = value
        for ref, value in zip(out_refs[len(outs) :], found[len(outs) :]):

            @pl.when(pl.program_id(0) == 0)
            def _():
                ref[...] = jnp.zeros_like(ref)

            ref[...] += value

    size = length * columns * (sum(i.dtype.itemsize for i in inputs) + 4 * len(outs))
    return pl.pallas_call(
        kernel,
        grid=(4,),
        in_specs=[spec(*i.shape) for i in inputs],
        out_specs=[spec(length, width) for width, _ in outs] + [spec(1, columns)] * sums,
        out_shape=[jax.ShapeDtypeStruct((length, width), kind) for width, kind in outs]
        + [jax.ShapeDtypeStruct((1, columns), jnp.float32)] * sums,
        cost_estimate=small_cost(0, size),
        compiler_params=pltpu.CompilerParams(vmem_limit_bytes=VMEM_LIMIT),
    )(*inputs)


def halves(values):
    half = values.shape[1] // 2
    return values, values[:, :half], values[:, half:]


def both_parts(first, second):
    return wide(jnp.concatenate([first, second], axis=1))


def norm_forward(residual, own, first, second, gain):
    middle = wide(residual) + (own + both_parts(first, second))
    unit, _ = statistics(middle)
    return middle, *halves(lower(unit * gain))


def norm_gradient(source, own, first, second, base, gain):
    unit, inverse = statistics(wide(source))
    grad = own + both_parts(first, second)
    total = wide(base) + norm_backward(unit, inverse, gain, grad)
    return total, lower(total)


def norm_gradient_halves(*values):
    total, rounded = norm_gradient(*values)
    return total, *halves(rounded)


class PlaneSum:
    def __init__(self, grid, parts, form):
        half = len(parts) // 2
        self.grid, self.sent, self.own = grid, tuple(parts[:half]), tuple(parts[half:])
        self.numbers = (form,) if form in (0, 1) else (1, 0)

    def start(self, *after):
        swaps = zip(self.sent, self.numbers)
        self.got = [self.grid.swap(tie(sent, *after), number) for sent, number in swaps]
        return self

    def second(self, *after):
        sent, self.groups = [], []
        for own, got, number in zip(self.own, self.got, self.numbers):
            away, kept = add_halves([own, tie(got, *after)], 1 - number)
            sent.append(away)
            self.groups.append([kept, self.grid.swap(away, 1 - number)])
        self.sent = tuple(sent)
        return self


class BitSum:
    def __init__(self, grid, parts):
        self.grid, self.sent, self.kept = grid, *parts

    def start(self, *after):
        self.got = self.grid.swap(tie(self.sent, *after), 2)
        return self

    def step(self, number, *after):
        def cut(array):
            rows, columns = array.shape[-2:]
            count = array.size // (rows * columns)
            if number >= 2:
                count, rows = count // 4, rows * 4
            else:
                count = 1
                rows = array.size // (2 * columns)
            return array.reshape(count if number < 2 else count // 2, 2, rows, columns)

        self.sent, self.kept = add_halves([cut(self.kept), cut(tie(self.got, *after))], number)
        self.got = self.grid.swap(self.sent, number)
        if number >= 2:
            shape = (self.sent.shape[0], 4, self.sent.shape[1] // 4, self.sent.shape[2])
            self.kept, self.got = self.kept.reshape(shape), self.got.reshape(shape)
        return self

    def line(self, *after):
        for number in self.grid.line_bits[1:]:
            self.step(number, *after)
        return self

    def result(self):
        return wide(self.kept[0]) + wide(self.got[0])


class LineSum:
    def __init__(self, grid, sums):
        self.grid, self.packs = grid, [found.groups for found in sums]

    def step(self, number, after):
        packs = [
            [
                [t.reshape((t.shape[0] // 2, 2) + t.shape[1:]) for t in (*kept, tie(got, *after))]
                for *kept, got in groups
            ]
            for groups in self.packs
        ]
        self.sent, kept = add_joined(packs, number)
        self.packs = [[[kept, self.grid.swap(self.sent, number)]]]
        return self

    def third(self, *after):
        return self.step(self.grid.line_bits[0], after)

    def fourth(self, *after):
        for number in self.grid.line_bits[1:]:
            self.step(number, after)
        return self

    def result(self):
        return sum(wide(term[0]) for term in self.packs[0][0])


def running_sum(values, reverse):
    length = values.shape[1]
    place = lax.broadcasted_iota(jnp.int32, values.shape, 1)
    shift = 1
    while shift < length:
        if reverse:
            moved = jnp.where(place < length - shift, pltpu.roll(values, length - shift, 1), 0.0)
        else:
            moved = jnp.where(place >= shift, pltpu.roll(values, shift, 1), 0.0)
        values = values + moved
        shift *= 2
    return values


def decay_kernel(heads, logit_ref, bias_ref, row_ref, column_ref):
    length, lanes = logit_ref.shape
    groups, per, _ = row_ref.shape
    padded = -(-heads // 8) * 8
    logit = (logit_ref[...] + bias_ref[...]).T[:padded]
    decay = running_sum(-jnp.log1p(jnp.exp(-logit)), False)
    columns = jnp.concatenate([decay, jnp.zeros((lanes - padded, length), jnp.float32)], axis=0).T
    for group in range(groups):
        row_ref[group] = decay[group * per : (group + 1) * per]
        column_ref[group] = columns[:, group * per : (group + 1) * per]


def decays(logit, bias, heads, per):
    length = logit.shape[0]
    groups = heads // per
    return pl.pallas_call(
        functools.partial(decay_kernel, heads),
        out_shape=[
            jax.ShapeDtypeStruct((groups, per, length), jnp.float32),
            jax.ShapeDtypeStruct((groups, length, per), jnp.float32),
        ],
        compiler_params=pltpu.CompilerParams(vmem_limit_bytes=VMEM_LIMIT),
    )(logit, bias)


def forget_kernel(heads, row_ref, column_ref, logit_ref, bias_ref, grad_ref, sum_ref):
    length, lanes = logit_ref.shape
    groups, per, _ = row_ref.shape
    padded = -(-heads // 8) * 8
    rows = [row_ref[group] for group in range(groups)]
    columns = [column_ref[group] for group in range(groups)]
    columns = jnp.concatenate(
        columns + [jnp.zeros((length, lanes - heads), jnp.float32)], axis=1
    ).T[:padded]
    if padded > heads:
        rows = rows + [jnp.zeros((padded - heads, length), jnp.float32)]
    grad_log = running_sum(jnp.concatenate(rows, axis=0) - columns, True)
    grad_log = jnp.concatenate([grad_log, jnp.zeros((lanes - padded, length), jnp.float32)], axis=0).T
    grad = lower(grad_log * jax.nn.sigmoid(-(logit_ref[...] + bias_ref[...])))
    lane = lax.broadcasted_iota(jnp.int32, grad.shape, 1)
    grad = jnp.where(lane < heads, grad, jnp.bfloat16(0))
    grad_ref[...] = grad
    sum_ref[...] = jnp.sum(wide(grad), axis=0, keepdims=True)


def forget_backward(row, column, logit, bias, heads):
    return pl.pallas_call(
        functools.partial(forget_kernel, heads),
        out_shape=[
            jax.ShapeDtypeStruct(logit.shape, jnp.bfloat16),
            jax.ShapeDtypeStruct(bias.shape, jnp.float32),
        ],
        compiler_params=pltpu.CompilerParams(vmem_limit_bytes=VMEM_LIMIT),
    )(row, column, logit, bias)


def fwd_kernel(scale, head, q_ref, k_ref, v_ref, col_ref, row_ref, o_ref, lse_ref, out_t):
    length, lanes = q_ref.shape
    span = min(256, length)
    lane = lax.broadcasted_iota(jnp.int32, (span, lanes), 1) // head
    below = lax.broadcasted_iota(jnp.int32, (span, span), 0) <= lax.broadcasted_iota(jnp.int32, (span, span), 1)
    v_t = v_ref[...].T
    for h in range(lanes // head):
        for b in range(length // span):
            lo, hi = b * span, (b + 1) * span
            q = jnp.where(lane == h, q_ref[lo:hi, :] * scale, 0).astype(jnp.bfloat16)
            row = row_ref[0, h:h+1, lo:hi]
            diag = second_contract(k_ref[lo:hi, :], q) + row - col_ref[0, lo:hi, h:h+1]
            diag = jnp.where(below, diag, -1e30)
            top = jnp.max(diag, axis=0, keepdims=True)
            if lo:
                off = second_contract(k_ref[:lo, :], q) + row - col_ref[0, :lo, h:h+1]
                top = jnp.maximum(top, jnp.max(off, axis=0, keepdims=True))
            e = jnp.exp(diag - top)
            total = jnp.sum(e, axis=0, keepdims=True)
            v_h = v_t[h*head:(h+1)*head]
            acc = matmul(v_h[:, lo:hi], lower(e))
            if lo:
                e = jnp.exp(off - top)
                total = total + jnp.sum(e, axis=0, keepdims=True)
                acc = acc + matmul(v_h[:, :lo], lower(e))
            out_t[h*head:(h+1)*head, lo:hi] = acc / total
            lse_ref[0, h:h+1, lo:hi] = top + jnp.log(total)
    o_ref[...] = out_t[...].T

def bwd_kernel(scale, head, q_ref, k_ref, v_ref, do_ref, col_ref, row_ref, lse_ref, dq_ref, dk_ref, dv_ref, drow_ref, dcol_ref, dq_t, dk_acc, dv_acc):
    length, lanes = q_ref.shape
    span = min(256, length)
    heads = lanes // head
    lane = lax.broadcasted_iota(jnp.int32, (span, lanes), 1) // head
    sub = lax.broadcasted_iota(jnp.int32, (lanes, length), 0) // head
    below = lax.broadcasted_iota(jnp.int32, (span, span), 0) <= lax.broadcasted_iota(jnp.int32, (span, span), 1)
    k_t = k_ref[...].T
    one = jnp.bfloat16(1)
    for h in range(heads):
        kt_h = jnp.where(sub == h, k_t, one)
        mine = lane == h
        for b in range(length // span):
            lo, hi = b * span, (b + 1) * span
            q = q_ref[lo:hi, :] * jnp.bfloat16(scale)
            qz = jnp.where(mine, q, jnp.bfloat16(0))
            q1 = jnp.where(mine, q, one)
            do = do_ref[lo:hi, :]
            doz = jnp.where(mine, do, jnp.bfloat16(0))
            row = row_ref[0, h:h+1, lo:hi] - lse_ref[0, h:h+1, lo:hi]
            s = second_contract(k_ref[lo:hi, :], qz) + row - col_ref[0, lo:hi, h:h+1]
            p = jnp.exp(jnp.where(below, s, -1e30))
            dp = second_contract(v_ref[lo:hi, :], doz)
            centre = jnp.sum(p * dp, axis=0, keepdims=True)
            if lo:
                s0 = second_contract(k_ref[:lo, :], qz) + row - col_ref[0, :lo, h:h+1]
                p0 = jnp.exp(s0)
                dp0 = second_contract(v_ref[:lo, :], doz)
                centre = centre + jnp.sum(p0 * dp0, axis=0, keepdims=True)
            ds = lower(p * (dp - centre))
            dqt = matmul(kt_h[:, lo:hi], ds)
            dv_acc[h, lo:hi, :] = matmul(lower(p), do)
            dk_acc[h, lo:hi, :] = matmul(ds, q1)
            if lo:
                ds0 = lower(p0 * (dp0 - centre))
                dqt = dqt + matmul(kt_h[:, :lo], ds0)
                dv_acc[h, :lo, :] = dv_acc[h, :lo, :] + matmul(lower(p0), do)
                dk_acc[h, :lo, :] = dk_acc[h, :lo, :] + matmul(ds0, q1)
            dq_t[h*head:(h+1)*head, lo:hi] = dqt[h*head:(h+1)*head] * scale
            other = ((h + 1) % heads) * head
            drow_ref[0, h:h+1, lo:hi] = dqt[other:other+1]
    lane_all = lax.broadcasted_iota(jnp.int32, (length, lanes), 1) // head
    dk, dv = dk_acc[0], dv_acc[0]
    for h in range(1, heads):
        dk = jnp.where(lane_all == h, dk_acc[h], dk)
        dv = jnp.where(lane_all == h, dv_acc[h], dv)
    for h in range(heads):
        other = ((h + 1) % heads) * head
        dcol_ref[0, :, h:h+1] = dk_acc[h][:, other:other+1]
    dq_ref[...] = lower(dq_t[...].T)
    dk_ref[...] = lower(dk)
    dv_ref[...] = lower(dv)


def pair_specs(length, groups, per):
    def block(offset):
        return pl.BlockSpec((length, LANES), lambda group: (0, group + offset))

    column = pl.BlockSpec((1, length, per), lambda group: (group, 0, 0))
    row = pl.BlockSpec((1, per, length), lambda group: (group, 0, 0))
    return block, column, row


def attention_cost(length, width, head, products):
    return small_cost(products * 6 * length * length * width, 16 * length * width)


def attend(qk, values, column, row, head):
    length, width = values.shape[0], qk.shape[1] // 2
    groups, per, _ = row.shape
    block, column_spec, row_spec = pair_specs(length, groups, per)
    return pl.pallas_call(
        functools.partial(fwd_kernel, head**-0.5, head),
        grid=(groups,),
        in_specs=[block(0), block(groups), block(0), column_spec, row_spec],
        out_specs=[block(0), row_spec],
        out_shape=[
            jax.ShapeDtypeStruct((length, width), jnp.float32),
            jax.ShapeDtypeStruct(row.shape, jnp.float32),
        ],
        scratch_shapes=[pltpu.VMEM((LANES, length), jnp.float32)],
        cost_estimate=attention_cost(length, width, head, 2),
        compiler_params=pltpu.CompilerParams(vmem_limit_bytes=VMEM_LIMIT),
    )(qk, qk, values, column, row)


def attend_backward(qk, values, grad, column, row, logsum, head):
    length, width = values.shape[0], qk.shape[1] // 2
    groups, per, _ = row.shape
    block, column_spec, row_spec = pair_specs(length, groups, per)
    wide_out = jax.ShapeDtypeStruct((length, width), jnp.bfloat16)
    return pl.pallas_call(
        functools.partial(bwd_kernel, head**-0.5, head),
        grid=(groups,),
        in_specs=[block(0), block(groups), block(0), block(0), column_spec, row_spec, row_spec],
        out_specs=[block(0), block(0), block(0), row_spec, column_spec],
        out_shape=[
            wide_out,
            wide_out,
            wide_out,
            jax.ShapeDtypeStruct(row.shape, jnp.float32),
            jax.ShapeDtypeStruct(column.shape, jnp.float32),
        ],
        scratch_shapes=[
            pltpu.VMEM((LANES, length), jnp.float32),
            pltpu.VMEM((per, length, LANES), jnp.float32),
            pltpu.VMEM((per, length, LANES), jnp.float32),
        ],
        cost_estimate=attention_cost(length, width, head, 5),
        compiler_params=pltpu.CompilerParams(vmem_limit_bytes=VMEM_LIMIT),
    )(qk, qk, values, grad, column, row, logsum)


def per_device(
    tokens,
    w_query,
    w_key,
    w_value,
    w_gate_attn,
    w_forget,
    forget_bias,
    w_out,
    norm_attn,
    norm_mlp,
    w_gate,
    w_up,
    w_down,
    cotangent,
):
    grid = Grid()
    side = lax.axis_index("tensor")
    heads_here = forget_bias.shape[0]
    width = w_query.shape[1]
    head_size = width // heads_here
    hidden_here = w_gate.shape[1]
    scale = head_size ** (-0.5)
    rows_here = tokens.shape[0]

    load_qk = Gather(grid, jnp.concatenate([lower(w_query), lower(w_key)], axis=1))
    own_gains = jnp.stack([norm_attn, norm_mlp])
    other_gains = partner(own_gains)
    gains = jnp.where(
        side == 0,
        jnp.concatenate([own_gains, other_gains], axis=1),
        jnp.concatenate([other_gains, own_gains], axis=1),
    )[None]
    pair_gains, gain_codes = gains[0], [0]
    for number in range(len(grid.line_bits) + 2):
        gains = jnp.concatenate([gains, grid.swap(gains, number)], axis=0)
        gain_codes = gain_codes + [code ^ (1 << number) for code in gain_codes]
        if number == 1:
            load_qk.line_end(gains)
    (all_gains,) = grid.place([(gain_codes, gains)], [gains.shape[2]])
    all_gains = all_gains.reshape(grid.count, 2, all_gains.shape[1])
    gain_attn = all_gains[:, 0].reshape(-1)
    gain_mlp = all_gains[:, 1].reshape(-1)
    load_qk.plane(fine=True)
    other_cotangent = partner(tie(cotangent, gains))

    padding = jnp.zeros((w_forget.shape[0], LANES - heads_here), jnp.bfloat16)
    forget_lanes = jnp.concatenate([lower(w_forget), padding], axis=1)
    load_vf = Gather(
        grid, jnp.concatenate([lower(w_value), forget_lanes], axis=1), load_qk.far, gains
    )
    load_vf.line_end(*load_qk.corner_parts).plane(*load_qk.corners)
    load_go = Gather(
        grid, jnp.concatenate([lower(w_gate_attn), lower(w_out).T], axis=1), load_vf.far
    )
    load_go.line_end(load_vf.block)
    gain_attn, gain_mlp = gain_attn[None], gain_mlp[None]
    low = jnp.bfloat16
    columns = tokens.shape[1]
    rounded_outs = [(columns, low), (columns // 2, low), (columns // 2, low)]

    def exchanged(parts):
        return [partner(part) for part in parts]

    own_attn, *sent = row_kernel(
        lambda rows, gain: halves(lower(statistics(wide(rows))[0] * gain)),
        [tokens, gain_attn],
        rounded_outs,
    )
    normed_attn, normed_attn_t = joined_rows(own_attn, exchanged(sent), True)
    grad_output, grad_output_t = joined_rows(cotangent, [other_cotangent], False)

    load_go.plane(*load_vf.corners, normed_attn)
    load_gate = Gather(grid, lower(w_gate), load_go.far).line_end(load_go.block)
    load_up = Gather(grid, lower(w_up), load_gate.far, load_go.corners[0])
    value_w, forget_w = load_vf.weight.part(0, width), load_vf.weight.part(width, LANES)
    query_w, key_w = load_qk.weight.part(0, width), load_qk.weight.part(width, width)
    gate_w, out_w = load_go.weight.part(0, width), load_go.weight.part(width, width)

    (qk,) = multiply(
        normed_attn, load_qk.weight, 3, lambda p: (lower(p),), [], [(2 * width, low)]
    )
    values_all, forget_logit = multiply(
        normed_attn,
        load_vf.weight,
        1,
        lambda p: (lower(p[:, :width]), p[:, width:]),
        [],
        [(width, low), (LANES, jnp.float32)],
    )
    bias_lanes = jnp.pad(forget_bias, (0, LANES - heads_here))[None]
    decay_row, decay_column = decays(forget_logit, bias_lanes, heads_here, LANES // head_size)
    load_gate.plane(*load_go.corners, qk, to_end=False)
    load_up.line_end(load_gate.block, decay_row, values_all)
    qk = tie(qk, load_gate.block)
    attended, logsum = attend(qk, values_all, decay_column, decay_row, head_size)
    load_gate.plane_end(attended)
    load_up.plane(*load_gate.corners)
    load_down = Gather(grid, lower(w_down).T, load_up.far, load_gate.corners[0])
    load_down.line_end(load_up.block)
    mlp_gate, mlp_up = load_gate.weight, load_up.weight

    def gate_output(product, attended):
        sigmoid = jax.nn.sigmoid(product)
        return sigmoid, lower(attended * sigmoid)

    gate_sig, gated = multiply(
        normed_attn, gate_w, 2, gate_output, [attended], [(width, jnp.float32), (width, low)]
    )
    arrived = exchanged(multiply_back([(gated, out_w)], 1 - side, low, 2))
    (own_part,) = multiply_back([(gated, out_w)], side)
    middle, own_normed, *sent = row_kernel(
        norm_forward,
        [tokens, own_part, *arrived, gain_mlp],
        [(columns, jnp.float32)] + rounded_outs,
    )
    normed_mlp, normed_mlp_t = joined_rows(own_normed, exchanged(sent), False)
    (gate_act,) = multiply(
        normed_mlp, mlp_gate, 4, lambda p: (lower(p),), [], [(hidden_here, low)]
    )

    load_down.plane(*load_up.corners, gate_act, to_end=False)

    def hidden_units(up, gate):
        gate = wide(gate)
        return lower(up), lower(gate * jax.nn.sigmoid(gate) * up)

    up_act, hidden = multiply(
        normed_mlp, mlp_up, 4, hidden_units, [gate_act], [(hidden_here, low)] * 2
    )
    sum_down = weight_gradient(grid, [(grad_output_t, hidden)], 4, "line").start()
    mlp_down = load_down.plane_end(sum_down.sent).weight

    def hidden_backward(grad, gate, up):
        gate, up = wide(gate), wide(up)
        sigmoid = jax.nn.sigmoid(gate)
        return (
            lower(grad * (gate * sigmoid)),
            lower(grad * up * sigmoid * (1.0 + gate * (1.0 - sigmoid))),
        )

    grad_up, grad_gate = multiply(
        tie(grad_output, sum_down.sent),
        mlp_down,
        4,
        hidden_backward,
        [gate_act, up_act],
        [(hidden_here, low)] * 2,
    )
    sum_up = weight_gradient(grid, [(normed_mlp_t, grad_up)], 4, 0)
    sum_up.start()
    grad_gate = tie(grad_gate, *sum_up.sent)
    sum_gate = weight_gradient(grid, [(normed_mlp_t, grad_gate)], 4, 1).start()
    grad_gate = tie(grad_gate, *sum_gate.sent)
    back = [(grad_gate, mlp_gate), (grad_up, mlp_up)]
    arrived = exchanged(multiply_back(back, jnp.int32(1), low, 2))
    (own_part,) = multiply_back(back, jnp.int32(0))
    sum_down.line(own_part)
    own_part = tie(own_part, sum_down.sent)
    grad_middle, own_branch, *sent = row_kernel(
        norm_gradient_halves,
        [middle, own_part, *arrived, cotangent, gain_mlp],
        [(columns, jnp.float32)] + rounded_outs,
    )
    other_branch = exchanged(sent)
    grad_branch, grad_branch_t = joined_rows(own_branch, other_branch, True)

    def gate_backward(grad, sigmoid, attended):
        return lower(grad * sigmoid), lower(grad * attended * sigmoid * (1.0 - sigmoid))

    grad_attended, grad_gate_logit = multiply(
        grad_branch,
        out_w,
        2,
        gate_backward,
        [gate_sig, attended],
        [(width, low)] * 2,
    )
    sum_up.second(grad_attended)
    sum_gate.second(grad_attended)
    grad_gate_logit = tie(grad_gate_logit, *sum_up.sent, *sum_gate.sent)
    sum_go = weight_gradient(
        grid, [(normed_attn_t, grad_gate_logit), (grad_branch_t, gated)], 4, "halves"
    ).start()
    grad_attended = tie(grad_attended, *sum_go.sent)
    grad_queries, grad_keys, grad_values, row_total, column_total = attend_backward(
        qk, values_all, grad_attended, decay_column, decay_row, logsum, head_size
    )
    line_mlp = LineSum(grid, [sum_gate, sum_up]).third(grad_queries)
    sum_down.step(1, grad_queries)
    grad_queries = tie(grad_queries, line_mlp.sent, sum_down.sent)
    sum_qk = weight_gradient(
        grid, [(normed_attn_t, grad_queries), (normed_attn_t, grad_keys)], 4, "halves"
    )
    sum_qk.start()
    sum_go.second(*sum_qk.sent)
    grad_forget, bias_part = forget_backward(
        row_total, column_total, forget_logit, bias_lanes, heads_here
    )
    bias_block = jnp.pad(
        bias_part[0, :heads_here, None],
        ((0, w_forget.shape[0] - heads_here), (heads_here, LANES - heads_here - 1)),
    )
    bias_extra = jnp.tile(bias_block, (grid.count, 1))
    grad_values = tie(grad_values, *sum_qk.sent, *sum_go.sent)
    sum_vf = weight_gradient(
        grid,
        [(normed_attn_t, grad_values), (normed_attn_t, grad_forget)],
        1,
        "halves",
        bias_extra,
    )
    back = [
        (tie(grad_gate_logit, *sum_vf.sent), gate_w),
        (grad_queries, query_w),
        (grad_keys, key_w),
        (grad_values, value_w),
        (grad_forget, forget_w),
    ]
    other_part = multiply_back(back, 1 - side, low, 2)
    arrived = exchanged(other_part)
    line_mlp.fourth(*other_part)
    sum_qk.second(*other_part)
    hidden = tie(hidden, line_mlp.sent, *sum_qk.sent)
    other_down = multiply_back([(hidden, mlp_down)], jnp.int32(1), low)
    arrived_down = exchanged(other_down)
    sum_vf.start(*sum_qk.sent)
    back[1] = (tie(grad_queries, line_mlp.sent, *sum_qk.sent), query_w)
    (own_part,) = multiply_back(back, side)
    line_go = LineSum(grid, [sum_go]).third(own_part)
    own_part = tie(own_part, line_go.sent)
    _, tokens_grad = row_kernel(
        norm_gradient,
        [tokens, own_part, *arrived, grad_middle, gain_attn],
        [(columns, jnp.float32), (columns, low)],
    )
    sum_vf.second(tokens_grad)
    line_qkv = LineSum(grid, [sum_qk, sum_vf]).third()
    line_qkv.fourth()
    (own_down,) = multiply_back([(tie(hidden, line_qkv.sent), mlp_down)], jnp.int32(0))
    (mixed,) = row_kernel(
        lambda middle, own, part: (lower(middle + (own + wide(part))),),
        [middle, own_down, *arrived_down],
        [(columns, low)],
    )
    line_go.fourth(line_qkv.sent)
    sum_down.step(0, line_qkv.sent)
    down_grad, go_grad, qkv_grad = sum_down.result().T, line_go.result(), line_qkv.result()
    mlp_grad = line_mlp.result()

    def gain_gradient(gain, *pairs):
        return sum(jnp.sum(wide(lower(w)) * grad, axis=1) for w, grad in pairs) / gain

    forget_at = 3 * width
    parts = jnp.stack(
        [
            gain_gradient(
                pair_gains[0],
                (w_query, qkv_grad[:, :width]),
                (w_key, qkv_grad[:, width : 2 * width]),
                (w_value, qkv_grad[:, 2 * width : forget_at]),
                (w_forget, qkv_grad[:, forget_at : forget_at + heads_here]),
                (w_gate_attn, go_grad[:, :width]),
            ),
            gain_gradient(
                pair_gains[1], (w_gate, mlp_grad[:, :hidden_here]), (w_up, mlp_grad[:, hidden_here:])
            ),
        ]
    ).reshape(2, 2, norm_attn.shape[0])
    gain_grads = pick(parts, 1, side) + partner(pick(parts, 1, 1 - side))
    return (
        mixed,
        tokens_grad,
        qkv_grad[:, :width],
        qkv_grad[:, width : 2 * width],
        qkv_grad[:, 2 * width : 3 * width],
        go_grad[:, :width],
        qkv_grad[:, 3 * width : 3 * width + heads_here],
        qkv_grad[:heads_here, forget_at + heads_here],
        go_grad[:, width:].T,
        gain_grads[0],
        gain_grads[1],
        mlp_grad[:, :hidden_here],
        mlp_grad[:, hidden_here:],
        down_grad,
    )


def solution(mesh):
    return jax.shard_map(
        per_device,
        mesh=mesh,
        in_specs=(
            P(("dp", "tensor"), None),
            P("dp", "tensor"),
            P("dp", "tensor"),
            P("dp", "tensor"),
            P("dp", "tensor"),
            P("dp", "tensor"),
            P("tensor"),
            P("tensor", "dp"),
            P(("dp", "tensor")),
            P(("dp", "tensor")),
            P("dp", "tensor"),
            P("dp", "tensor"),
            P("tensor", "dp"),
            P(("dp", "tensor"), None),
        ),
        out_specs=(
            P(("dp", "tensor"), None),
            P(("dp", "tensor"), None),
            P("dp", "tensor"),
            P("dp", "tensor"),
            P("dp", "tensor"),
            P("dp", "tensor"),
            P("dp", "tensor"),
            P("tensor"),
            P("tensor", "dp"),
            P(("dp", "tensor")),
            P(("dp", "tensor")),
            P("dp", "tensor"),
            P("dp", "tensor"),
            P("tensor", "dp"),
        ),
        check_vma=False,
    )
```

```python
import functools

import jax
import jax.numpy as jnp
from jax import lax
from jax.experimental import pallas as pl
from jax.experimental.pallas import tpu as pltpu
from jax.sharding import PartitionSpec as P

EPSILON = 1e-06
LANES = 128
VMEM_LIMIT = 50 * 2**20
COST_SCALE = 0.02


def lower(values):
    return values.astype(jnp.bfloat16)


def wide(values):
    return values.astype(jnp.float32)


def matmul(left, right):
    return jnp.dot(left, right, preferred_element_type=jnp.float32)


def first_contract(left, right):
    return lax.dot_general(
        left, right, (((0,), (0,)), ((), ())), preferred_element_type=jnp.float32
    )


def second_contract(left, right):
    return lax.dot_general(
        left, right, (((1,), (1,)), ((), ())), preferred_element_type=jnp.float32
    )


def statistics(values):
    inverse = lax.rsqrt(jnp.mean(values * values, axis=-1, keepdims=True) + EPSILON)
    return (values * inverse, inverse)


def norm_backward(unit, inverse, gain, grad):
    scaled = gain * grad
    return inverse * (scaled - unit * jnp.mean(scaled * unit, axis=-1, keepdims=True))


def partner(values):
    return lax.ppermute(values, "tensor", [(0, 1), (1, 0)])


def tie(value, *others):
    if not others:
        return value
    return lax.optimization_barrier((value, *others))[0]


def small_cost(flops, size):
    return pl.CostEstimate(
        flops=int(COST_SCALE * flops), bytes_accessed=int(COST_SCALE * size), transcendentals=0
    )


class Grid:
    def __init__(self):
        self.count = lax.axis_size("dp")
        self.index = lax.axis_index("dp")
        bits = self.count.bit_length() - 1
        self.line_bits = list(range(2, bits))

    def bit(self, number):
        return (self.index >> number) & 1

    def swap(self, values, number):
        pairs = [(i, i ^ (1 << number)) for i in range(self.count)]
        return lax.ppermute(values, "dp", pairs)

    def place(self, pieces, splits):
        rows = pieces[0][1].shape[1]
        arrays = [piece for _, piece in pieces]
        codes = [code for found, _ in pieces for code in found]
        kind = arrays[0].dtype

        def body(*refs):
            inputs, results, sem = refs[: len(arrays)], refs[len(arrays) : -1], refs[-1]
            here = lax.axis_index("dp")
            copies = []
            for (found, _), ref in zip(pieces, inputs):
                for number, code in enumerate(found):
                    start = 0
                    for width, result in zip(splits, results):
                        copies.append(
                            pltpu.make_async_copy(
                                ref.at[number, :, pl.ds(start, width)],
                                result.at[here ^ code],
                                sem.at[len(copies)],
                            )
                        )
                        start += width
            for copy in copies:
                copy.start()
            for copy in copies:
                copy.wait()

        size = self.count * rows * sum(splits) * kind.itemsize
        results = pl.pallas_call(
            body,
            out_shape=[jax.ShapeDtypeStruct((self.count, rows, w), kind) for w in splits],
            in_specs=[pl.BlockSpec(memory_space=pl.ANY)] * len(arrays),
            out_specs=[pl.BlockSpec(memory_space=pltpu.VMEM)] * len(splits),
            scratch_shapes=[pltpu.SemaphoreType.DMA((len(codes) * len(splits),))],
            compiler_params=pltpu.CompilerParams(vmem_limit_bytes=VMEM_LIMIT),
            cost_estimate=small_cost(0, 2 * size),
        )(*arrays)
        return [r.reshape(self.count * rows, w) for r, w in zip(results, splits)]


class Weight:
    def __init__(self, grid, pieces, first=0, width=None):
        self.grid, self.pieces, self.first = grid, pieces, first
        self.rows = pieces[0][1].shape[1]
        self.width = width or pieces[0][1].shape[2]
        self.in_kernel = self.rows % 16 == 0

    def part(self, first, width):
        return Weight(self.grid, self.pieces, self.first + first, width)

    def arrays(self):
        return [piece for _, piece in self.pieces]

    def assembled(self):
        pieces = [
            (codes, piece[:, :, self.first : self.first + self.width])
            for codes, piece in self.pieces
        ]
        return self.grid.place(pieces, [self.width])[0]

    def copies(self, refs, target, sem, tiles):
        here = lax.axis_index("dp")
        tile = self.width // tiles
        found = []
        for step in range(tiles):
            for (codes, _), ref in zip(self.pieces, refs):
                for number, code in enumerate(codes):
                    block = here ^ code
                    source = ref.at[number, :, pl.ds(self.first + step * tile, tile)]
                    found.append(
                        pltpu.make_async_copy(source, target(step, block), sem.at[step, block])
                    )
        return found


def multiply(left, weight, tiles, epilogue, extras, outs):
    if not weight.in_kernel:
        return epilogue(matmul(left, weight.assembled()), *extras)
    grid, rows = weight.grid, weight.rows
    length, depth = left.shape
    tile = weight.width // tiles
    arrays = weight.arrays()

    def body(*refs):
        left_ref, refs = refs[0], refs[1:]
        piece_refs, refs = refs[: len(arrays)], refs[len(arrays) :]
        extra_refs, refs = refs[: len(extras)], refs[len(extras) :]
        out_refs, (held, sem) = refs[: len(outs)], refs[len(outs) :]
        step = pl.program_id(0)

        def target(place, block):
            return held.at[place, pl.ds(pl.multiple_of(block * rows, 16), rows)]

        @pl.when(step == 0)
        def _():
            for copy in weight.copies(piece_refs, target, sem, tiles):
                copy.start()

        for block in range(grid.count):
            there = target(step, block)
            pltpu.make_async_copy(there, there, sem.at[step, block]).wait()
        results = epilogue(matmul(left_ref[...], held[step]), *[ref[...] for ref in extra_refs])
        for ref, result in zip(out_refs, results):
            ref[...] = result

    def column_block(width):
        return pl.BlockSpec((length, width // tiles), lambda step: (0, step))

    size = (
        left.size * 2
        + depth * weight.width * 2
        + sum(e.size * e.dtype.itemsize for e in extras)
        + sum(length * w * jnp.dtype(kind).itemsize for w, kind in outs)
    )
    return pl.pallas_call(
        body,
        grid=(tiles,),
        in_specs=[pl.BlockSpec((length, depth), lambda step: (0, 0))]
        + [pl.BlockSpec(memory_space=pl.ANY)] * len(arrays)
        + [column_block(extra.shape[1]) for extra in extras],
        out_specs=[column_block(width) for width, _ in outs],
        out_shape=[jax.ShapeDtypeStruct((length, width), kind) for width, kind in outs],
        scratch_shapes=[
            pltpu.VMEM((tiles, depth, tile), jnp.bfloat16),
            pltpu.SemaphoreType.DMA((tiles, grid.count)),
        ],
        cost_estimate=small_cost(2 * length * depth * weight.width, size),
        compiler_params=pltpu.CompilerParams(vmem_limit_bytes=VMEM_LIMIT),
    )(left, *arrays, *extras)


def multiply_back(terms, half, kind=jnp.float32, parts=1, tiles=4):
    grid, rows = terms[0][1].grid, terms[0][1].rows
    length = terms[0][0].shape[0] // 2
    if not terms[0][1].in_kernel:
        total = sum(
            second_contract(
                lax.dynamic_slice_in_dim(left, half * length, length, 0), weight.assembled()
            )
            for left, weight in terms
        )
        return jnp.split(total.astype(kind), parts, axis=1)
    depth = grid.count * rows
    tile, share = depth // tiles, grid.count // tiles
    run = tiles // parts

    def part_spec(number):
        return pl.BlockSpec(
            (length, tile), lambda step, which: (0, jnp.clip(step - number * run, 0, run - 1))
        )

    sources, counts = [], []
    for _, weight in terms:
        sources = sources + weight.arrays()
        counts.append(len(weight.pieces))

    def body(half_ref, *refs):
        left_refs, refs = refs[: len(terms)], refs[len(terms) :]
        piece_refs, refs = refs[: len(sources)], refs[len(sources) :]
        out_refs, refs = refs[:parts], refs[parts:]
        held, sems = refs[: len(terms)], refs[len(terms) :]
        step = pl.program_id(0)

        def target(number):
            def found(_, block):
                return held[number].at[pl.ds(pl.multiple_of(block * rows, 16), rows)]

            return found

        @pl.when(step == 0)
        def _():
            first = 0
            for number, (_, weight) in enumerate(terms):
                mine = piece_refs[first : first + counts[number]]
                first += counts[number]
                for copy in weight.copies(mine, target(number), sems[number], 1):
                    copy.start()

        total = None
        for number in range(len(terms)):
            for part in range(share):
                block = step * share + part
                there = target(number)(0, block)
                pltpu.make_async_copy(there, there, sems[number].at[0, block]).wait()
            found = held[number][pl.ds(pl.multiple_of(step * tile, 16), tile), :]
            product = second_contract(left_refs[number][...], found)
            total = product if total is None else total + product
        for number, out_ref in enumerate(out_refs):

            @pl.when(step // run == number)
            def _():
                out_ref[...] = total.astype(kind)

    size = length * depth * 4 + sum(l.size + depth * w.width * 2 for l, w in terms)
    flops = sum(2 * length * depth * w.width for _, w in terms)
    return pl.pallas_call(
        body,
        grid_spec=pltpu.PrefetchScalarGridSpec(
            num_scalar_prefetch=1,
            grid=(tiles,),
            in_specs=[
                pl.BlockSpec((length, left.shape[1]), lambda step, which: (which[0], 0))
                for left, _ in terms
            ]
            + [pl.BlockSpec(memory_space=pl.ANY)] * len(sources),
            out_specs=[part_spec(number) for number in range(parts)],
            scratch_shapes=[pltpu.VMEM((depth, w.width), jnp.bfloat16) for _, w in terms]
            + [pltpu.SemaphoreType.DMA((1, grid.count)) for _ in terms],
        ),
        out_shape=[jax.ShapeDtypeStruct((length, depth // parts), kind)] * parts,
        cost_estimate=small_cost(flops, size),
        compiler_params=pltpu.CompilerParams(vmem_limit_bytes=VMEM_LIMIT),
    )(jnp.reshape(half, (1,)).astype(jnp.int32), *[left for left, _ in terms], *sources)


class Gather:
    def __init__(self, grid, shard, *after):
        near, codes = tie(shard[None], *after), [0]
        for number in reversed(grid.line_bits[1:]):
            found = grid.swap(near, number)
            near = jnp.concatenate([near, found], axis=0)
            codes = codes + self.moved(codes, 1 << number)
        self.grid, self.near, self.codes = grid, near, codes

    def moved(self, found, plane):
        return [code ^ plane for code in found]

    def line_end(self, *after):
        last = self.grid.line_bits[0]
        self.near = tie(self.near, *after)
        self.far = self.grid.swap(self.near, last)
        self.far_codes = self.moved(self.codes, 1 << last)
        return self

    def plane(self, *after, fine=False, to_end=True):
        grid, near, far, codes, far_codes = (
            self.grid,
            self.near,
            self.far,
            self.codes,
            self.far_codes,
        )
        moved, both, half = self.moved, self.codes + self.far_codes, len(self.codes)
        if fine:
            near_x, near_y = grid.swap(near, 0), grid.swap(near, 1)
            far_x, far_y = grid.swap(far, 0), grid.swap(far, 1)
            sides = [
                (codes, near),
                (far_codes, far),
                (moved(codes, 1), near_x),
                (moved(codes, 2), near_y),
                (moved(far_codes, 1), far_x),
                (moved(far_codes, 2), far_y),
            ]
            received = (near_y, far_x)
        else:
            block = tie(jnp.concatenate([near, far], axis=0), *after)
            side_x, side_y = grid.swap(block, 0), grid.swap(block, 1)
            near_x, far_y = side_x[:half], side_y[half:]
            sides = [(both, block), (moved(both, 1), side_x), (moved(both, 2), side_y)]
            received = ()
            self.block = block
        self.corner_parts, self.received, self.sides = (near_x, far_y), received, sides
        return self.plane_end() if to_end else self

    def plane_end(self, *after):
        grid, codes, far_codes = self.grid, self.codes, self.far_codes
        moved, sides = self.moved, self.sides
        near_x, far_y = [tie(part, *after) for part in self.corner_parts]
        near_corner, far_corner = grid.swap(near_x, 1), grid.swap(far_y, 0)
        self.corners = (near_corner, far_corner, *self.received)
        corners = [(moved(codes, 3), near_corner), (moved(far_codes, 3), far_corner)]
        self.weight = Weight(grid, sides + corners)
        return self


def gradient_parts(grid, pairs, tiles, form, extra=None):
    depth, length = pairs[0][0].shape
    rows, line = depth // grid.count, grid.count // 4
    width = sum(right.shape[1] for _, right in pairs)
    lefts = []
    for left, _ in pairs:
        if not any(left is other for other in lefts):
            lefts.append(left)
    which = [[left is other for other in lefts].index(True) for left, _ in pairs]
    tile = width // tiles
    starts, first = [], 0
    for _, right in pairs:
        starts.append(first)
        first += right.shape[1]

    def body(*refs):
        left_refs, refs = refs[: len(lefts)], refs[len(lefts) :]
        right_refs, refs = refs[: len(pairs)], refs[len(pairs) :]
        if extra is not None:
            extra_ref, refs = refs[0], refs[1:]
        outs, total = refs[:-1], refs[-1]
        step = pl.program_id(0)
        if tiles == 1:
            for place in range(len(pairs)):
                ahead = starts[place]
                total[:, ahead : ahead + pairs[place][1].shape[1]] = matmul(
                    left_refs[which[place]][...], right_refs[place][...]
                )
        elif len(pairs) == 1:
            total[...] = matmul(left_refs[0][...], right_refs[0][...])
        else:
            for place in range(len(pairs)):
                low = starts[place] // tile
                high = low + pairs[place][1].shape[1] // tile

                @pl.when((step >= low) & (step < high))
                def _():
                    total[...] = matmul(left_refs[which[place]][...], right_refs[place][...])

        if extra is not None:
            total[:, tile - extra.shape[1] :] += extra_ref[...]
        index = lax.axis_index("dp")

        def block(place):
            return lower(total[pl.ds(pl.multiple_of(place * rows, 8), rows), :])

        if form == "line":
            here = (index >> 2) & 1
            for place in range(half):
                for plane in range(4):
                    outs[0][place, plane] = block((2 * place + 1 - here) * 4 + plane)
                    outs[1][place, plane] = block((2 * place + here) * 4 + plane)
            return

        for number, first, count, away, own in (
            [(form, 0, line, *outs)]
            if form in (0, 1)
            else [(1, 0, half, outs[0], outs[2]), (0, half, half, outs[1], outs[3])]
        ):
            here = (index >> number) & 1
            for place in range(count):
                for side in range(2):
                    base = (first + place) * 4 + side * (3 - (1 << number))
                    away[place, side] = block(base + ((1 - here) << number))
                    own[place, side] = block(base + (here << number))

    def right_spec(place):
        columns = pairs[place][1].shape[1]
        if tiles == 1:
            return pl.BlockSpec((length, columns), lambda step: (0, 0))
        low, count = starts[place] // tile, columns // tile
        return pl.BlockSpec((length, tile), lambda step: (0, jnp.clip(step - low, 0, count - 1)))

    half = line // 2
    cut, parts = {"line": ((half, 4), 2), "halves": ((half, 2), 4)}.get(form, ((line, 2), 2))
    out = jax.ShapeDtypeStruct((*cut, rows, width), jnp.bfloat16)
    out_spec = pl.BlockSpec((*cut, rows, tile), lambda step: (0, 0, 0, step))
    size = depth * width * 2 + sum(l.size * 2 for l in lefts) + sum(r.size * 2 for _, r in pairs)
    return pl.pallas_call(
        body,
        grid=(tiles,),
        in_specs=[pl.BlockSpec((depth, length), lambda step: (0, 0))] * len(lefts)
        + [right_spec(place) for place in range(len(pairs))]
        + ([] if extra is None else [pl.BlockSpec(extra.shape, lambda step: (0, 0))]),
        out_specs=[out_spec] * parts,
        out_shape=[out] * parts,
        scratch_shapes=[pltpu.VMEM((depth, tile), jnp.float32)],
        cost_estimate=small_cost(2 * depth * length * width, size),
        compiler_params=pltpu.CompilerParams(vmem_limit_bytes=VMEM_LIMIT),
    )(*lefts, *[right for _, right in pairs], *([] if extra is None else [extra]))


def pick(array, axis, place):
    return lax.dynamic_index_in_dim(array, place, axis, keepdims=False)


def cut_parts(grid, array, form):
    line, rows = grid.count // 4, array.shape[0] // grid.count
    blocks = array.reshape(line, 2, 2, rows, array.shape[1])

    def cut(blocks, number):
        here, axis = grid.bit(number), 2 - number
        return pick(blocks, axis, 1 - here), pick(blocks, axis, here)

    if form in (0, 1):
        return cut(blocks, form)
    if form == "line":
        here, whole = grid.bit(2), array.reshape(line // 2, 2, 4, rows, array.shape[1])
        return pick(whole, 1, 1 - here), pick(whole, 1, here)
    low, high = cut(blocks[: line // 2], 1), cut(blocks[line // 2 :], 0)
    return low[0], high[0], low[1], high[1]


def weight_gradient(grid, pairs, tiles, form, extra=None):
    rows = pairs[0][0].shape[0] // grid.count
    if rows % 16 == 0:
        parts = gradient_parts(grid, pairs, tiles, form, extra)
    else:
        found = [matmul(left, right) for left, right in pairs]
        if extra is not None:
            found[-1] = found[-1] + extra
        parts = cut_parts(grid, lower(jnp.concatenate(found, axis=1)), form)
    return BitSum(grid, parts) if form == "line" else PlaneSum(grid, parts, form)


def add_halves(terms, number):
    count, _, rows, columns = terms[0].shape
    tile = next(t for t in (512, 384, 256, 128, columns) if columns % t == 0)

    def body(*refs):
        inputs, (away, kept) = refs[: len(terms)], refs[len(terms) :]
        side = (lax.axis_index("dp") >> number) & 1
        for place in range(count):
            away[place] = lower(sum(wide(ref[place, 1 - side]) for ref in inputs))
            kept[place] = lower(sum(wide(ref[place, side]) for ref in inputs))

    block = pl.BlockSpec((count, 2, rows, tile), lambda step: (0, 0, 0, step))
    half = pl.BlockSpec((count, rows, tile), lambda step: (0, 0, step))
    size = terms[0].size * (2 * len(terms) + 2)
    return pl.pallas_call(
        body,
        grid=(columns // tile,),
        in_specs=[block] * len(terms),
        out_specs=[half] * 2,
        out_shape=[jax.ShapeDtypeStruct((count, rows, columns), jnp.bfloat16)] * 2,
        cost_estimate=small_cost(0, size),
        compiler_params=pltpu.CompilerParams(vmem_limit_bytes=VMEM_LIMIT),
    )(*terms)


def add_joined(packs, number):
    rows = packs[0][0][0].shape[2]
    widths = [pack[0][0].shape[3] for pack in packs]
    count = sum(group[0].shape[0] for group in packs[0])
    flat = [term for pack in packs for group in pack for term in group]

    def body(*refs):
        inputs, (away, kept) = list(refs[: len(flat)]), refs[len(flat) :]
        side = (lax.axis_index("dp") >> number) & 1
        start = 0
        for pack, width in zip(packs, widths):
            place = 0
            for group in pack:
                terms = [inputs.pop(0) for _ in group]
                for row in range(group[0].shape[0]):
                    other = sum(wide(term[row, 1 - side]) for term in terms)
                    own = sum(wide(term[row, side]) for term in terms)
                    away[place, :, start : start + width] = lower(other)
                    kept[place, :, start : start + width] = lower(own)
                    place += 1
            start += width

    out = jax.ShapeDtypeStruct((count, rows, sum(widths)), jnp.bfloat16)
    return pl.pallas_call(
        body,
        out_shape=[out] * 2,
        cost_estimate=small_cost(0, 2 * sum(term.size for term in flat)),
        compiler_params=pltpu.CompilerParams(vmem_limit_bytes=VMEM_LIMIT),
    )(*flat)


def joined_rows(own, others, in_sequence):
    rows, columns = own.shape
    tile, run = columns // 4, 4 // len(others)

    def body(own_ref, *refs):
        other_refs, (rows_ref, turned_ref) = refs[: len(others)], refs[len(others) :]
        first, second = own_ref[...], other_refs[0][...]
        for number in range(1, len(others)):
            later = pl.program_id(0) >= number * run
            second = jnp.where(later, other_refs[number][...], second)
        if in_sequence:
            ahead = lax.axis_index("tensor") == 0
            first, second = jnp.where(ahead, first, second), jnp.where(ahead, second, first)
        rows_ref[:rows] = first
        rows_ref[rows:] = second
        turned_ref[:, :rows] = first.T
        turned_ref[:, rows:] = second.T

    def part_spec(number):
        return pl.BlockSpec(
            (rows, tile), lambda step: (0, jnp.clip(step - number * run, 0, run - 1))
        )

    return pl.pallas_call(
        body,
        grid=(4,),
        in_specs=[pl.BlockSpec((rows, tile), lambda step: (0, step))]
        + [part_spec(number) for number in range(len(others))],
        out_specs=[
            pl.BlockSpec((2 * rows, tile), lambda step: (0, step)),
            pl.BlockSpec((tile, 2 * rows), lambda step: (step, 0)),
        ],
        out_shape=[
            jax.ShapeDtypeStruct((2 * rows, columns), own.dtype),
            jax.ShapeDtypeStruct((columns, 2 * rows), own.dtype),
        ],
        cost_estimate=small_cost(0, 12 * rows * columns),
        compiler_params=pltpu.CompilerParams(vmem_limit_bytes=VMEM_LIMIT),
    )(own, *others)


def row_kernel(body, inputs, outs, sums=0):
    length, columns = inputs[0].shape
    tile = length // 4

    def spec(rows, width):
        if rows == 1:
            return pl.BlockSpec((1, width), lambda step: (0, 0))
        return pl.BlockSpec((tile, width), lambda step: (step, 0))

    def kernel(*refs):
        found = body(*[ref[...] for ref in refs[: len(inputs)]])
        out_refs = refs[len(inputs) :]
        for ref, value in zip(out_refs[: len(outs)], found):
            ref[...] = value
        for ref, value in zip(out_refs[len(outs) :], found[len(outs) :]):

            @pl.when(pl.program_id(0) == 0)
            def _():
                ref[...] = jnp.zeros_like(ref)

            ref[...] += value

    size = length * columns * (sum(i.dtype.itemsize for i in inputs) + 4 * len(outs))
    return pl.pallas_call(
        kernel,
        grid=(4,),
        in_specs=[spec(*i.shape) for i in inputs],
        out_specs=[spec(length, width) for width, _ in outs] + [spec(1, columns)] * sums,
        out_shape=[jax.ShapeDtypeStruct((length, width), kind) for width, kind in outs]
        + [jax.ShapeDtypeStruct((1, columns), jnp.float32)] * sums,
        cost_estimate=small_cost(0, size),
        compiler_params=pltpu.CompilerParams(vmem_limit_bytes=VMEM_LIMIT),
    )(*inputs)


def halves(values):
    half = values.shape[1] // 2
    return values, values[:, :half], values[:, half:]


def both_parts(first, second):
    return wide(jnp.concatenate([first, second], axis=1))


def norm_forward(residual, own, first, second, gain):
    middle = wide(residual) + (own + both_parts(first, second))
    unit, _ = statistics(middle)
    return middle, *halves(lower(unit * gain))


def norm_gradient(source, own, first, second, base, gain):
    unit, inverse = statistics(wide(source))
    grad = own + both_parts(first, second)
    total = wide(base) + norm_backward(unit, inverse, gain, grad)
    return total, lower(total)


def norm_gradient_halves(*values):
    total, rounded = norm_gradient(*values)
    return total, *halves(rounded)


class PlaneSum:
    def __init__(self, grid, parts, form):
        half = len(parts) // 2
        self.grid, self.sent, self.own = grid, tuple(parts[:half]), tuple(parts[half:])
        self.numbers = (form,) if form in (0, 1) else (1, 0)

    def start(self, *after):
        swaps = zip(self.sent, self.numbers)
        self.got = [self.grid.swap(tie(sent, *after), number) for sent, number in swaps]
        return self

    def second(self, *after):
        sent, self.groups = [], []
        for own, got, number in zip(self.own, self.got, self.numbers):
            away, kept = add_halves([own, tie(got, *after)], 1 - number)
            sent.append(away)
            self.groups.append([kept, self.grid.swap(away, 1 - number)])
        self.sent = tuple(sent)
        return self


class BitSum:
    def __init__(self, grid, parts):
        self.grid, self.sent, self.kept = grid, *parts

    def start(self, *after):
        self.got = self.grid.swap(tie(self.sent, *after), 2)
        return self

    def step(self, number, *after):
        def cut(array):
            rows, columns = array.shape[-2:]
            count = array.size // (rows * columns)
            if number >= 2:
                count, rows = count // 4, rows * 4
            else:
                count = 1
                rows = array.size // (2 * columns)
            return array.reshape(count if number < 2 else count // 2, 2, rows, columns)

        self.sent, self.kept = add_halves([cut(self.kept), cut(tie(self.got, *after))], number)
        self.got = self.grid.swap(self.sent, number)
        if number >= 2:
            shape = (self.sent.shape[0], 4, self.sent.shape[1] // 4, self.sent.shape[2])
            self.kept, self.got = self.kept.reshape(shape), self.got.reshape(shape)
        return self

    def line(self, *after):
        for number in self.grid.line_bits[1:]:
            self.step(number, *after)
        return self

    def result(self):
        return wide(self.kept[0]) + wide(self.got[0])


class LineSum:
    def __init__(self, grid, sums):
        self.grid, self.packs = grid, [found.groups for found in sums]

    def step(self, number, after):
        packs = [
            [
                [t.reshape((t.shape[0] // 2, 2) + t.shape[1:]) for t in (*kept, tie(got, *after))]
                for *kept, got in groups
            ]
            for groups in self.packs
        ]
        self.sent, kept = add_joined(packs, number)
        self.packs = [[[kept, self.grid.swap(self.sent, number)]]]
        return self

    def third(self, *after):
        return self.step(self.grid.line_bits[0], after)

    def fourth(self, *after):
        for number in self.grid.line_bits[1:]:
            self.step(number, after)
        return self

    def result(self):
        return sum(wide(term[0]) for term in self.packs[0][0])


def running_sum(values, reverse):
    length = values.shape[1]
    place = lax.broadcasted_iota(jnp.int32, values.shape, 1)
    shift = 1
    while shift < length:
        if reverse:
            moved = jnp.where(place < length - shift, pltpu.roll(values, length - shift, 1), 0.0)
        else:
            moved = jnp.where(place >= shift, pltpu.roll(values, shift, 1), 0.0)
        values = values + moved
        shift *= 2
    return values


def decay_kernel(heads, logit_ref, bias_ref, row_ref, column_ref):
    length, lanes = logit_ref.shape
    groups, per, _ = row_ref.shape
    padded = -(-heads // 8) * 8
    logit = (logit_ref[...] + bias_ref[...]).T[:padded]
    decay = running_sum(-jnp.log1p(jnp.exp(-logit)), False)
    columns = jnp.concatenate([decay, jnp.zeros((lanes - padded, length), jnp.float32)], axis=0).T
    for group in range(groups):
        row_ref[group] = decay[group * per : (group + 1) * per]
        column_ref[group] = columns[:, group * per : (group + 1) * per]


def decays(logit, bias, heads, per):
    length = logit.shape[0]
    groups = heads // per
    return pl.pallas_call(
        functools.partial(decay_kernel, heads),
        out_shape=[
            jax.ShapeDtypeStruct((groups, per, length), jnp.float32),
            jax.ShapeDtypeStruct((groups, length, per), jnp.float32),
        ],
        compiler_params=pltpu.CompilerParams(vmem_limit_bytes=VMEM_LIMIT),
    )(logit, bias)


def forget_kernel(heads, row_ref, column_ref, logit_ref, bias_ref, grad_ref, sum_ref):
    length, lanes = logit_ref.shape
    groups, per, _ = row_ref.shape
    padded = -(-heads // 8) * 8
    rows = [row_ref[group] for group in range(groups)]
    columns = [column_ref[group] for group in range(groups)]
    columns = jnp.concatenate(
        columns + [jnp.zeros((length, lanes - heads), jnp.float32)], axis=1
    ).T[:padded]
    if padded > heads:
        rows = rows + [jnp.zeros((padded - heads, length), jnp.float32)]
    grad_log = running_sum(jnp.concatenate(rows, axis=0) - columns, True)
    grad_log = jnp.concatenate([grad_log, jnp.zeros((lanes - padded, length), jnp.float32)], axis=0).T
    grad = lower(grad_log * jax.nn.sigmoid(-(logit_ref[...] + bias_ref[...])))
    lane = lax.broadcasted_iota(jnp.int32, grad.shape, 1)
    grad = jnp.where(lane < heads, grad, jnp.bfloat16(0))
    grad_ref[...] = grad
    sum_ref[...] = jnp.sum(wide(grad), axis=0, keepdims=True)


def forget_backward(row, column, logit, bias, heads):
    return pl.pallas_call(
        functools.partial(forget_kernel, heads),
        out_shape=[
            jax.ShapeDtypeStruct(logit.shape, jnp.bfloat16),
            jax.ShapeDtypeStruct(bias.shape, jnp.float32),
        ],
        compiler_params=pltpu.CompilerParams(vmem_limit_bytes=VMEM_LIMIT),
    )(row, column, logit, bias)


def fwd_kernel(scale, head, q_ref, k_ref, v_ref, col_ref, row_ref, o_ref, lse_ref, out_t):
    length, lanes = q_ref.shape
    span = min(256, length)
    lane = lax.broadcasted_iota(jnp.int32, (span, lanes), 1) // head
    below = lax.broadcasted_iota(jnp.int32, (span, span), 0) <= lax.broadcasted_iota(jnp.int32, (span, span), 1)
    v_t = v_ref[...].T
    for h in range(lanes // head):
        for b in range(length // span):
            lo, hi = b * span, (b + 1) * span
            q = jnp.where(lane == h, q_ref[lo:hi, :] * scale, 0).astype(jnp.bfloat16)
            row = row_ref[0, h:h+1, lo:hi]
            diag = second_contract(k_ref[lo:hi, :], q) + row - col_ref[0, lo:hi, h:h+1]
            diag = jnp.where(below, diag, -1e30)
            top = jnp.max(diag, axis=0, keepdims=True)
            if lo:
                off = second_contract(k_ref[:lo, :], q) + row - col_ref[0, :lo, h:h+1]
                top = jnp.maximum(top, jnp.max(off, axis=0, keepdims=True))
            e = jnp.exp(diag - top)
            total = jnp.sum(e, axis=0, keepdims=True)
            v_h = v_t[h*head:(h+1)*head]
            acc = matmul(v_h[:, lo:hi], lower(e))
            if lo:
                e = jnp.exp(off - top)
                total = total + jnp.sum(e, axis=0, keepdims=True)
                acc = acc + matmul(v_h[:, :lo], lower(e))
            out_t[h*head:(h+1)*head, lo:hi] = acc / total
            lse_ref[0, h:h+1, lo:hi] = top + jnp.log(total)
    o_ref[...] = out_t[...].T

def bwd_kernel(scale, head, q_ref, k_ref, v_ref, do_ref, col_ref, row_ref, lse_ref, dq_ref, dk_ref, dv_ref, drow_ref, dcol_ref, dq_t, dk_acc, dv_acc):
    length, lanes = q_ref.shape
    span = min(256, length)
    heads = lanes // head
    lane = lax.broadcasted_iota(jnp.int32, (span, lanes), 1) // head
    sub = lax.broadcasted_iota(jnp.int32, (lanes, length), 0) // head
    below = lax.broadcasted_iota(jnp.int32, (span, span), 0) <= lax.broadcasted_iota(jnp.int32, (span, span), 1)
    k_t = k_ref[...].T
    one = jnp.bfloat16(1)
    for h in range(heads):
        kt_h = jnp.where(sub == h, k_t, one)
        mine = lane == h
        for b in range(length // span):
            lo, hi = b * span, (b + 1) * span
            q = q_ref[lo:hi, :] * jnp.bfloat16(scale)
            qz = jnp.where(mine, q, jnp.bfloat16(0))
            q1 = jnp.where(mine, q, one)
            do = do_ref[lo:hi, :]
            doz = jnp.where(mine, do, jnp.bfloat16(0))
            row = row_ref[0, h:h+1, lo:hi] - lse_ref[0, h:h+1, lo:hi]
            s = second_contract(k_ref[lo:hi, :], qz) + row - col_ref[0, lo:hi, h:h+1]
            p = jnp.exp(jnp.where(below, s, -1e30))
            dp = second_contract(v_ref[lo:hi, :], doz)
            centre = jnp.sum(p * dp, axis=0, keepdims=True)
            if lo:
                s0 = second_contract(k_ref[:lo, :], qz) + row - col_ref[0, :lo, h:h+1]
                p0 = jnp.exp(s0)
                dp0 = second_contract(v_ref[:lo, :], doz)
                centre = centre + jnp.sum(p0 * dp0, axis=0, keepdims=True)
            ds = lower(p * (dp - centre))
            dqt = matmul(kt_h[:, lo:hi], ds)
            dv_acc[h, lo:hi, :] = matmul(lower(p), do)
            dk_acc[h, lo:hi, :] = matmul(ds, q1)
            if lo:
                ds0 = lower(p0 * (dp0 - centre))
                dqt = dqt + matmul(kt_h[:, :lo], ds0)
                dv_acc[h, :lo, :] = dv_acc[h, :lo, :] + matmul(lower(p0), do)
                dk_acc[h, :lo, :] = dk_acc[h, :lo, :] + matmul(ds0, q1)
            dq_t[h*head:(h+1)*head, lo:hi] = dqt[h*head:(h+1)*head] * scale
            other = ((h + 1) % heads) * head
            drow_ref[0, h:h+1, lo:hi] = dqt[other:other+1]
    lane_all = lax.broadcasted_iota(jnp.int32, (length, lanes), 1) // head
    dk, dv = dk_acc[0], dv_acc[0]
    for h in range(1, heads):
        dk = jnp.where(lane_all == h, dk_acc[h], dk)
        dv = jnp.where(lane_all == h, dv_acc[h], dv)
    for h in range(heads):
        other = ((h + 1) % heads) * head
        dcol_ref[0, :, h:h+1] = dk_acc[h][:, other:other+1]
    dq_ref[...] = lower(dq_t[...].T)
    dk_ref[...] = lower(dk)
    dv_ref[...] = lower(dv)


def pair_specs(length, groups, per):
    def block(offset):
        return pl.BlockSpec((length, LANES), lambda group: (0, group + offset))

    column = pl.BlockSpec((1, length, per), lambda group: (group, 0, 0))
    row = pl.BlockSpec((1, per, length), lambda group: (group, 0, 0))
    return block, column, row


def attention_cost(length, width, head, products):
    return small_cost(products * 6 * length * length * width, 16 * length * width)


def attend(qk, values, column, row, head):
    length, width = values.shape[0], qk.shape[1] // 2
    groups, per, _ = row.shape
    block, column_spec, row_spec = pair_specs(length, groups, per)
    return pl.pallas_call(
        functools.partial(fwd_kernel, head**-0.5, head),
        grid=(groups,),
        in_specs=[block(0), block(groups), block(0), column_spec, row_spec],
        out_specs=[block(0), row_spec],
        out_shape=[
            jax.ShapeDtypeStruct((length, width), jnp.float32),
            jax.ShapeDtypeStruct(row.shape, jnp.float32),
        ],
        scratch_shapes=[pltpu.VMEM((LANES, length), jnp.float32)],
        cost_estimate=attention_cost(length, width, head, 2),
        compiler_params=pltpu.CompilerParams(vmem_limit_bytes=VMEM_LIMIT),
    )(qk, qk, values, column, row)


def attend_backward(qk, values, grad, column, row, logsum, head):
    length, width = values.shape[0], qk.shape[1] // 2
    groups, per, _ = row.shape
    block, column_spec, row_spec = pair_specs(length, groups, per)
    wide_out = jax.ShapeDtypeStruct((length, width), jnp.bfloat16)
    return pl.pallas_call(
        functools.partial(bwd_kernel, head**-0.5, head),
        grid=(groups,),
        in_specs=[block(0), block(groups), block(0), block(0), column_spec, row_spec, row_spec],
        out_specs=[block(0), block(0), block(0), row_spec, column_spec],
        out_shape=[
            wide_out,
            wide_out,
            wide_out,
            jax.ShapeDtypeStruct(row.shape, jnp.float32),
            jax.ShapeDtypeStruct(column.shape, jnp.float32),
        ],
        scratch_shapes=[
            pltpu.VMEM((LANES, length), jnp.float32),
            pltpu.VMEM((per, length, LANES), jnp.float32),
            pltpu.VMEM((per, length, LANES), jnp.float32),
        ],
        cost_estimate=attention_cost(length, width, head, 5),
        compiler_params=pltpu.CompilerParams(vmem_limit_bytes=VMEM_LIMIT),
    )(qk, qk, values, grad, column, row, logsum)


def per_device(
    tokens,
    w_query,
    w_key,
    w_value,
    w_gate_attn,
    w_forget,
    forget_bias,
    w_out,
    norm_attn,
    norm_mlp,
    w_gate,
    w_up,
    w_down,
    cotangent,
):
    grid = Grid()
    side = lax.axis_index("tensor")
    heads_here = forget_bias.shape[0]
    width = w_query.shape[1]
    head_size = width // heads_here
    hidden_here = w_gate.shape[1]
    scale = head_size ** (-0.5)
    rows_here = tokens.shape[0]

    load_qk = Gather(grid, jnp.concatenate([lower(w_query), lower(w_key)], axis=1))
    own_gains = jnp.stack([norm_attn, norm_mlp])
    other_gains = partner(own_gains)
    gains = jnp.where(
        side == 0,
        jnp.concatenate([own_gains, other_gains], axis=1),
        jnp.concatenate([other_gains, own_gains], axis=1),
    )[None]
    pair_gains, gain_codes = gains[0], [0]
    for number in range(len(grid.line_bits) + 2):
        gains = jnp.concatenate([gains, grid.swap(gains, number)], axis=0)
        gain_codes = gain_codes + [code ^ (1 << number) for code in gain_codes]
        if number == 1:
            load_qk.line_end(gains)
    (all_gains,) = grid.place([(gain_codes, gains)], [gains.shape[2]])
    all_gains = all_gains.reshape(grid.count, 2, all_gains.shape[1])
    gain_attn = all_gains[:, 0].reshape(-1)
    gain_mlp = all_gains[:, 1].reshape(-1)
    load_qk.plane(fine=True)
    other_cotangent = partner(tie(cotangent, gains))

    padding = jnp.zeros((w_forget.shape[0], LANES - heads_here), jnp.bfloat16)
    forget_lanes = jnp.concatenate([lower(w_forget), padding], axis=1)
    load_vf = Gather(
        grid, jnp.concatenate([lower(w_value), forget_lanes], axis=1), load_qk.far, gains
    )
    load_vf.line_end(*load_qk.corner_parts).plane(*load_qk.corners)
    load_go = Gather(
        grid, jnp.concatenate([lower(w_gate_attn), lower(w_out).T], axis=1), load_vf.far
    )
    load_go.line_end(load_vf.block)
    gain_attn, gain_mlp = gain_attn[None], gain_mlp[None]
    low = jnp.bfloat16
    columns = tokens.shape[1]
    rounded_outs = [(columns, low), (columns // 2, low), (columns // 2, low)]

    def exchanged(parts):
        return [partner(part) for part in parts]

    own_attn, *sent = row_kernel(
        lambda rows, gain: halves(lower(statistics(wide(rows))[0] * gain)),
        [tokens, gain_attn],
        rounded_outs,
    )
    normed_attn, normed_attn_t = joined_rows(own_attn, exchanged(sent), True)
    grad_output, grad_output_t = joined_rows(cotangent, [other_cotangent], False)

    load_go.plane(*load_vf.corners, normed_attn)
    load_gate = Gather(grid, lower(w_gate), load_go.far).line_end(load_go.block)
    load_up = Gather(grid, lower(w_up), load_gate.far, load_go.corners[0])
    value_w, forget_w = load_vf.weight.part(0, width), load_vf.weight.part(width, LANES)
    query_w, key_w = load_qk.weight.part(0, width), load_qk.weight.part(width, width)
    gate_w, out_w = load_go.weight.part(0, width), load_go.weight.part(width, width)

    (qk,) = multiply(
        normed_attn, load_qk.weight, 3, lambda p: (lower(p),), [], [(2 * width, low)]
    )
    values_all, forget_logit = multiply(
        normed_attn,
        load_vf.weight,
        1,
        lambda p: (lower(p[:, :width]), p[:, width:]),
        [],
        [(width, low), (LANES, jnp.float32)],
    )
    bias_lanes = jnp.pad(forget_bias, (0, LANES - heads_here))[None]
    decay_row, decay_column = decays(forget_logit, bias_lanes, heads_here, LANES // head_size)
    load_gate.plane(*load_go.corners, qk, to_end=False)
    load_up.line_end(load_gate.block, decay_row, values_all)
    qk = tie(qk, load_gate.block)
    attended, logsum = attend(qk, values_all, decay_column, decay_row, head_size)
    load_gate.plane_end(attended)
    load_up.plane(*load_gate.corners)
    load_down = Gather(grid, lower(w_down).T, load_up.far, load_gate.corners[0])
    load_down.line_end(load_up.block)
    mlp_gate, mlp_up = load_gate.weight, load_up.weight

    def gate_output(product, attended):
        sigmoid = jax.nn.sigmoid(product)
        return sigmoid, lower(attended * sigmoid)

    gate_sig, gated = multiply(
        normed_attn, gate_w, 2, gate_output, [attended], [(width, jnp.float32), (width, low)]
    )
    arrived = exchanged(multiply_back([(gated, out_w)], 1 - side, low, 2))
    (own_part,) = multiply_back([(gated, out_w)], side)
    middle, own_normed, *sent = row_kernel(
        norm_forward,
        [tokens, own_part, *arrived, gain_mlp],
        [(columns, jnp.float32)] + rounded_outs,
    )
    normed_mlp, normed_mlp_t = joined_rows(own_normed, exchanged(sent), False)
    (gate_act,) = multiply(
        normed_mlp, mlp_gate, 4, lambda p: (lower(p),), [], [(hidden_here, low)]
    )

    load_down.plane(*load_up.corners, gate_act, to_end=False)

    def hidden_units(up, gate):
        gate = wide(gate)
        return lower(up), lower(gate * jax.nn.sigmoid(gate) * up)

    up_act, hidden = multiply(
        normed_mlp, mlp_up, 4, hidden_units, [gate_act], [(hidden_here, low)] * 2
    )
    sum_down = weight_gradient(grid, [(grad_output_t, hidden)], 4, "line").start()
    mlp_down = load_down.plane_end(sum_down.sent).weight

    def hidden_backward(grad, gate, up):
        gate, up = wide(gate), wide(up)
        sigmoid = jax.nn.sigmoid(gate)
        return (
            lower(grad * (gate * sigmoid)),
            lower(grad * up * sigmoid * (1.0 + gate * (1.0 - sigmoid))),
        )

    grad_up, grad_gate = multiply(
        tie(grad_output, sum_down.sent),
        mlp_down,
        4,
        hidden_backward,
        [gate_act, up_act],
        [(hidden_here, low)] * 2,
    )
    sum_up = weight_gradient(grid, [(normed_mlp_t, grad_up)], 4, 0)
    sum_up.start()
    grad_gate = tie(grad_gate, *sum_up.sent)
    sum_gate = weight_gradient(grid, [(normed_mlp_t, grad_gate)], 4, 1).start()
    grad_gate = tie(grad_gate, *sum_gate.sent)
    back = [(grad_gate, mlp_gate), (grad_up, mlp_up)]
    arrived = exchanged(multiply_back(back, jnp.int32(1), low, 2))
    (own_part,) = multiply_back(back, jnp.int32(0))
    sum_down.line(own_part)
    own_part = tie(own_part, sum_down.sent)
    grad_middle, own_branch, *sent = row_kernel(
        norm_gradient_halves,
        [middle, own_part, *arrived, cotangent, gain_mlp],
        [(columns, jnp.float32)] + rounded_outs,
    )
    other_branch = exchanged(sent)
    grad_branch, grad_branch_t = joined_rows(own_branch, other_branch, True)

    def gate_backward(grad, sigmoid, attended):
        return lower(grad * sigmoid), lower(grad * attended * sigmoid * (1.0 - sigmoid))

    grad_attended, grad_gate_logit = multiply(
        grad_branch,
        out_w,
        2,
        gate_backward,
        [gate_sig, attended],
        [(width, low)] * 2,
    )
    sum_up.second(grad_attended)
    sum_gate.second(grad_attended)
    grad_gate_logit = tie(grad_gate_logit, *sum_up.sent, *sum_gate.sent)
    sum_go = weight_gradient(
        grid, [(normed_attn_t, grad_gate_logit), (grad_branch_t, gated)], 4, "halves"
    ).start()
    grad_attended = tie(grad_attended, *sum_go.sent)
    grad_queries, grad_keys, grad_values, row_total, column_total = attend_backward(
        qk, values_all, grad_attended, decay_column, decay_row, logsum, head_size
    )
    line_mlp = LineSum(grid, [sum_gate, sum_up]).third(grad_queries)
    sum_down.step(1, grad_queries)
    grad_queries = tie(grad_queries, line_mlp.sent, sum_down.sent)
    sum_qk = weight_gradient(
        grid, [(normed_attn_t, grad_queries), (normed_attn_t, grad_keys)], 4, "halves"
    )
    sum_qk.start()
    sum_go.second(*sum_qk.sent)
    grad_forget, bias_part = forget_backward(
        row_total, column_total, forget_logit, bias_lanes, heads_here
    )
    bias_block = jnp.pad(
        bias_part[0, :heads_here, None],
        ((0, w_forget.shape[0] - heads_here), (heads_here, LANES - heads_here - 1)),
    )
    bias_extra = jnp.tile(bias_block, (grid.count, 1))
    grad_values = tie(grad_values, *sum_qk.sent, *sum_go.sent)
    sum_vf = weight_gradient(
        grid,
        [(normed_attn_t, grad_values), (normed_attn_t, grad_forget)],
        1,
        "halves",
        bias_extra,
    )
    back = [
        (tie(grad_gate_logit, *sum_vf.sent), gate_w),
        (grad_queries, query_w),
        (grad_keys, key_w),
        (grad_values, value_w),
        (grad_forget, forget_w),
    ]
    other_part = multiply_back(back, 1 - side, low, 2)
    arrived = exchanged(other_part)
    line_mlp.fourth(*other_part)
    sum_qk.second(*other_part)
    hidden = tie(hidden, line_mlp.sent, *sum_qk.sent)
    other_down = multiply_back([(hidden, mlp_down)], jnp.int32(1), low)
    arrived_down = exchanged(other_down)
    sum_vf.start(*sum_qk.sent)
    back[1] = (tie(grad_queries, line_mlp.sent, *sum_qk.sent), query_w)
    (own_part,) = multiply_back(back, side)
    line_go = LineSum(grid, [sum_go]).third(own_part)
    own_part = tie(own_part, line_go.sent)
    _, tokens_grad = row_kernel(
        norm_gradient,
        [tokens, own_part, *arrived, grad_middle, gain_attn],
        [(columns, jnp.float32), (columns, low)],
    )
    sum_vf.second(tokens_grad)
    line_qkv = LineSum(grid, [sum_qk, sum_vf]).third()
    line_go.fourth(line_qkv.sent)
    line_qkv.fourth()
    (own_down,) = multiply_back([(tie(hidden, line_qkv.sent), mlp_down)], jnp.int32(0))
    (mixed,) = row_kernel(
        lambda middle, own, part: (lower(middle + (own + wide(part))),),
        [middle, own_down, *arrived_down],
        [(columns, low)],
    )
    sum_down.step(0, line_qkv.sent)
    down_grad, go_grad, qkv_grad = sum_down.result().T, line_go.result(), line_qkv.result()
    mlp_grad = line_mlp.result()

    def gain_gradient(gain, *pairs):
        return sum(jnp.sum(wide(lower(w)) * grad, axis=1) for w, grad in pairs) / gain

    forget_at = 3 * width
    parts = jnp.stack(
        [
            gain_gradient(
                pair_gains[0],
                (w_query, qkv_grad[:, :width]),
                (w_key, qkv_grad[:, width : 2 * width]),
                (w_value, qkv_grad[:, 2 * width : forget_at]),
                (w_forget, qkv_grad[:, forget_at : forget_at + heads_here]),
                (w_gate_attn, go_grad[:, :width]),
            ),
            gain_gradient(
                pair_gains[1], (w_gate, mlp_grad[:, :hidden_here]), (w_up, mlp_grad[:, hidden_here:])
            ),
        ]
    ).reshape(2, 2, norm_attn.shape[0])
    gain_grads = pick(parts, 1, side) + partner(pick(parts, 1, 1 - side))
    return (
        mixed,
        tokens_grad,
        qkv_grad[:, :width],
        qkv_grad[:, width : 2 * width],
        qkv_grad[:, 2 * width : 3 * width],
        go_grad[:, :width],
        qkv_grad[:, 3 * width : 3 * width + heads_here],
        qkv_grad[:heads_here, forget_at + heads_here],
        go_grad[:, width:].T,
        gain_grads[0],
        gain_grads[1],
        mlp_grad[:, :hidden_here],
        mlp_grad[:, hidden_here:],
        down_grad,
    )


def solution(mesh):
    return jax.shard_map(
        per_device,
        mesh=mesh,
        in_specs=(
            P(("dp", "tensor"), None),
            P("dp", "tensor"),
            P("dp", "tensor"),
            P("dp", "tensor"),
            P("dp", "tensor"),
            P("dp", "tensor"),
            P("tensor"),
            P("tensor", "dp"),
            P(("dp", "tensor")),
            P(("dp", "tensor")),
            P("dp", "tensor"),
            P("dp", "tensor"),
            P("tensor", "dp"),
            P(("dp", "tensor"), None),
        ),
        out_specs=(
            P(("dp", "tensor"), None),
            P(("dp", "tensor"), None),
            P("dp", "tensor"),
            P("dp", "tensor"),
            P("dp", "tensor"),
            P("dp", "tensor"),
            P("dp", "tensor"),
            P("tensor"),
            P("tensor", "dp"),
            P(("dp", "tensor")),
            P(("dp", "tensor")),
            P("dp", "tensor"),
            P("dp", "tensor"),
            P("tensor", "dp"),
        ),
        check_vma=False,
    )
```
